32 devices in a mesh: row: 8 (over z, core), col: 4 (over y, x).
Axes of the slice: x: 2, y: 2, z: 4, core: 2. Of those that a mesh axis runs over, the one named last changes fastest.
Arguments:
- latents: bfloat16 [128, 512, 256], P('row', 'col'), may hold values from -64 to 64
- code_ids: int32 [128, 512], P('row', 'col'), may hold values from 0 to 16383, as said below
- norm_gain: float32 [256], replicated, may hold values from 0.1 to 1.9
- norm_bias: float32 [256], replicated, may hold values from -2 to 2
- encoder_weight: bfloat16 [3, 3, 256, 256], replicated, may hold values from -0.125 to 0.125
- codebook: bfloat16 [16384, 256], replicated, may hold values from -6 to 6
- decoder_weight: bfloat16 [3, 3, 256, 256], replicated, may hold values from -0.125 to 0.125
- decoded_cotangent: bfloat16 [128, 512, 256], P('row', 'col'), may hold values from -6 to 6
Outputs:
- decoded: bfloat16 [128, 512, 256], P('row', 'col')
- latents_grad: bfloat16 [128, 512, 256], P('row', 'col')
- norm_gain_grad: float32 [256], replicated
- norm_bias_grad: float32 [256], replicated
- encoder_weight_grad: float32 [3, 3, 256, 256], replicated
- decoder_weight_grad: float32 [3, 3, 256, 256], replicated
- codebook_grad: float32 [16384, 256], P(('row', 'col'))
The draws below stay inside these ranges and needn't reach their ends.
Inputs may be any that keep to these rules, and one draw needn't show every extreme that they name: On the 16 x 128 positions of one device, at most 128 code_ids fall in any one aligned block of 512 codes; in every draw one block holds exactly 128 of them on every device.
All inputs are finite; a program needn't handle non-finite values.
Results may differ from the reference program's by a relative error of at most 0.002.
The reference program's roundings to bfloat16 on the way (of `smooth`, `quantized` and `enc_back_b`) count: a program that leaves them out, or rounds other values in their place, can miss the bound.
Values may be sent and summed in bfloat16 or wider, within the bound.
No kernel may reach another device: no remote copies, remote signals or barrier semaphores. Data moves between devices by JAX's collectives and lax.ppermute only.
A program may use at most 128 MiB of HBM per device.

```python
import jax
import jax.numpy as jnp
from jax import lax

C = 256
K = 16384
G = 32
HT = 16
WT = 128
H = 128
W = 512
N_ROW = 8
N_COL = 4


def draw_latents(key, part):
    height = HT * N_ROW
    breadth = WT * N_COL
    key_base, key_chan = jax.random.split(key, 2)
    centre_row = height // 2 + HT / 2.0
    row_dist = jnp.abs(jnp.arange(height, dtype=jnp.float32) + 0.5 - centre_row) / height
    row_shape = jnp.maximum(0.0, 1.0 - 4.0 * row_dist)
    col_frac = jnp.arange(breadth, dtype=jnp.float32) / max(breadth - 1, 1)
    base_draw = jnp.clip(jax.random.normal(key_base, (height, breadth, C), jnp.float32), -4.0, 4.0)
    row_scale = jnp.exp(jnp.log(10.0) * row_shape)
    chan_scale = jnp.exp(jax.random.uniform(key_chan, (C,), jnp.float32, jnp.log(0.7), jnp.log(1.4)))
    col_scale = jnp.exp(-jnp.log(3.0) * col_frac)
    scale_all = row_scale[:, None, None] * col_scale[None, :, None] * chan_scale[None, None, :]
    return (base_draw * scale_all).astype(jnp.bfloat16)


def draw_code_ids(key, part):
    devices = N_ROW * N_COL
    positions = HT * WT
    base_count = positions // devices
    block_codes = K // devices
    key_star, key_blocks = jax.random.split(jax.random.fold_in(key, 11))
    star_owner = jax.random.randint(key_star, (), 0, devices)

    def one_block(block_key):
        key_perm, key_delta, key_order, key_local = jax.random.split(block_key, 4)
        perm_owner = jax.random.permutation(key_perm, devices)
        deltas = jax.random.randint(key_delta, (devices // 2,), 0, base_count + 1).at[0].set(base_count)
        paired = jnp.stack([base_count + deltas, base_count - deltas], 1).reshape(devices)
        counts_owner = jnp.zeros((devices,), jnp.int32).at[perm_owner].set(paired.astype(jnp.int32))
        rotate_by = (star_owner - perm_owner[0]) % devices
        counts_owner = jnp.roll(counts_owner, rotate_by)
        owner_list = jnp.repeat(jnp.arange(devices, dtype=jnp.int32), counts_owner, total_repeat_length=positions)
        owner_list = jax.random.permutation(key_order, owner_list)
        local_code = jax.random.randint(key_local, (positions,), 0, block_codes)
        return (owner_list * block_codes + local_code).astype(jnp.int32).reshape(HT, WT)
    block_keys = jax.random.split(key_blocks, devices)
    blocks_all = jax.vmap(one_block)(block_keys)
    return blocks_all.reshape(N_ROW, N_COL, HT, WT).transpose(0, 2, 1, 3).reshape(HT * N_ROW, WT * N_COL)


def block_scale(own_key, shape, shards, least, high):
    loudness = 1.0
    for position, blocks in shards:
        heights = jax.random.uniform(jax.random.fold_in(jax.random.fold_in(own_key, 6), position), (blocks,), jnp.float32, least / len(shards), high / len(shards))
        loudness = loudness * jnp.repeat(jnp.exp(heights), shape[position] // blocks).reshape((-1,) + (1,) * (len(shape) - 1 - position))
    return loudness


def normal_values(own_key, shape, width, bound, cuts=(), kind=jnp.bfloat16):
    gain = block_scale(own_key, shape, cuts, -0.22, 0.18) if cuts else 1.0
    result = jax.random.normal(own_key, shape, jnp.float32) * width * gain
    return jnp.minimum(jnp.maximum(result, -bound), bound).astype(kind)


def setup_inputs(seed: int = 0) -> dict:
    key_of = jax.random.split(jax.random.key(seed), 9)
    return {
        "latents": draw_latents(jax.random.fold_in(key_of[8], 71), 0),
        "code_ids": draw_code_ids(jax.random.fold_in(key_of[8], 71), 0),
        "norm_gain": jnp.clip(1.0 + 0.18 * jax.random.normal(key_of[2], (C,), jnp.float32), 0.1, 1.9),
        "norm_bias": normal_values(key_of[3], (C,), 0.5, 2.0, (), jnp.float32),
        "encoder_weight": normal_values(key_of[4], (3, 3, C, C), (9 * C) ** -0.5, 0.125),
        "codebook": normal_values(key_of[5], (K, C), 1.0, 6.0),
        "decoder_weight": normal_values(key_of[6], (3, 3, C, C), (9 * C) ** -0.5, 0.125),
        "decoded_cotangent": normal_values(key_of[7], (H, W, C), 1.0, 6.0, ((0, 8), (1, 4))),
    }


epsilon = 1e-06
commit_beta = 0.25

def conv_forward(inputs, weight):
    height = inputs.shape[0]
    breadth = inputs.shape[1]
    padded = jnp.pad(inputs.astype(jnp.float32), ((1, 1), (1, 1), (0, 0)))
    weight_float = weight.astype(jnp.float32)
    summed = jnp.zeros((height, breadth, weight.shape[3]), jnp.float32)
    for shift_r in range(3):
        for shift_c in range(3):
            window = padded[shift_r:shift_r + height, shift_c:shift_c + breadth]
            summed = summed + jnp.einsum('hwi,io->hwo', window, weight_float[shift_r, shift_c])
    return summed

def conv_back(grads, weight):
    height = grads.shape[0]
    breadth = grads.shape[1]
    padded = jnp.pad(grads.astype(jnp.float32), ((1, 1), (1, 1), (0, 0)))
    weight_float = weight.astype(jnp.float32)
    summed = jnp.zeros((height, breadth, weight.shape[2]), jnp.float32)
    for shift_r in range(3):
        for shift_c in range(3):
            window = padded[2 - shift_r:2 - shift_r + height, 2 - shift_c:2 - shift_c + breadth]
            summed = summed + jnp.einsum('hwo,io->hwi', window, weight_float[shift_r, shift_c])
    return summed

def weight_grad(inputs, grads):
    height = inputs.shape[0]
    breadth = inputs.shape[1]
    padded = jnp.pad(inputs.astype(jnp.float32), ((1, 1), (1, 1), (0, 0)))
    grads_float = grads.astype(jnp.float32)
    pieces = []
    for shift_r in range(3):
        for shift_c in range(3):
            window = padded[shift_r:shift_r + height, shift_c:shift_c + breadth]
            pieces.append(jnp.einsum('hwi,hwo->io', window, grads_float))
    stacked = jnp.stack(pieces)
    return stacked.reshape(3, 3, stacked.shape[1], stacked.shape[2])

def rotate_back(encoded, embed, back):
    z_norm = jnp.sqrt(lax.optimization_barrier(jnp.sum(encoded * encoded, -1, keepdims=True)) + epsilon)
    e_norm = jnp.sqrt(lax.optimization_barrier(jnp.sum(embed * embed, -1, keepdims=True)) + epsilon)
    z_unit = encoded / z_norm
    e_unit = embed / e_norm
    mirror = z_unit + e_unit
    mirror = mirror / jnp.sqrt(lax.optimization_barrier(jnp.sum(mirror * mirror, -1, keepdims=True)) + epsilon)
    stretch = e_norm / z_norm
    along_mirror = lax.optimization_barrier(jnp.sum(mirror * back, -1, keepdims=True))
    along_code = lax.optimization_barrier(jnp.sum(e_unit * back, -1, keepdims=True))
    turned = back - 2.0 * mirror * along_mirror + 2.0 * z_unit * along_code
    return stretch * turned + commit_beta * (encoded - embed)

def reference(latents, code_ids, norm_gain, norm_bias, encoder_weight, codebook, decoder_weight, decoded_cotangent):
    channels = latents.shape[2]
    per_group = channels // G
    group_count = H * W * per_group
    xfloat = latents.astype(jnp.float32)
    mean_group = lax.optimization_barrier(jnp.sum(xfloat, (0, 1))).reshape(G, per_group).sum(1) / group_count
    centered = xfloat - jnp.repeat(mean_group, per_group)
    var_group = lax.optimization_barrier(jnp.sum(centered * centered, (0, 1))).reshape(G, per_group).sum(1) / group_count
    inv_std = jnp.repeat(lax.rsqrt(var_group + epsilon), per_group)
    normed = centered * inv_std
    act = normed * norm_gain + norm_bias
    smooth = jax.nn.silu(act).astype(jnp.bfloat16)
    encoded = xfloat + conv_forward(smooth, encoder_weight)
    quantized = codebook[code_ids]
    decoded = conv_forward(quantized, decoder_weight).astype(jnp.bfloat16)
    back_quant = conv_back(decoded_cotangent, decoder_weight)
    decoder_weight_grad = weight_grad(quantized, decoded_cotangent)
    embed = quantized.astype(jnp.float32)
    enc_back = rotate_back(encoded, embed, back_quant)
    enc_back_b = enc_back.astype(jnp.bfloat16)
    code_pull = K / (H * W) * (embed - encoded)
    codebook_grad = jnp.zeros((K, channels), jnp.float32).at[code_ids.reshape(-1)].add(code_pull.reshape(-1, channels))
    back_smooth = conv_back(enc_back_b, encoder_weight)
    encoder_weight_grad = weight_grad(smooth, enc_back_b)
    sigmoid_act = jax.nn.sigmoid(act)
    back_act = back_smooth * sigmoid_act * (1.0 + act * (1.0 - sigmoid_act))
    norm_bias_grad = lax.optimization_barrier(jnp.sum(back_act, (0, 1)))
    norm_gain_grad = lax.optimization_barrier(jnp.sum(back_act * normed, (0, 1)))
    first_mean = jnp.repeat((norm_gain * norm_bias_grad).reshape(G, per_group).sum(1) / group_count, per_group)
    second_mean = jnp.repeat((norm_gain * norm_gain_grad).reshape(G, per_group).sum(1) / group_count, per_group)
    latents_grad = (inv_std * (back_act * norm_gain - first_mean - normed * second_mean) + enc_back).astype(jnp.bfloat16)
    return (decoded, latents_grad, norm_gain_grad, norm_bias_grad, encoder_weight_grad, decoder_weight_grad, codebook_grad)
```

```python
import jax
import jax.numpy as jnp
from jax import lax
from jax.experimental import pallas as pl
from jax.experimental.pallas import tpu as pltpu
from jax.sharding import PartitionSpec as P

G = 32
epsilon = 1e-06
commit_beta = 0.25
F32 = jnp.float32
BF16 = jnp.bfloat16
F16 = jnp.float16
AXES = ("row", "col")
SIDE = 8
VMEM = pl.BlockSpec(memory_space=pltpu.VMEM)
SMEM = pl.BlockSpec(memory_space=pltpu.SMEM)
NT = (((1,), (1,)), ((), ()))
NN = (((1,), (0,)), ((), ()))
HIGH = lax.Precision.HIGHEST


def call(kernel, ins, outs, scratch=(), specs=None, flops=0, moved=0):
    return pl.pallas_call(
        kernel,
        in_specs=specs or [VMEM] * len(ins),
        out_specs=jax.tree.map(lambda _: VMEM, outs),
        out_shape=outs,
        scratch_shapes=list(scratch),
        compiler_params=pltpu.CompilerParams(vmem_limit_bytes=56 * 1024 * 1024),
        cost_estimate=pl.CostEstimate(flops=flops, bytes_accessed=moved, transcendentals=0),
    )(*ins)


def shaped(shape, dtype=F32):
    return jax.ShapeDtypeStruct(shape, dtype)


def dot(a, b, dims=NN, precision=None):
    return lax.dot_general(a, b, dims, precision=precision, preferred_element_type=F32)


def front_kernel(devices, shard, cap, lat, ids, payload, slots):
    height, width, channels = lat.shape
    count = height * width

    def add_row(r, total):
        return total + jnp.sum(lat[r].astype(F32), 0, keepdims=True)

    mean = lax.fori_loop(0, height, add_row, jnp.zeros((1, channels), F32)) * (1.0 / count)

    def add_square(r, total):
        gap = lat[r].astype(F32) - mean
        return total + jnp.sum(gap * gap, 0, keepdims=True)

    square = lax.fori_loop(0, height, add_square, jnp.zeros((1, channels), F32))
    lane = lax.broadcasted_iota(jnp.int32, (devices, width), 1)
    owner = lax.broadcasted_iota(jnp.int32, (devices, width), 0)
    upper = (
        lax.broadcasted_iota(jnp.int32, (width, width), 0)
        < lax.broadcasted_iota(jnp.int32, (width, width), 1)
    ).astype(BF16)
    slot_row = lax.broadcasted_iota(jnp.int32, (width, width), 0)
    base = jnp.zeros((devices, 1), F32)
    placed = jnp.zeros((devices, width), F32)
    for r in range(height):
        codes = ids[r : r + 1, :]
        dest = codes // shard
        local = codes - dest * shard
        member = owner == dest
        member_f = member.astype(F32)
        before = dot(member_f.astype(BF16), upper) + base
        rank = jnp.sum(member_f * before, 0, keepdims=True).astype(jnp.int32)
        slots[r : r + 1, :] = dest * cap + rank
        hit = (slot_row == rank).astype(BF16)
        tagged = local + 1
        high = tagged // 32
        low = tagged - high * 32
        zero = jnp.zeros((devices, width), F32)
        placed = placed + 32.0 * dot(
            jnp.where(member, high.astype(F32), zero).astype(BF16), hit, NT
        )
        placed = placed + dot(jnp.where(member, low.astype(F32), zero).astype(BF16), hit, NT)
        base = base + jnp.sum(member_f, 1, keepdims=True)
    half = width
    rows = [mean[:, :half], mean[:, half:], square[:, :half], square[:, half:]]
    for i, part in enumerate(rows):
        payload[:, i, :] = jnp.broadcast_to(part, (devices, half))
    payload[:, 4, :] = placed
    ids_f = ids[...].astype(F32)
    payload[:, 5, :] = jnp.broadcast_to(ids_f[0:1], (devices, width))
    payload[:, 6, :] = jnp.broadcast_to(ids_f[height - 1 :], (devices, width))
    place = lax.broadcasted_iota(jnp.int32, (height, width), 1)
    level = lax.broadcasted_iota(jnp.int32, (height, width), 0)
    first = jnp.sum(jnp.where(place == level, ids_f[:, 0:1], 0.0), 0, keepdims=True)
    last = jnp.sum(
        jnp.where(place == level + height, ids_f[:, width - 1 :], 0.0), 0, keepdims=True
    )
    payload[:, 7, :] = jnp.broadcast_to(first + last, (devices, width))


def place_of():
    return (
        lax.axis_index("row"),
        lax.axis_index("col"),
        lax.axis_size("row"),
        lax.axis_size("col"),
    )


def ring_kernel(height, gathered, out):
    row, col, rows, cols = place_of()
    width = gathered.shape[2]

    def peer(dr, dc, which):
        r = jnp.clip(row + dr, 0, rows - 1)
        c = jnp.clip(col + dc, 0, cols - 1)
        return gathered[r * cols + c][which : which + 1]

    lane = lax.broadcasted_iota(jnp.int32, (1, width), 1)

    def pick(values, at):
        return jnp.sum(jnp.where(lane == at, values, 0.0), 1, keepdims=True)

    sides = jnp.where(lane < height, peer(0, 1, 7), peer(0, -1, 7))
    start = 2 * height
    corners = [
        pick(peer(-1, -1, 6), width - 1),
        pick(peer(-1, 1, 6), 0),
        pick(peer(1, -1, 5), width - 1),
        pick(peer(1, 1, 5), 0),
    ]
    misc = jnp.where(lane < start, sides, 0.0)
    for i, corner in enumerate(corners):
        misc = jnp.where(lane == start + i, corner, misc)
    out[0:1, :] = peer(-1, 0, 6).astype(jnp.int32)
    out[1:2, :] = peer(1, 0, 5).astype(jnp.int32)
    out[2:3, :] = misc.astype(jnp.int32)


def fill_tile(scr, own, left, right, up, down, ring):
    height, width, channels = own.shape
    pitch = width + 2 * SIDE
    for r in range(height):
        base = SIDE + (ring + r) * pitch
        scr[base : base + SIDE] = left[r].astype(F32)
        scr[base + SIDE : base + SIDE + width] = own[r].astype(F32)
        scr[base + SIDE + width : base + pitch] = right[r].astype(F32)
    depth = up.shape[0]
    for i in range(ring):
        top = SIDE + i * pitch
        scr[top : top + pitch] = up[depth - ring + i].astype(F32)
        low = SIDE + (ring + height + i) * pitch
        scr[low : low + pitch] = down[i].astype(F32)
    ends(scr, channels)


def ends(scr, channels):
    blank = jnp.zeros((SIDE, channels), F32)
    scr[0:SIDE] = blank
    scr[scr.shape[0] - SIDE :] = blank


def fill_codes(scr, own, ring):
    height, width, channels = own.shape
    pitch = width + 2 * SIDE
    row, col, rows, cols = place_of()
    misc = ring[2].astype(F32)
    right_ok = (col < cols - 1).astype(F32)
    left_ok = (col > 0).astype(F32)
    up_ok = (row > 0).astype(F32)
    down_ok = (row < rows - 1).astype(F32)
    blank = jnp.zeros((SIDE, channels), F32)
    for r in range(height + 2):
        base = SIDE + r * pitch
        if r == 0:
            mid = ring[0].astype(F32) * up_ok
            corner_l, corner_r = 2 * height, 2 * height + 1
            left_f, right_f = up_ok * left_ok, up_ok * right_ok
        elif r == height + 1:
            mid = ring[1].astype(F32) * down_ok
            corner_l, corner_r = 2 * height + 2, 2 * height + 3
            left_f, right_f = down_ok * left_ok, down_ok * right_ok
        else:
            mid = own[r - 1].astype(F32)
            corner_l, corner_r = height + r - 1, r - 1
            left_f, right_f = left_ok, right_ok
        scr[base : base + SIDE] = blank
        scr[base + SIDE - 1 : base + SIDE] = misc[corner_l : corner_l + 1] * left_f
        scr[base + SIDE : base + SIDE + width] = mid
        scr[base + SIDE + width : base + pitch] = blank
        scr[base + SIDE + width : base + SIDE + width + 1] = misc[corner_r : corner_r + 1] * right_f
    ends(scr, channels)


def spread(scr, wide, count, pitch, channels):
    def one(r, _):
        value = scr[pl.ds(pl.multiple_of(r * pitch, 8), pitch + 2 * SIDE), :]
        at = pl.ds(pl.multiple_of(r * pitch, 16), pitch)
        for j in range(3):
            start = SIDE + j - 1
            wide[at, j * channels : (j + 1) * channels] = value[start : start + pitch].astype(BF16)
        return 0

    lax.fori_loop(0, count, one, 0)


def rows_at(r, pitch, count):
    return pl.ds(pl.multiple_of(r * pitch, 16), count * pitch)


def forward_rows(wide, weight, r, step, pitch):
    total = dot(wide[rows_at(r, pitch, step), :], weight[0])
    for dy in (1, 2):
        total = total + dot(wide[rows_at(r + dy, pitch, step), :], weight[dy])
    return total


def backward_rows(wide, weight, r, step, pitch):
    total = dot(wide[rows_at(r + 2, pitch, step), :], weight[0], NT)
    for dy in (1, 2):
        total = total + dot(wide[rows_at(r + 2 - dy, pitch, step), :], weight[dy], NT)
    return total


def kernel_grad(turned, wide, out, pitch, height, first_row):
    channels = turned.shape[0]
    half = channels // 2
    count = height * pitch
    for dy in range(3):
        start = (first_row + 1 - dy) * pitch
        product = dot(turned[...], wide[start : start + count, :])
        for j in range(3):
            at = (dy * 3 + 2 - j) * channels
            for side in range(2):
                lanes = j * channels + side * half
                out[side, at : at + channels, :] = product[:, lanes : lanes + half]


def turn_own(own, turned):
    height, width, channels = own.shape
    pitch = width + 2 * SIDE
    blank = jnp.zeros((SIDE, channels), F32)
    for r in range(0, height, 8):
        parts = []
        for k in range(8):
            parts += [blank, own[r + k].astype(F32), blank]
        block = jnp.concatenate(parts, 0)
        turned[:, r * pitch : (r + 8) * pitch] = block.T.astype(BF16)


def decoder_grad_kernel(cot, codes, left, right, up, down, out, scr, wide, turned):
    height, width, channels = cot.shape
    pitch = width + 2 * SIDE
    fill_tile(scr, cot, left.at[1], right.at[1], up.at[1], down.at[1], 1)
    spread(scr, wide, height + 2, pitch, channels)
    turn_own(codes, turned)
    kernel_grad(turned, wide, out, pitch, height, 1)


def decoder_kernel(codes, ring, weight, out, scr, wide):
    height, width, channels = codes.shape
    pitch = width + 2 * SIDE
    fill_codes(scr, codes, ring)
    spread(scr, wide, height + 2, pitch, channels)
    step = 4

    def part(k, _):
        value = forward_rows(wide, weight, k * step, step, pitch)
        for u in range(step):
            at = u * pitch + SIDE
            out[k * step + u] = value[at : at + width].astype(BF16)
        return 0

    lax.fori_loop(0, height // step, part, 0)


def group_stats(gathered, height, width):
    devices = gathered.shape[0]
    rows, cols = lax.axis_size("row"), lax.axis_size("col")
    local = jnp.concatenate([gathered[:, 0, :], gathered[:, 1, :]], 1)
    square = jnp.concatenate([gathered[:, 2, :], gathered[:, 3, :]], 1)
    channels = local.shape[1]
    per_group = channels // G
    same = lax.broadcasted_iota(jnp.int32, (channels, channels), 0) // per_group
    same = same == lax.broadcasted_iota(jnp.int32, (channels, channels), 1) // per_group
    mix = jnp.where(same, 1.0 / per_group, 0.0).astype(F32)
    centre = jnp.broadcast_to(jnp.sum(local, 0, keepdims=True) * (1.0 / devices), (8, channels))
    mean = dot(centre, mix, precision=HIGH)[0:1]
    gap = local - mean
    spread_sum = square + (height * width) * (gap * gap)
    total = jnp.sum(spread_sum, 0, keepdims=True) * (1.0 / (devices * height * width))
    var = dot(jnp.broadcast_to(total, (8, channels)), mix, precision=HIGH)[0:1]
    return mean, lax.rsqrt(var + epsilon)


def main_kernel(
    lat, cot, left, right, up, down, codes, ring, gathered, gain, bias, enc_w, dec_w,
    pull, enc_back, back_wide, turned, stats,
    lat_s, tmp_s, code_s, lat_wide, cot_wide,
):
    height, width, channels = lat.shape
    pitch = width + 2 * SIDE
    row, col, rows, cols = place_of()
    mean, inv = group_stats(gathered, height, width)
    stats[0:1, :] = mean
    stats[1:2, :] = inv
    fill_tile(tmp_s, cot, left.at[1], right.at[1], up.at[1], down.at[1], 2)
    spread(tmp_s, cot_wide, height + 4, pitch, channels)
    fill_tile(lat_s, lat, left.at[0], right.at[0], up.at[0], down.at[0], 2)
    fill_codes(code_s, codes, ring)

    place = lax.broadcasted_iota(jnp.int32, (pitch, 1), 0) - SIDE + col * width
    inside_col = (place >= 0) & (place < cols * width)
    scale = inv * gain[...]
    offset = bias[...]

    def smooth_row(r, _):
        at = pl.ds(pl.multiple_of(SIDE + r * pitch, 8), pitch)
        act = (lat_s[at, :] - mean) * scale + offset
        value = act * jax.nn.sigmoid(act)
        high = row * height + r - 2
        keep = inside_col & (high >= 0) & (high < rows * height)
        tmp_s[at, :] = jnp.where(keep, value, 0.0)
        return 0

    lax.fori_loop(0, height + 4, smooth_row, 0)
    spread(tmp_s, lat_wide, height + 4, pitch, channels)
    blank = jnp.zeros((SIDE, channels), F32)
    for r in range(0, height, 8):
        parts = []
        for k in range(8):
            base = SIDE + (2 + r + k) * pitch + SIDE
            parts += [blank, tmp_s[base : base + width], blank]
        turned[:, r * pitch : (r + 8) * pitch] = jnp.concatenate(parts, 0).T.astype(BF16)

    step = 3
    code_scale = pull_scale(codes_total(enc_w, gathered), rows, cols, height, width)

    def part(k, _):
        r = k * step
        at = pl.ds(pl.multiple_of(SIDE + (r + 1) * pitch, 8), step * pitch)
        z = lat_s[at, :] + forward_rows(lat_wide, enc_w, r, step, pitch)
        back = backward_rows(cot_wide, dec_w, r, step, pitch)
        e = code_s[pl.ds(pl.multiple_of(SIDE + r * pitch, 8), step * pitch), :]
        z_norm = jnp.sqrt(jnp.sum(z * z, 1, keepdims=True) + epsilon)
        e_norm = jnp.sqrt(jnp.sum(e * e, 1, keepdims=True) + epsilon)
        z_inv = 1.0 / z_norm
        z_unit = z * z_inv
        e_unit = e * (1.0 / e_norm)
        mirror = z_unit + e_unit
        m_inv = 1.0 / (jnp.sum(mirror * mirror, 1, keepdims=True) + epsilon)
        along_mirror = jnp.sum(mirror * back, 1, keepdims=True) * m_inv
        along_code = jnp.sum(e_unit * back, 1, keepdims=True)
        turn = back - (2.0 * along_mirror) * mirror + (2.0 * along_code) * z_unit
        gap = z - e
        result = (e_norm * z_inv) * turn + commit_beta * gap
        for u in range(step):
            line = r + u
            high = row * height + line - 1
            keep = inside_col & (high >= 0) & (high < rows * height)
            some = jnp.where(keep, result[u * pitch : (u + 1) * pitch], 0.0)
            tmp_s[pl.ds(pl.multiple_of(SIDE + line * pitch, 8), pitch), :] = some

            @pl.when((line >= 1) & (line <= height))
            def _():
                at = u * pitch + SIDE
                enc_back[line - 1] = some[SIDE : SIDE + width]
                own = pl.ds(pl.multiple_of((line - 1) * width, 8), width)
                pull[own, :] = gap[at : at + width] * (-code_scale)

        return 0

    lax.fori_loop(0, (height + 2) // step, part, 0)
    low = SIDE + (height + 2) * pitch
    tmp_s[low : low + SIDE] = blank
    spread(tmp_s, back_wide, height + 2, pitch, channels)


def codes_total(weight, gathered):
    return None


def pull_scale(total, rows, cols, height, width):
    return CODES[0] / (height * width * rows * cols)


CODES = [16384]


def pack_kernel(slots, pull, out, biggest):
    count = slots.shape[0]
    out[...] = jnp.zeros(out.shape, F32)

    def some(i, top):
        value = pull[pl.ds(pl.multiple_of(i * 16, 8), 16), :]
        for u in range(16):
            out[pl.ds(slots[i * 16 + u], 1), :] = value[u : u + 1, :]
        return jnp.maximum(top, jnp.abs(value))

    top = lax.fori_loop(0, count // 16, some, jnp.zeros((16, pull.shape[1]), F32))
    biggest[...] = jnp.broadcast_to(jnp.max(top), biggest.shape)


def encoder_grad_kernel(turned, back_wide, out):
    channels = turned.shape[0]
    height = SHAPE[0]
    kernel_grad(turned, back_wide, out, turned.shape[1] // height, height, 1)


SHAPE = [16]


def back_kernel(lat, back_wide, enc_w, stats, gain, bias, back_act, sums):
    height, width, channels = lat.shape
    pitch = width + 2 * SIDE
    mean, inv = stats[0:1, :], stats[1:2, :]
    step = 4

    def part(k, totals):
        value = backward_rows(back_wide, enc_w, k * step, step, pitch)
        first, second = totals
        for u in range(step):
            at = u * pitch + SIDE
            normed = (lat[k * step + u].astype(F32) - mean) * inv
            act = normed * gain[...] + bias[...]
            s = jax.nn.sigmoid(act)
            some = value[at : at + width] * s * (1.0 + act * (1.0 - s))
            back_act[k * step + u] = some
            first = first + jnp.sum(some, 0, keepdims=True)
            second = second + jnp.sum(some * normed, 0, keepdims=True)
        return first, second

    zero = jnp.zeros((1, channels), F32)
    first, second = lax.fori_loop(0, height // step, part, (zero, zero))
    half = channels // 2
    for i, some in enumerate((first, second)):
        for j in range(2):
            line = jnp.broadcast_to(some[:, j * half : (j + 1) * half], (sums.shape[0], half))
            sums[:, 2 * i + j, :] = line


def last_kernel(lat, back_act, enc_back, stats, gain, gathered, out, grads):
    height, width, channels = lat.shape
    mean, inv = stats[0:1, :], stats[1:2, :]
    per_group = channels // G
    count = height * width * gathered.shape[0] * per_group
    first = jnp.concatenate([gathered[:, 0, :], gathered[:, 1, :]], 1)
    second = jnp.concatenate([gathered[:, 2, :], gathered[:, 3, :]], 1)
    first = jnp.sum(first, 0, keepdims=True)
    second = jnp.sum(second, 0, keepdims=True)
    grads[0:1, :] = first
    grads[1:2, :] = second
    same = lax.broadcasted_iota(jnp.int32, (channels, channels), 0) // per_group
    same = same == lax.broadcasted_iota(jnp.int32, (channels, channels), 1) // per_group
    mix = jnp.where(same, 1.0, 0.0).astype(F32)
    both = jnp.concatenate([first * gain[...], second * gain[...]] + [first] * 6, 0)
    means = dot(both, mix, precision=HIGH) * (1.0 / count)

    def one(r, _):
        normed = (lat[r].astype(F32) - mean) * inv
        d = back_act[r] * gain[...]
        out[r] = (inv * (d - means[0:1] - normed * means[1:2]) + enc_back[r]).astype(BF16)
        return 0

    lax.fori_loop(0, height, one, 0)


def owner_kernel(tags, wide, out):
    shard, channels = out.shape
    total = jnp.zeros((shard, 2 * channels), F32)
    rows = wide.shape[0]
    chunk = 1024
    code = lax.broadcasted_iota(jnp.int32, (shard, tags.shape[1]), 0) + 1
    lines = chunk // tags.shape[1]
    for k in range(rows // chunk):
        hit = jnp.concatenate(
            [
                (code == tags[k * lines + u : k * lines + u + 1, :]).astype(F32).astype(BF16)
                for u in range(lines)
            ],
            1,
        )
        total = total + dot(hit, wide[k * chunk : (k + 1) * chunk, :])
    out[...] = total[:, :channels] + total[:, channels:]


def exponent(biggest):
    return 14.0 - jnp.ceil(jnp.log2(jnp.maximum(biggest, 1e-30)))


def exchange(x):
    return lax.all_to_all(x, AXES, split_axis=0, concat_axis=0, tiled=True)


def pair_swap(x):
    size = lax.axis_size("row")
    return lax.ppermute(x, "row", [(i, i ^ 1) for i in range(size)])


def scatter_sum(grad, extra=None):
    core = lax.axis_index("row") % 2
    devices = lax.axis_size("row") * lax.axis_size("col")
    keep = jnp.where(core == 0, grad[0], grad[1])
    give = jnp.where(core == 0, grad[1], grad[0])
    mine = keep + pair_swap(give)
    power = exponent(jnp.max(jnp.abs(mine)))
    chunk = mine.shape[0] // devices
    body = (mine * jnp.exp2(power)).reshape(devices, chunk, -1)
    tail = [jnp.full((devices, 1, body.shape[2]), power, F32)]
    extra = jnp.zeros((), F32) if extra is None else extra
    tail.append(jnp.full((devices, 7, body.shape[2]), extra, F32))
    got = exchange(jnp.concatenate([body] + tail, 1).astype(F16))
    powers = got[:, chunk, 0].astype(F32)
    values = got[:, :chunk].astype(F32) * jnp.exp2(-powers)[:, None, None]
    rows, cols = lax.axis_size("row"), lax.axis_size("col")
    values = values.reshape(rows // 2, 2, cols, chunk, -1).sum((0, 2))
    return values, got[:, chunk + 1, 0].astype(F32)


def gather_sum(chunks):
    core = lax.axis_index("row") % 2
    rows, cols = lax.axis_size("row"), lax.axis_size("col")
    devices = rows * cols
    chunk, half = chunks.shape[1:]
    power = exponent(jnp.max(jnp.abs(chunks)))
    body = chunks * jnp.exp2(power)
    tail = jnp.full((2, 8, half), power, F32)
    body = jnp.concatenate([body, tail], 1).astype(F16)
    body = jnp.broadcast_to(body[None, :, None], (rows // 2, 2, cols, chunk + 8, half))
    got = exchange(body.reshape(devices, chunk + 8, half))
    other = pair_swap(got)

    def whole(x):
        values = x[:, :chunk].astype(F32) * jnp.exp2(-x[:, chunk, 0].astype(F32))[:, None, None]
        return values.reshape(devices * chunk, half)

    got, other = whole(got), whole(other)
    left = jnp.where(core == 0, got, other)
    right = jnp.where(core == 0, other, got)
    both = jnp.concatenate([left, right], 1)
    return both.reshape(3, 3, 2 * half, 2 * half)


def halo(lat, cot):
    rows, cols = lax.axis_size("row"), lax.axis_size("col")
    forth = lambda n: [(i, i + 1) for i in range(n - 1)]
    back = lambda n: [(i + 1, i) for i in range(n - 1)]
    left_edge = jnp.stack([lat[:, :SIDE], cot[:, :SIDE]])
    right_edge = jnp.stack([lat[:, -SIDE:], cot[:, -SIDE:]])
    left = lax.ppermute(right_edge, "col", forth(cols))
    right = lax.ppermute(left_edge, "col", back(cols))

    def lines(at):
        mid = jnp.stack([lat[at], cot[at]])
        return jnp.concatenate([left[:, at], mid, right[:, at]], 2)

    up = lax.ppermute(lines(slice(-2, None)), "row", forth(rows))
    down = lax.ppermute(lines(slice(0, 2)), "row", back(rows))
    return left, right, up, down


def body(
    latents,
    code_ids,
    norm_gain,
    norm_bias,
    encoder_weight,
    codebook,
    decoder_weight,
    decoded_cotangent,
):
    height, width, channels = latents.shape
    devices = lax.axis_size("row") * lax.axis_size("col")
    codes_total = codebook.shape[0]
    shard = codes_total // devices
    count = height * width
    cap = 2 * count // devices
    pitch = width + 2 * SIDE
    CODES[0] = codes_total
    SHAPE[0] = height
    conv_flops = 2 * count * 9 * channels * channels

    payload, slots = call(
        lambda *refs: front_kernel(devices, shard, cap, *refs),
        (latents, code_ids),
        (shaped((devices, 8, width)), shaped((height, width), jnp.int32)),
        flops=10**9,
        moved=10**6,
    )
    gathered = exchange(payload)
    quantized = codebook[code_ids]
    left, right, up, down = halo(latents, decoded_cotangent)
    gain = norm_gain.reshape(1, channels)
    bias = norm_bias.reshape(1, channels)
    taps = 9 * channels

    dec_grad = call(
        decoder_grad_kernel,
        (decoded_cotangent, quantized, left, right, up, down),
        shaped((2, taps, channels // 2)),
        [
            pltpu.VMEM(((height + 2) * pitch + 2 * SIDE, channels), F32),
            pltpu.VMEM(((height + 2) * pitch, 3 * channels), BF16),
            pltpu.VMEM((channels, height * pitch), BF16),
        ],
        flops=conv_flops,
        moved=5 * 10**6,
    )
    dec_chunks, _ = scatter_sum(dec_grad)

    ring_ids = call(
        lambda *refs: ring_kernel(height, *refs), (gathered,), shaped((3, width), jnp.int32)
    )
    ring = codebook[ring_ids]
    enc_fwd = encoder_weight.reshape(3, 3 * channels, channels)
    dec_fwd = decoder_weight.reshape(3, 3 * channels, channels)
    flip = lambda w: w[:, ::-1].transpose(0, 2, 1, 3).reshape(3, channels, 3 * channels)
    enc_bwd, dec_bwd = flip(encoder_weight), flip(decoder_weight)
    big = (height + 4) * pitch
    pull, enc_back, back_wide, turned, stats = call(
        main_kernel,
        (
            latents, decoded_cotangent, left, right, up, down, quantized, ring, gathered,
            gain, bias, enc_fwd, dec_bwd,
        ),
        (
            shaped((count, channels)),
            shaped((height, width, channels)),
            shaped(((height + 2) * pitch, 3 * channels), BF16),
            shaped((channels, height * pitch), BF16),
            shaped((8, channels)),
        ),
        [
            pltpu.VMEM((big + 2 * SIDE, channels), F32),
            pltpu.VMEM((big + 2 * SIDE, channels), F32),
            pltpu.VMEM(((height + 2) * pitch + 2 * SIDE, channels), F32),
            pltpu.VMEM((big, 3 * channels), BF16),
            pltpu.VMEM((big, 3 * channels), BF16),
        ],
        flops=3 * conv_flops,
        moved=15 * 10**6,
    )
    packed, biggest = call(
        pack_kernel,
        (slots.reshape(-1), pull),
        (shaped((devices * cap, channels)), shaped((8, 128))),
        specs=[SMEM, VMEM],
        flops=5 * 10**9,
        moved=6 * 10**6,
    )
    pull_power = exponent(biggest[0, 0])
    send = (packed * jnp.exp2(pull_power)).astype(F16).reshape(devices, cap, channels)
    received = exchange(send)

    enc_grad = call(
        encoder_grad_kernel,
        (turned, back_wide),
        shaped((2, taps, channels // 2)),
        flops=conv_flops,
        moved=8 * 10**6,
    )
    enc_chunks, pull_powers = scatter_sum(enc_grad, pull_power)
    back_act, sums = call(
        back_kernel,
        (latents, back_wide, enc_bwd, stats, gain, bias),
        (shaped((height, width, channels)), shaped((devices, 4, channels // 2))),
        flops=conv_flops,
        moved=8 * 10**6,
    )
    sums = exchange(sums)
    decoded = call(
        decoder_kernel,
        (quantized, ring, dec_fwd),
        shaped((height, width, channels), BF16),
        [
            pltpu.VMEM(((height + 2) * pitch + 2 * SIDE, channels), F32),
            pltpu.VMEM(((height + 2) * pitch, 3 * channels), BF16),
        ],
        flops=conv_flops,
        moved=4 * 10**6,
    )
    latents_grad, norm_grads = call(
        last_kernel,
        (latents, back_act, enc_back, stats, gain, sums),
        (shaped((height, width, channels), BF16), shaped((2, channels))),
        flops=10**8,
        moved=6 * 10**6,
    )
    decoder_weight_grad = gather_sum(dec_chunks)
    encoder_weight_grad = gather_sum(enc_chunks)

    rows_f = received.astype(F32) * jnp.exp2(-pull_powers)[:, None, None]
    rows_f = rows_f.reshape(devices * cap, channels)
    high = lax.reduce_precision(rows_f, 8, 7)
    low = rows_f - high
    wide = jnp.concatenate([high.astype(BF16), low.astype(BF16)], 1)
    tags = gathered[:, 4, :cap].astype(jnp.int32).reshape(-1, 128)
    codebook_grad = call(
        owner_kernel,
        (tags, wide),
        shaped((shard, channels)),
        flops=2 * 10**9,
        moved=6 * 10**6,
    )
    return (
        decoded,
        latents_grad,
        norm_grads[1],
        norm_grads[0],
        encoder_weight_grad,
        decoder_weight_grad,
        codebook_grad,
    )


def solution(mesh):
    return jax.shard_map(
        body,
        mesh=mesh,
        in_specs=(
            P("row", "col", None),
            P("row", "col"),
            P(),
            P(),
            P(),
            P(),
            P(),
            P("row", "col", None),
        ),
        out_specs=(
            P("row", "col", None),
            P("row", "col", None),
            P(),
            P(),
            P(),
            P(),
            P(("row", "col"), None),
        ),
        check_vma=False,
    )
```

```python
import jax
import jax.numpy as jnp
from jax import lax
from jax.experimental import pallas as pl
from jax.experimental.pallas import tpu as pltpu
from jax.sharding import PartitionSpec as P

G = 32
epsilon = 1e-06
commit_beta = 0.25
F32 = jnp.float32
BF16 = jnp.bfloat16
F16 = jnp.float16
AXES = ("row", "col")
SIDE = 8
HALO = 2
VMEM = pl.BlockSpec(memory_space=pltpu.VMEM)
SMEM = pl.BlockSpec(memory_space=pltpu.SMEM)
NT = (((1,), (1,)), ((), ()))
NN = (((1,), (0,)), ((), ()))
HIGH = lax.Precision.HIGHEST


def call(kernel, ins, outs, scratch=(), specs=None, flops=0, moved=0):
    return pl.pallas_call(
        kernel,
        in_specs=specs or [VMEM] * len(ins),
        out_specs=jax.tree.map(lambda _: VMEM, outs),
        out_shape=outs,
        scratch_shapes=list(scratch),
        compiler_params=pltpu.CompilerParams(vmem_limit_bytes=56 * 1024 * 1024),
        cost_estimate=pl.CostEstimate(flops=flops, bytes_accessed=moved, transcendentals=0),
    )(*ins)


def shaped(shape, dtype=F32):
    return jax.ShapeDtypeStruct(shape, dtype)


def dot(a, b, dims=NN, precision=None):
    return lax.dot_general(a, b, dims, precision=precision, preferred_element_type=F32)


def front_kernel(devices, shard, cap, lat, ids, payload, slots):
    height, width, channels = lat.shape
    count = height * width

    def add_row(r, total):
        return total + jnp.sum(lat[r].astype(F32), 0, keepdims=True)

    mean = lax.fori_loop(0, height, add_row, jnp.zeros((1, channels), F32)) * (1.0 / count)

    def add_square(r, total):
        gap = lat[r].astype(F32) - mean
        return total + jnp.sum(gap * gap, 0, keepdims=True)

    square = lax.fori_loop(0, height, add_square, jnp.zeros((1, channels), F32))
    lane = lax.broadcasted_iota(jnp.int32, (devices, width), 1)
    owner = lax.broadcasted_iota(jnp.int32, (devices, width), 0)
    upper = (
        lax.broadcasted_iota(jnp.int32, (width, width), 0)
        < lax.broadcasted_iota(jnp.int32, (width, width), 1)
    ).astype(BF16)
    slot_row = lax.broadcasted_iota(jnp.int32, (width, width), 0)
    base = jnp.zeros((devices, 1), F32)
    placed = jnp.zeros((devices, width), F32)
    for r in range(height):
        codes = ids[r : r + 1, :]
        dest = codes // shard
        local = codes - dest * shard
        member = owner == dest
        member_f = member.astype(F32)
        before = dot(member_f.astype(BF16), upper) + base
        rank = jnp.sum(member_f * before, 0, keepdims=True).astype(jnp.int32)
        slots[r : r + 1, :] = dest * cap + rank
        hit = (slot_row == rank).astype(BF16)
        tagged = local + 1
        high = tagged // 32
        low = tagged - high * 32
        zero = jnp.zeros((devices, width), F32)
        placed = placed + 32.0 * dot(
            jnp.where(member, high.astype(F32), zero).astype(BF16), hit, NT
        )
        placed = placed + dot(jnp.where(member, low.astype(F32), zero).astype(BF16), hit, NT)
        base = base + jnp.sum(member_f, 1, keepdims=True)
    half = width
    rows = [mean[:, :half], mean[:, half:], square[:, :half], square[:, half:]]
    for i, part in enumerate(rows):
        payload[:, i, :] = jnp.broadcast_to(part, (devices, half))
    payload[:, 4, :] = placed
    payload[:, 5:, :] = jnp.zeros((devices, 3, half), F32)


def place_of():
    return (
        lax.axis_index("row"),
        lax.axis_index("col"),
        lax.axis_size("row"),
        lax.axis_size("col"),
    )


def place_of():
    return (
        lax.axis_index("row"),
        lax.axis_index("col"),
        lax.axis_size("row"),
        lax.axis_size("col"),
    )


def fill_tile(scr, own, left, right, up, down, ring):
    height, width, channels = own.shape
    pitch = width + 2 * SIDE
    for r in range(height):
        base = SIDE + (ring + r) * pitch
        scr[base + SIDE - HALO : base + SIDE] = left[r].astype(F32)
        scr[base + SIDE : base + SIDE + width] = own[r].astype(F32)
        scr[base + SIDE + width : base + SIDE + width + HALO] = right[r].astype(F32)
    span = up.shape[1]
    for i in range(ring):
        top = SIDE + i * pitch + SIDE - HALO
        scr[top : top + span] = up[HALO - ring + i].astype(F32)
        low = SIDE + (ring + height + i) * pitch + SIDE - HALO
        scr[low : low + span] = down[i].astype(F32)
    blank = jnp.zeros((SIDE - HALO, channels), F32)
    for r in range(height + 2 * ring):
        base = SIDE + r * pitch
        scr[base : base + SIDE - HALO] = blank
        scr[base + pitch - SIDE + HALO : base + pitch] = blank
    ends(scr, channels)


def ends(scr, channels):
    blank = jnp.zeros((SIDE, channels), F32)
    scr[0:SIDE] = blank
    scr[scr.shape[0] - SIDE :] = blank


def spread(scr, wide, count, pitch, channels):
    def one(r, _):
        value = scr[pl.ds(pl.multiple_of(r * pitch, 8), pitch + 2 * SIDE), :]
        at = pl.ds(pl.multiple_of(r * pitch, 16), pitch)
        for j in range(3):
            start = SIDE + j - 1
            wide[at, j * channels : (j + 1) * channels] = value[start : start + pitch].astype(BF16)
        return 0

    lax.fori_loop(0, count, one, 0)


def rows_at(r, pitch, count):
    return pl.ds(pl.multiple_of(r * pitch, 16), count * pitch)


def forward_rows(wide, weight, r, step, pitch):
    total = dot(wide[rows_at(r, pitch, step), :], weight[0])
    for dy in (1, 2):
        total = total + dot(wide[rows_at(r + dy, pitch, step), :], weight[dy])
    return total


def backward_rows(wide, weight, r, step, pitch):
    total = dot(wide[rows_at(r + 2, pitch, step), :], weight[0], NT)
    for dy in (1, 2):
        total = total + dot(wide[rows_at(r + 2 - dy, pitch, step), :], weight[dy], NT)
    return total


def kernel_grad(turned, wide, keep, give, pitch, height, first_row):
    channels = turned.shape[0]
    half = channels // 2
    count = height * pitch
    core = lax.axis_index("row") % 2
    for dy in range(3):
        start = (first_row + 1 - dy) * pitch
        product = dot(turned[...], wide[start : start + count, :])
        for j in range(3):
            at = (dy * 3 + 2 - j) * channels
            low = product[:, j * channels : j * channels + half]
            high = product[:, j * channels + half : (j + 1) * channels]

            @pl.when(core == 0)
            def _():
                keep[at : at + channels, :] = low
                give[at : at + channels, :] = high

            @pl.when(core == 1)
            def _():
                keep[at : at + channels, :] = high
                give[at : at + channels, :] = low


def turn_own(own, turned):
    height, width, channels = own.shape
    pitch = width + 2 * SIDE
    blank = jnp.zeros((SIDE, channels), F32)
    for r in range(0, height, 8):
        parts = []
        for k in range(8):
            parts += [blank, own[r + k].astype(F32), blank]
        block = jnp.concatenate(parts, 0)
        turned[:, r * pitch : (r + 8) * pitch] = block.T.astype(BF16)


def decoder_grad_kernel(
    cot, codes, left, right, up, down, keep, give, scr, wide, turned
):
    height, width, channels = cot.shape
    pitch = width + 2 * SIDE
    fill_tile(scr, cot, left.at[1], right.at[1], up.at[1], down.at[1], 1)
    spread(scr, wide, height + 2, pitch, channels)
    turn_own(codes, turned)
    kernel_grad(turned, wide, keep, give, pitch, height, 1)


def decoder_kernel(codes, left, right, up, down, weight, out, scr, wide):
    height, width, channels = codes.shape
    pitch = width + 2 * SIDE
    fill_tile(scr, codes, left.at[2], right.at[2], up.at[2], down.at[2], 1)
    spread(scr, wide, height + 2, pitch, channels)
    step = 4

    def part(k, _):
        value = forward_rows(wide, weight, k * step, step, pitch)
        for u in range(step):
            at = u * pitch + SIDE
            out[k * step + u] = value[at : at + width].astype(BF16)
        return 0

    lax.fori_loop(0, height // step, part, 0)


def group_stats(gathered, height, width):
    devices = gathered.shape[0]
    rows, cols = lax.axis_size("row"), lax.axis_size("col")
    local = jnp.concatenate([gathered[:, 0, :], gathered[:, 1, :]], 1)
    square = jnp.concatenate([gathered[:, 2, :], gathered[:, 3, :]], 1)
    channels = local.shape[1]
    per_group = channels // G
    same = lax.broadcasted_iota(jnp.int32, (channels, channels), 0) // per_group
    same = same == lax.broadcasted_iota(jnp.int32, (channels, channels), 1) // per_group
    mix = jnp.where(same, 1.0 / per_group, 0.0).astype(F32)
    centre = jnp.broadcast_to(jnp.sum(local, 0, keepdims=True) * (1.0 / devices), (8, channels))
    mean = dot(centre, mix, precision=HIGH)[0:1]
    gap = local - mean
    spread_sum = square + (height * width) * (gap * gap)
    total = jnp.sum(spread_sum, 0, keepdims=True) * (1.0 / (devices * height * width))
    var = dot(jnp.broadcast_to(total, (8, channels)), mix, precision=HIGH)[0:1]
    return mean, lax.rsqrt(var + epsilon)


def inside_tile(row, col, rows, cols, height, width):
    pitch = width + 2 * SIDE
    place = lax.broadcasted_iota(jnp.int32, (pitch, 1), 0) - SIDE + col * width
    inside_col = (place >= 0) & (place < cols * width)

    def keep(line):
        high = row * height + line
        return inside_col & (high >= 0) & (high < rows * height)

    return keep


def encoder_kernel(
    code_scale,
    lat, left, right, up, down, codes, gathered, gain, bias, weight,
    z_out, pull, turned, stats,
    tmp_s, wide,
):
    height, width, channels = lat.shape
    pitch = width + 2 * SIDE
    keep = inside_tile(*place_of(), height, width)
    mean, inv = group_stats(gathered, height, width)
    stats[0:1, :] = mean
    stats[1:2, :] = inv
    fill_tile(tmp_s, lat, left.at[0], right.at[0], up.at[0], down.at[0], 2)
    z_out[...] = tmp_s[pitch : pitch + z_out.shape[0], :]
    scale = inv * gain[...]
    offset = bias[...]

    def smooth_row(r, _):
        at = pl.ds(pl.multiple_of(SIDE + r * pitch, 8), pitch)
        act = (tmp_s[at, :] - mean) * scale + offset
        value = act * jax.nn.sigmoid(act)
        tmp_s[at, :] = jnp.where(keep(r - 2), value, 0.0)
        return 0

    lax.fori_loop(0, height + 4, smooth_row, 0)
    spread(tmp_s, wide, height + 4, pitch, channels)
    blank = jnp.zeros((SIDE, channels), F32)
    for r in range(0, height, 8):
        parts = []
        for k in range(8):
            base = SIDE + (2 + r + k) * pitch + SIDE
            parts += [blank, tmp_s[base : base + width], blank]
        turned[:, r * pitch : (r + 8) * pitch] = jnp.concatenate(parts, 0).T.astype(BF16)
    step = 3

    def part(k, _):
        r = k * step
        at = pl.ds(pl.multiple_of(SIDE + r * pitch, 8), step * pitch)
        z = z_out[at, :] + forward_rows(wide, weight, r, step, pitch)
        z_out[at, :] = z
        for u in range(step):
            line = r + u - 1

            @pl.when((line >= 0) & (line < height))
            def _():
                first = u * pitch + SIDE
                e = codes[line].astype(F32)
                own = pl.ds(pl.multiple_of(line * width, 8), width)
                pull[own, :] = (e - z[first : first + width]) * code_scale

        return 0

    lax.fori_loop(0, (height + 2) // step, part, 0)


def pack_kernel(slots, pull, packed, biggest):
    packed[...] = jnp.zeros(packed.shape, F32)

    def some(i, top):
        value = pull[pl.ds(pl.multiple_of(i * 16, 8), 16), :]
        for u in range(16):
            packed[pl.ds(slots[i * 16 + u], 1), :] = value[u : u + 1, :]
        return jnp.maximum(top, jnp.abs(value))

    top = lax.fori_loop(0, pull.shape[0] // 16, some, jnp.zeros((16, pull.shape[1]), F32))
    biggest[...] = jnp.broadcast_to(jnp.max(top), biggest.shape)


def flip_weight(weight, flipped):
    channels = weight.shape[2]
    for dy in range(3):
        for j in range(3):
            flipped[dy, :, j * channels : (j + 1) * channels] = weight[dy, 2 - j]


def rotate_kernel(
    cot, left, right, up, down, codes, z_in, turned, dec_w,
    plane, keep_grad, give_grad,
    tmp_s, code_s, wide, back_wide, flipped,
):
    height, width, channels = cot.shape
    pitch = width + 2 * SIDE
    fill_tile(tmp_s, cot, left.at[1], right.at[1], up.at[1], down.at[1], 2)
    spread(tmp_s, wide, height + 4, pitch, channels)
    fill_tile(code_s, codes, left.at[2], right.at[2], up.at[2], down.at[2], 1)
    flip_weight(dec_w, flipped)
    ends(plane, channels)
    step = 3

    def part(k, _):
        r = k * step
        at = pl.ds(pl.multiple_of(SIDE + r * pitch, 8), step * pitch)
        plane[at, :] = backward_rows(wide, flipped, r, step, pitch)
        return 0

    lax.fori_loop(0, (height + 2) // step, part, 0)
    block = 24
    place = lax.broadcasted_iota(jnp.int32, (block, 1), 0)
    row, col, rows, cols = place_of()

    def total(x):
        return jnp.sum(x, 1, keepdims=True)

    def turn(line, _):
        spots = [
            pl.ds(pl.multiple_of(SIDE + line * pitch + b, 8), block)
            for b in range(0, pitch, block)
        ]
        sums = []
        for at in spots:
            z, e = z_in[at, :], code_s[at, :]
            sums.append((total(z * z) + epsilon, total(e * e) + epsilon))
        scales = []
        for at, (zz, ee) in zip(spots, sums):
            z, e, back = z_in[at, :], code_s[at, :], plane[at, :]
            z_inv, e_inv = lax.rsqrt(zz), lax.rsqrt(ee)
            e_unit = e * e_inv
            mirror = z * z_inv + e_unit
            scales.append(
                (z_inv, e_inv, ee, total(mirror * mirror) + epsilon, total(mirror * back),
                 total(e_unit * back))
            )
        high = row * height + line - 1
        keep = (high >= 0) & (high < rows * height)
        for b, (at, (z_inv, e_inv, ee, mm, along, code)) in enumerate(zip(spots, scales)):
            z, e, back = z_in[at, :], code_s[at, :], plane[at, :]
            stretch = ee * e_inv * z_inv
            along = 2.0 * along / mm
            z_part = stretch * z_inv * (2.0 * code - along) + commit_beta
            e_part = stretch * e_inv * along + commit_beta
            across = place + b * block - SIDE + col * width
            inside = keep & (across >= 0) & (across < cols * width)
            plane[at, :] = jnp.where(inside, stretch * back + z_part * z - e_part * e, 0.0)
        return 0

    lax.fori_loop(0, height + 2, turn, 0)
    spread(plane, back_wide, height + 2, pitch, channels)
    kernel_grad(turned, back_wide, keep_grad, give_grad, pitch, height, 1)


def back_kernel(lat, plane, stats, gain, bias, enc_w, power, back_act, tail, back_wide, flipped):
    height, width, channels = lat.shape
    pitch = width + 2 * SIDE
    spread(plane, back_wide, height + 2, pitch, channels)
    flip_weight(enc_w, flipped)
    mean, inv = stats[0:1, :], stats[1:2, :]
    step = 4

    def last(k, totals):
        value = backward_rows(back_wide, flipped, k * step, step, pitch)
        first, second = totals
        for u in range(step):
            at = u * pitch + SIDE
            normed = (lat[k * step + u].astype(F32) - mean) * inv
            act = normed * gain[...] + bias[...]
            s = jax.nn.sigmoid(act)
            some = value[at : at + width] * s * (1.0 + act * (1.0 - s))
            back_act[k * step + u] = some
            first = first + jnp.sum(some, 0, keepdims=True)
            second = second + jnp.sum(some * normed, 0, keepdims=True)
        return first, second

    zero = jnp.zeros((1, channels), F32)
    first, second = lax.fori_loop(0, height // step, last, (zero, zero))
    half = channels // 2
    lines = [first[:, :half], first[:, half:], second[:, :half], second[:, half:]]
    row, col, rows, cols = place_of()
    lane = lax.broadcasted_iota(jnp.int32, (1, half), 1)
    lines.append(jnp.where(lane == row * cols + col, power[...], 0.0))
    tail[...] = jnp.concatenate(lines + [jnp.zeros((3, half), F32)], 0)


def last_kernel(lat, back_act, plane, stats, gain, sums, out, grads):
    height, width, channels = lat.shape
    mean, inv = stats[0:1, :], stats[1:2, :]
    per_group = channels // G
    count = height * width * lax.axis_size("row") * lax.axis_size("col") * per_group
    first = jnp.concatenate([sums[0:1, :], sums[1:2, :]], 1)
    second = jnp.concatenate([sums[2:3, :], sums[3:4, :]], 1)
    grads[0:1, :] = first
    grads[1:2, :] = second
    same = lax.broadcasted_iota(jnp.int32, (channels, channels), 0) // per_group
    same = same == lax.broadcasted_iota(jnp.int32, (channels, channels), 1) // per_group
    mix = jnp.where(same, 1.0, 0.0).astype(F32)
    both = jnp.concatenate([first * gain[...], second * gain[...]] + [first] * 6, 0)
    means = dot(both, mix, precision=HIGH) * (1.0 / count)

    def one(r, _):
        normed = (lat[r].astype(F32) - mean) * inv
        d = back_act[r] * gain[...]
        at = pl.multiple_of((r + 1) * (width + 2 * SIDE) + 2 * SIDE, 8)
        enc_back = plane[pl.ds(at, width), :]
        out[r] = (inv * (d - means[0:1] - normed * means[1:2]) + enc_back).astype(BF16)
        return 0

    lax.fori_loop(0, height, one, 0)


def owner_kernel(tags, wide, out):
    shard, channels = out.shape
    total = jnp.zeros((shard, 2 * channels), F32)
    rows = wide.shape[0]
    chunk = 1024
    code = lax.broadcasted_iota(jnp.int32, (shard, tags.shape[1]), 0) + 1
    lines = chunk // tags.shape[1]
    for k in range(rows // chunk):
        hit = jnp.concatenate(
            [
                (code == tags[k * lines + u : k * lines + u + 1, :]).astype(F32).astype(BF16)
                for u in range(lines)
            ],
            1,
        )
        total = total + dot(hit, wide[k * chunk : (k + 1) * chunk, :])
    out[...] = total[:, :channels] + total[:, channels:]


def exponent(biggest):
    return 14.0 - jnp.ceil(jnp.log2(jnp.maximum(biggest, 1e-30)))


def exchange(x):
    return lax.all_to_all(x, AXES, split_axis=0, concat_axis=0, tiled=True)


def pair_swap(x):
    size = lax.axis_size("row")
    return lax.ppermute(x, "row", [(i, i ^ 1) for i in range(size)])


def shifts(n, stride=1):
    size = n * stride
    return [[((i + s * stride) % size, i) for i in range(size)] for s in range(1, n)]


def columns_kernel(enc, enc_b, dec, dec_b, tail, tail_b, *outs):
    row, col, rows, cols = place_of()
    lines = enc.shape[0] // cols
    for s, out in enumerate(outs):
        at = pl.ds(pl.multiple_of((col + cols - s) % cols * lines, 8), lines)
        out[:lines, :] = enc[at, :] + enc_b[at, :]
        out[lines : 2 * lines, :] = dec[at, :] + dec_b[at, :]
        out[2 * lines :, :] = tail[...] + tail_b[...]


def rows_kernel(cols, *refs):
    parts, outs = refs[:cols], refs[cols:]
    row, _, rows, _ = place_of()
    depth = rows // 2
    lines = outs[0].shape[0] // 2 - 4
    wide = lines * depth

    def added(first, count):
        value = parts[0][first : first + count, :]
        for ref in parts[1:]:
            value = value + ref[first : first + count, :]
        return value

    tail = added(2 * wide, 8)
    for z in range(depth):
        values = [added(i * wide + z * lines, lines) for i in range(2)]
        for s, out in enumerate(outs):

            @pl.when((row // 2 + depth - s) % depth == z)
            def _():
                for i in range(2):
                    out[i * lines : (i + 1) * lines, :] = values[i]

    for out in outs:
        out[2 * lines :, :] = tail


def chunk_kernel(depth, *refs):
    parts, (out, tail) = refs[:depth], refs[depth:]
    half = out.shape[1]
    lines = parts[0].shape[0] // 2 - 4
    value = parts[0][...]
    for ref in parts[1:]:
        value = value + ref[...]
    tail[...] = value[2 * lines :]
    for i in range(2):
        some = value[i * lines : (i + 1) * lines]
        top = jnp.max(jnp.max(jnp.abs(some), 0, keepdims=True), 1, keepdims=True)
        power = 14.0 - jnp.ceil(jnp.log2(jnp.maximum(top, 1e-30)))
        out[i * lines : (i + 1) * lines, :] = some * jnp.exp2(power)
        at = 2 * lines + 8 * i
        out[at : at + 8, :] = jnp.broadcast_to(power, (8, half))


def column_sums(arrays):
    cols = lax.axis_size("col")
    taps, half = arrays[0].shape
    parts = call(
        columns_kernel,
        arrays,
        [shaped((2 * taps // cols + 8, half))] * cols,
        moved=7 * 10**6,
    )
    return [parts[0]] + [lax.ppermute(x, "col", p) for x, p in zip(parts[1:], shifts(cols))]


def row_sums(parts):
    cols, depth = len(parts), lax.axis_size("row") // 2
    taps, half = parts[0].shape[0] // 2 - 4, parts[0].shape[1]
    lines = taps // depth
    parts = call(
        lambda *refs: rows_kernel(cols, *refs),
        parts,
        [shaped((2 * lines + 8, half))] * depth,
        moved=4 * 10**6,
    )
    parts = [parts[0]] + [lax.ppermute(x, "row", p) for x, p in zip(parts[1:], shifts(depth, 2))]
    return call(
        lambda *refs: chunk_kernel(depth, *refs),
        parts,
        (shaped((2 * lines + 16, half)), shaped((8, half))),
        moved=10**6,
    )


def gather_steps(chunk):
    rows, cols = lax.axis_size("row"), lax.axis_size("col")
    lines, half = chunk.shape[0] // 2 - 8, chunk.shape[1]
    own = chunk.astype(F16)
    stacked = jnp.stack([own] + [lax.ppermute(own, "row", p) for p in shifts(rows // 2, 2)])
    pieces = [stacked] + [lax.ppermute(stacked, "col", p) for p in shifts(cols)]
    pieces = pieces + [pair_swap(x) for x in pieces]
    chunks = cols * rows // 2
    return call(
        lambda *refs: assemble_kernel(lines, *refs),
        [x.astype(F32) for x in pieces],
        (shaped((chunks, lines, 2 * half)), shaped((chunks, lines, 2 * half))),
        moved=10**7,
    )


def assemble_kernel(lines, *refs):
    pieces, outs = refs[:-2], refs[-2:]
    row, col, rows, cols = place_of()
    depth = rows // 2
    half = outs[0].shape[2] // 2
    for k, ref in enumerate(pieces):
        core = (row + k // cols) % 2
        c = (col + k % cols) % cols
        lanes = pl.ds(pl.multiple_of(core * half, half), half)
        for s in range(depth):
            z = (row // 2 + s) % depth
            for i, out in enumerate(outs):
                at = 2 * lines + 8 * i
                scale = jnp.exp2(-ref[s, at : at + 1, :])
                value = ref[s, i * lines : (i + 1) * lines, :] * scale
                out[c * depth + z, :, lanes] = value


def halo(fields):
    rows, cols = lax.axis_size("row"), lax.axis_size("col")
    forth = lambda n: [(i, i + 1) for i in range(n - 1)]
    back = lambda n: [(i + 1, i) for i in range(n - 1)]
    left_edge = jnp.stack([x[:, :HALO] for x in fields])
    right_edge = jnp.stack([x[:, -HALO:] for x in fields])
    left = lax.ppermute(right_edge, "col", forth(cols))
    right = lax.ppermute(left_edge, "col", back(cols))

    def lines(at):
        return jnp.concatenate([left[:, at], jnp.stack([x[at] for x in fields]), right[:, at]], 2)

    up = lax.ppermute(lines(slice(-HALO, None)), "row", forth(rows))
    down = lax.ppermute(lines(slice(0, HALO)), "row", back(rows))
    return left, right, up, down


def body(
    latents,
    code_ids,
    norm_gain,
    norm_bias,
    encoder_weight,
    codebook,
    decoder_weight,
    decoded_cotangent,
):
    height, width, channels = latents.shape
    devices = lax.axis_size("row") * lax.axis_size("col")
    codes_total = codebook.shape[0]
    shard = codes_total // devices
    count = height * width
    cap = 2 * count // devices
    pitch = width + 2 * SIDE
    conv_flops = 2 * count * 9 * channels * channels
    taps = 9 * channels
    half = channels // 2
    plane = (height + 2) * pitch
    plane_rows = plane + 2 * SIDE
    big = (height + 4) * pitch
    after = lambda *x: lax.optimization_barrier(x)

    payload, slots = call(
        lambda *refs: front_kernel(devices, shard, cap, *refs),
        (latents, code_ids),
        (shaped((devices, 8, width)), shaped((height, width), jnp.int32)),
        flops=10**9,
        moved=10**6,
    )
    payload, code_ids, latents, decoded_cotangent = after(
        payload, code_ids, latents, decoded_cotangent
    )
    gathered = exchange(payload)
    quantized = codebook[code_ids]
    left, right, up, down = halo((latents, decoded_cotangent, quantized))
    gain = norm_gain.reshape(1, channels)
    bias = norm_bias.reshape(1, channels)

    dec_grad = call(
        decoder_grad_kernel,
        (decoded_cotangent, quantized, left, right, up, down),
        (shaped((taps, half)), shaped((taps, half))),
        [
            pltpu.VMEM((plane_rows, channels), F32),
            pltpu.VMEM((plane, 3 * channels), BF16),
            pltpu.VMEM((channels, height * pitch), BF16),
        ],
        flops=conv_flops,
        moved=5 * 10**6,
    )
    dec_keep, dec_give = dec_grad
    dec_given = pair_swap(dec_give)
    gathered, dec_keep = after(gathered, dec_keep)
    enc_fwd = encoder_weight.reshape(3, 3 * channels, channels)
    dec_fwd = decoder_weight.reshape(3, 3 * channels, channels)
    code_scale = codes_total / (count * devices)
    z, pull, turned, stats = call(
        lambda *refs: encoder_kernel(code_scale, *refs),
        (latents, left, right, up, down, quantized, gathered, gain, bias, enc_fwd),
        (
            shaped((plane_rows, channels)),
            shaped((count, channels)),
            shaped((channels, height * pitch), BF16),
            shaped((8, channels)),
        ),
        [
            pltpu.VMEM((big + 2 * SIDE, channels), F32),
            pltpu.VMEM((big, 3 * channels), BF16),
        ],
        flops=conv_flops,
        moved=10 * 10**6,
    )
    packed, biggest = call(
        pack_kernel,
        (slots.reshape(-1), pull),
        (shaped((devices * cap, channels)), shaped((8, 128))),
        specs=[SMEM, VMEM],
        flops=5 * 10**9,
        moved=6 * 10**6,
    )
    pull_power = exponent(biggest[0, 0])
    send = (packed * jnp.exp2(pull_power)).astype(F16).reshape(devices, cap, channels)
    send, z = after(send, z)
    received = exchange(send)
    back_plane, keep_grad, give_grad = call(
        rotate_kernel,
        (
            decoded_cotangent, left, right, up, down, quantized, z, turned, decoder_weight,
        ),
        (
            shaped((plane_rows, channels)),
            shaped((taps, half)),
            shaped((taps, half)),
        ),
        [
            pltpu.VMEM((big + 2 * SIDE, channels), F32),
            pltpu.VMEM((plane_rows, channels), F32),
            pltpu.VMEM((big, 3 * channels), BF16),
            pltpu.VMEM((plane, 3 * channels), BF16),
            pltpu.VMEM((3, channels, 3 * channels), BF16),
        ],
        flops=2 * conv_flops,
        moved=15 * 10**6,
    )
    given = pair_swap(give_grad)

    back_act, tail = call(
        back_kernel,
        (
            latents, back_plane, stats, gain, bias, encoder_weight,
            pull_power.reshape(1, 1),
        ),
        (shaped((height, width, channels)), shaped((8, half))),
        [
            pltpu.VMEM((plane, 3 * channels), BF16),
            pltpu.VMEM((3, channels, 3 * channels), BF16),
        ],
        flops=conv_flops,
        moved=8 * 10**6,
    )
    parts = column_sums((keep_grad, given, dec_keep, dec_given, tail, pair_swap(tail)))
    received, *parts = after(received, *parts)
    chunk, sums = row_sums(parts)
    decoded = call(
        decoder_kernel,
        (quantized, left, right, up, down, dec_fwd),
        shaped((height, width, channels), BF16),
        [
            pltpu.VMEM((plane_rows, channels), F32),
            pltpu.VMEM((plane, 3 * channels), BF16),
        ],
        flops=conv_flops,
        moved=4 * 10**6,
    )
    latents_grad, norm_grads = call(
        last_kernel,
        (latents, back_act, back_plane, stats, gain, sums),
        (shaped((height, width, channels), BF16), shaped((2, channels))),
        flops=10**8,
        moved=6 * 10**6,
    )
    grads = gather_steps(chunk)
    encoder_weight_grad, decoder_weight_grad = [
        x.reshape(3, 3, channels, channels) for x in grads
    ]

    rows_f = received.astype(F32) * jnp.exp2(-jnp.round(sums[4, :devices]))[:, None, None]
    rows_f = rows_f.reshape(devices * cap, channels)
    high = lax.reduce_precision(rows_f, 8, 7)
    low = rows_f - high
    wide = jnp.concatenate([high.astype(BF16), low.astype(BF16)], 1)
    tags = gathered[:, 4, :cap].astype(jnp.int32).reshape(-1, 128)
    codebook_grad = call(
        owner_kernel,
        (tags, wide),
        shaped((shard, channels)),
        flops=2 * 10**9,
        moved=6 * 10**6,
    )
    return (
        decoded,
        latents_grad,
        norm_grads[1],
        norm_grads[0],
        encoder_weight_grad,
        decoder_weight_grad,
        codebook_grad,
    )


def solution(mesh):
    return jax.shard_map(
        body,
        mesh=mesh,
        in_specs=(
            P("row", "col", None),
            P("row", "col"),
            P(),
            P(),
            P(),
            P(),
            P(),
            P("row", "col", None),
        ),
        out_specs=(
            P("row", "col", None),
            P("row", "col", None),
            P(),
            P(),
            P(),
            P(),
            P(("row", "col"), None),
        ),
        check_vma=False,
    )
```

```python
import jax
import jax.numpy as jnp
from jax import lax
from jax.experimental import pallas as pl
from jax.experimental.pallas import tpu as pltpu
from jax.sharding import PartitionSpec as P

G = 32
epsilon = 1e-06
commit_beta = 0.25
F32 = jnp.float32
BF16 = jnp.bfloat16
F16 = jnp.float16
AXES = ("row", "col")
SIDE = 8
HALO = 2
VMEM = pl.BlockSpec(memory_space=pltpu.VMEM)
SMEM = pl.BlockSpec(memory_space=pltpu.SMEM)
ANY = pl.BlockSpec(memory_space=pltpu.HBM)
NT = (((1,), (1,)), ((), ()))
NN = (((1,), (0,)), ((), ()))
HIGH = lax.Precision.HIGHEST


class Late:
    def __init__(self, ref, copy):
        self.ref, self.copy = ref, copy
        copy.start()

    def get(self):
        if self.copy is not None:
            self.copy.wait()
            self.copy = None
        return self.ref


def call(kernel, ins, outs, scratch=(), specs=None, flops=0, moved=0, room=16, late=()):
    room = 56 if late else room
    specs = list(specs or [VMEM] * len(ins))
    first = len(ins) + len(jax.tree.leaves(outs)) + len(scratch)
    scratch = list(scratch)
    for i, field in late:
        specs[i] = ANY
        shape = ins[i].shape if field is None else ins[i].shape[1:]
        scratch.append(pltpu.VMEM(shape, ins[i].dtype))
    if late:
        scratch.append(pltpu.SemaphoreType.DMA((len(late),)))

    def wrapped(*refs):
        given = list(refs[:first])
        loads = []
        for j, (i, field) in enumerate(late):
            source = refs[i] if field is None else refs[i].at[field]
            copy = pltpu.make_async_copy(source, refs[first + j], refs[-1].at[j])
            given[i] = Late(refs[first + j], copy)
            loads.append(given[i])
        kernel(*given)
        for load in loads:
            load.get()

    return pl.pallas_call(
        wrapped,
        in_specs=specs,
        out_specs=jax.tree.map(lambda _: VMEM, outs),
        out_shape=outs,
        scratch_shapes=scratch,
        compiler_params=pltpu.CompilerParams(vmem_limit_bytes=room * 2**20),
        cost_estimate=pl.CostEstimate(flops=flops, bytes_accessed=moved, transcendentals=0),
    )(*ins)


def use(*refs):
    return [ref.get() if isinstance(ref, Late) else ref for ref in refs]


def shaped(shape, dtype=F32):
    return jax.ShapeDtypeStruct(shape, dtype)


def dot(a, b, dims=NN, precision=None):
    return lax.dot_general(a, b, dims, precision=precision, preferred_element_type=F32)


def front_kernel(devices, shard, cap, lat, ids, payload, slots):
    height, width = ids.shape
    count = height * width

    owner = lax.broadcasted_iota(jnp.int32, (devices, width), 0)
    upper = (
        lax.broadcasted_iota(jnp.int32, (width, width), 0)
        < lax.broadcasted_iota(jnp.int32, (width, width), 1)
    ).astype(BF16)
    slot_row = lax.broadcasted_iota(jnp.int32, (width, width), 0)
    base = jnp.zeros((devices, 1), F32)
    placed = jnp.zeros((devices, width), F32)
    for r in range(height):
        codes = ids[r : r + 1, :]
        dest = codes // shard
        local = codes - dest * shard
        member = owner == dest
        member_f = member.astype(F32)
        before = dot(member_f.astype(BF16), upper) + base
        rank = jnp.sum(member_f * before, 0, keepdims=True).astype(jnp.int32)
        slots[r : r + 1, :] = dest * cap + rank
        hit = (slot_row == rank).astype(BF16)
        tagged = local + 1
        high = tagged // 32
        low = tagged - high * 32
        zero = jnp.zeros((devices, width), F32)
        placed = placed + 32.0 * dot(
            jnp.where(member, high.astype(F32), zero).astype(BF16), hit, NT
        )
        placed = placed + dot(jnp.where(member, low.astype(F32), zero).astype(BF16), hit, NT)
        base = base + jnp.sum(member_f, 1, keepdims=True)
    (lat,) = use(lat)
    channels = lat.shape[2]

    def add_row(r, total):
        return total + jnp.sum(lat[r].astype(F32), 0, keepdims=True)

    mean = lax.fori_loop(0, height, add_row, jnp.zeros((1, channels), F32)) * (1.0 / count)

    def add_square(r, total):
        gap = lat[r].astype(F32) - mean
        return total + jnp.sum(gap * gap, 0, keepdims=True)

    square = lax.fori_loop(0, height, add_square, jnp.zeros((1, channels), F32))
    half = width
    rows = [mean[:, :half], mean[:, half:], square[:, :half], square[:, half:]]
    for i, part in enumerate(rows):
        payload[:, i, :] = jnp.broadcast_to(part, (devices, half))
    payload[:, 4, :] = placed
    payload[:, 5:, :] = jnp.zeros((devices, 3, half), F32)


def place_of():
    return (
        lax.axis_index("row"),
        lax.axis_index("col"),
        lax.axis_size("row"),
        lax.axis_size("col"),
    )


def place_of():
    return (
        lax.axis_index("row"),
        lax.axis_index("col"),
        lax.axis_size("row"),
        lax.axis_size("col"),
    )


def fill_tile(scr, own, left, right, up, down, ring):
    height, width, channels = own.shape
    pitch = width + 2 * SIDE
    for r in range(height):
        base = SIDE + (ring + r) * pitch
        scr[base + SIDE - HALO : base + SIDE] = left[r].astype(F32)
        scr[base + SIDE : base + SIDE + width] = own[r].astype(F32)
        scr[base + SIDE + width : base + SIDE + width + HALO] = right[r].astype(F32)
    span = up.shape[1]
    for i in range(ring):
        top = SIDE + i * pitch + SIDE - HALO
        scr[top : top + span] = up[HALO - ring + i].astype(F32)
        low = SIDE + (ring + height + i) * pitch + SIDE - HALO
        scr[low : low + span] = down[i].astype(F32)
    blank = jnp.zeros((SIDE - HALO, channels), F32)
    for r in range(height + 2 * ring):
        base = SIDE + r * pitch
        scr[base : base + SIDE - HALO] = blank
        scr[base + pitch - SIDE + HALO : base + pitch] = blank
    ends(scr, channels)


def ends(scr, channels):
    blank = jnp.zeros((SIDE, channels), F32)
    scr[0:SIDE] = blank
    scr[scr.shape[0] - SIDE :] = blank


def spread(scr, wide, count, pitch, channels):
    def one(r, _):
        value = scr[pl.ds(pl.multiple_of(r * pitch, 8), pitch + 2 * SIDE), :]
        at = pl.ds(pl.multiple_of(r * pitch, 16), pitch)
        for j in range(3):
            start = SIDE + j - 1
            wide[at, j * channels : (j + 1) * channels] = value[start : start + pitch].astype(BF16)
        return 0

    lax.fori_loop(0, count, one, 0)


def rows_at(r, pitch, count):
    return pl.ds(pl.multiple_of(r * pitch, 16), count * pitch)


def forward_rows(wide, weight, r, step, pitch):
    total = dot(wide[rows_at(r, pitch, step), :], weight[0])
    for dy in (1, 2):
        total = total + dot(wide[rows_at(r + dy, pitch, step), :], weight[dy])
    return total


def backward_rows(wide, weight, r, step, pitch):
    total = dot(wide[rows_at(r + 2, pitch, step), :], weight[0], NT)
    for dy in (1, 2):
        total = total + dot(wide[rows_at(r + 2 - dy, pitch, step), :], weight[dy], NT)
    return total


def kernel_grad(turned, wide, keep, give, pitch, height, first_row):
    channels = turned.shape[0]
    half = channels // 2
    count = height * pitch
    core = lax.axis_index("row") % 2
    for dy in range(3):
        start = (first_row + 1 - dy) * pitch
        product = dot(turned[...], wide[start : start + count, :])
        for j in range(3):
            at = (dy * 3 + 2 - j) * channels
            low = product[:, j * channels : j * channels + half]
            high = product[:, j * channels + half : (j + 1) * channels]

            keep[at : at + channels, :] = jnp.where(core == 0, low, high)
            give[at : at + channels, :] = jnp.where(core == 0, high, low)


def turn_own(own, turned):
    height, width, channels = own.shape
    pitch = width + 2 * SIDE
    blank = jnp.zeros((SIDE, channels), F32)
    for r in range(0, height, 8):
        parts = []
        for k in range(8):
            parts += [blank, own[r + k].astype(F32), blank]
        block = jnp.concatenate(parts, 0)
        turned[:, r * pitch : (r + 8) * pitch] = block.T.astype(BF16)


def decoder_grad_kernel(
    cot, codes, left, right, up, down, keep, give, scr, wide, turned
):
    cot, left, right, up, down = use(cot, left, right, up, down)
    height, width, channels = cot.shape
    pitch = width + 2 * SIDE
    fill_tile(scr, cot, left, right, up, down, 1)
    spread(scr, wide, height + 2, pitch, channels)
    turn_own(*use(codes), turned)
    kernel_grad(turned, wide, keep, give, pitch, height, 1)


def decoder_kernel(codes, left, right, up, down, weight, out, scr, wide):
    codes, left, right, up, down = use(codes, left, right, up, down)
    height, width, channels = codes.shape
    pitch = width + 2 * SIDE
    fill_tile(scr, codes, left, right, up, down, 1)
    spread(scr, wide, height + 2, pitch, channels)
    step = 4
    (weight,) = use(weight)

    def part(k, _):
        value = forward_rows(wide, weight, k * step, step, pitch)
        for u in range(step):
            at = u * pitch + SIDE
            out[k * step + u] = value[at : at + width].astype(BF16)
        return 0

    lax.fori_loop(0, height // step, part, 0)


def group_stats(gathered, height, width):
    devices = gathered.shape[0]
    rows, cols = lax.axis_size("row"), lax.axis_size("col")
    local = jnp.concatenate([gathered[:, 0, :], gathered[:, 1, :]], 1)
    square = jnp.concatenate([gathered[:, 2, :], gathered[:, 3, :]], 1)
    channels = local.shape[1]
    per_group = channels // G
    same = lax.broadcasted_iota(jnp.int32, (channels, channels), 0) // per_group
    same = same == lax.broadcasted_iota(jnp.int32, (channels, channels), 1) // per_group
    mix = jnp.where(same, 1.0 / per_group, 0.0).astype(F32)
    centre = jnp.broadcast_to(jnp.sum(local, 0, keepdims=True) * (1.0 / devices), (8, channels))
    mean = dot(centre, mix, precision=HIGH)[0:1]
    gap = local - mean
    spread_sum = square + (height * width) * (gap * gap)
    total = jnp.sum(spread_sum, 0, keepdims=True) * (1.0 / (devices * height * width))
    var = dot(jnp.broadcast_to(total, (8, channels)), mix, precision=HIGH)[0:1]
    return mean, lax.rsqrt(var + epsilon)


def inside_tile(row, col, rows, cols, height, width):
    pitch = width + 2 * SIDE
    place = lax.broadcasted_iota(jnp.int32, (pitch, 1), 0) - SIDE + col * width
    inside_col = (place >= 0) & (place < cols * width)

    def keep(line):
        high = row * height + line
        return inside_col & (high >= 0) & (high < rows * height)

    return keep


def encoder_kernel(
    code_scale,
    lat, left, right, up, down, codes, gathered, gain, bias, weight,
    z_out, pull, turned, stats, power,
    tmp_s, wide,
):
    height, width, channels = codes.ref.shape
    pitch = width + 2 * SIDE
    keep = inside_tile(*place_of(), height, width)
    mean, inv = group_stats(gathered, height, width)
    stats[0:1, :] = mean
    stats[1:2, :] = inv
    fill_tile(tmp_s, *use(lat, left, right, up, down), 2)
    z_out[...] = tmp_s[pitch : pitch + z_out.shape[0], :]
    scale = inv * gain[...]
    offset = bias[...]

    def smooth_row(r, _):
        at = pl.ds(pl.multiple_of(SIDE + r * pitch, 8), pitch)
        act = (tmp_s[at, :] - mean) * scale + offset
        value = act * jax.nn.sigmoid(act)
        tmp_s[at, :] = jnp.where(keep(r - 2), value, 0.0)
        return 0

    lax.fori_loop(0, height + 4, smooth_row, 0)
    spread(tmp_s, wide, height + 4, pitch, channels)
    blank = jnp.zeros((SIDE, channels), F32)
    for r in range(0, height, 8):
        parts = []
        for k in range(8):
            base = SIDE + (2 + r + k) * pitch + SIDE
            parts += [blank, tmp_s[base : base + width], blank]
        turned[:, r * pitch : (r + 8) * pitch] = jnp.concatenate(parts, 0).T.astype(BF16)
    step = 3
    power[...] = jnp.zeros(power.shape, F32)
    weight, codes = use(weight, codes)

    def part(k, _):
        r = k * step
        at = pl.ds(pl.multiple_of(SIDE + r * pitch, 8), step * pitch)
        z = z_out[at, :] + forward_rows(wide, weight, r, step, pitch)
        z_out[at, :] = z
        for u in range(step):
            line = r + u - 1

            @pl.when((line >= 0) & (line < height))
            def _():
                first = u * pitch + SIDE
                e = codes[line].astype(F32)
                own = pl.ds(pl.multiple_of(line * width, 8), width)
                some = (e - z[first : first + width]) * code_scale
                pull[own, :] = some
                power[...] = jnp.maximum(power[...], jnp.max(jnp.abs(some), 0, keepdims=True))

        return 0

    lax.fori_loop(0, (height + 2) // step, part, 0)
    top = jnp.max(power[...], 1, keepdims=True)
    power[...] = jnp.broadcast_to(exponent(top), power.shape)


def pack_kernel(slots, pull, power, packed):
    packed[...] = jnp.zeros(packed.shape, F32)
    scale = jnp.exp2(power[0:1, :])

    def some(i, _):
        value = pull[pl.ds(pl.multiple_of(i * 16, 8), 16), :] * scale
        for u in range(16):
            packed[pl.ds(slots[i * 16 + u], 1), :] = value[u : u + 1, :]
        return 0

    lax.fori_loop(0, pull.shape[0] // 16, some, 0)


def flip_weight(weight, flipped):
    channels = weight.shape[2]
    for dy in range(3):
        for j in range(3):
            flipped[dy, :, j * channels : (j + 1) * channels] = weight[dy, 2 - j]


def rotate_kernel(
    cot, left, right, up, down, codes, code_l, code_r, code_u, code_d, z_in, turned, dec_w, power,
    plane, keep_grad, give_grad,
    tmp_s, code_s, wide, back_wide, flipped,
):
    height, width, channels = cot.ref.shape
    pitch = width + 2 * SIDE
    fill_tile(tmp_s, *use(cot, left, right, up, down), 2)
    spread(tmp_s, wide, height + 4, pitch, channels)
    fill_tile(code_s, *use(codes, code_l, code_r, code_u, code_d), 1)
    flip_weight(*use(dec_w), flipped)
    ends(plane, channels)
    step = 3

    def part(k, _):
        r = k * step
        at = pl.ds(pl.multiple_of(SIDE + r * pitch, 8), step * pitch)
        plane[at, :] = backward_rows(wide, flipped, r, step, pitch)
        return 0

    lax.fori_loop(0, (height + 2) // step, part, 0)
    block = 24
    z_in, turned = use(z_in, turned)
    place = lax.broadcasted_iota(jnp.int32, (block, 1), 0)
    row, col, rows, cols = place_of()

    def total(x):
        return jnp.sum(x, 1, keepdims=True)

    def turn(line, _):
        spots = [
            pl.ds(pl.multiple_of(SIDE + line * pitch + b, 8), block)
            for b in range(0, pitch, block)
        ]
        sums = []
        for at in spots:
            z, e = z_in[at, :], code_s[at, :]
            sums.append((total(z * z) + epsilon, total(e * e) + epsilon))
        scales = []
        for at, (zz, ee) in zip(spots, sums):
            z, e, back = z_in[at, :], code_s[at, :], plane[at, :]
            z_inv, e_inv = lax.rsqrt(zz), lax.rsqrt(ee)
            e_unit = e * e_inv
            mirror = z * z_inv + e_unit
            scales.append(
                (z_inv, e_inv, ee, total(mirror * mirror) + epsilon, total(mirror * back),
                 total(e_unit * back))
            )
        high = row * height + line - 1
        keep = (high >= 0) & (high < rows * height)
        for b, (at, (z_inv, e_inv, ee, mm, along, code)) in enumerate(zip(spots, scales)):
            z, e, back = z_in[at, :], code_s[at, :], plane[at, :]
            stretch = ee * e_inv * z_inv
            along = 2.0 * along / mm
            z_part = stretch * z_inv * (2.0 * code - along) + commit_beta
            e_part = stretch * e_inv * along + commit_beta
            across = place + b * block - SIDE + col * width
            inside = keep & (across >= 0) & (across < cols * width)
            plane[at, :] = jnp.where(inside, stretch * back + z_part * z - e_part * e, 0.0)
        return 0

    lax.fori_loop(0, height + 2, turn, 0)
    spread(plane, back_wide, height + 2, pitch, channels)
    kernel_grad(turned, back_wide, keep_grad, give_grad, pitch, height, 1)
    taps, half = keep_grad.shape[0] - 8, keep_grad.shape[1]
    lane = lax.broadcasted_iota(jnp.int32, (8, half), 1)
    mine = jnp.where(lane == row * cols + col, power[:, :half], 0.0)
    keep_grad[taps:, :] = mine
    give_grad[taps:, :] = mine


def back_kernel(lat, plane, stats, gain, bias, enc_w, back_act, tail, back_wide, flipped):
    (plane,) = use(plane)
    height, width, channels = lat.ref.shape
    pitch = width + 2 * SIDE
    spread(plane, back_wide, height + 2, pitch, channels)
    flip_weight(*use(enc_w), flipped)
    (lat,) = use(lat)
    mean, inv = stats[0:1, :], stats[1:2, :]
    step = 4

    def last(k, totals):
        value = backward_rows(back_wide, flipped, k * step, step, pitch)
        first, second = totals
        for u in range(step):
            at = u * pitch + SIDE
            normed = (lat[k * step + u].astype(F32) - mean) * inv
            act = normed * gain[...] + bias[...]
            s = jax.nn.sigmoid(act)
            some = value[at : at + width] * s * (1.0 + act * (1.0 - s))
            back_act[k * step + u] = some
            first = first + jnp.sum(some, 0, keepdims=True)
            second = second + jnp.sum(some * normed, 0, keepdims=True)
        return first, second

    zero = jnp.zeros((1, channels), F32)
    first, second = lax.fori_loop(0, height // step, last, (zero, zero))
    half = channels // 2
    lines = [first[:, :half], first[:, half:], second[:, :half], second[:, half:]]
    tail[...] = jnp.concatenate(lines + [jnp.zeros((4, half), F32)], 0)


def last_kernel(lat, back_act, plane, stats, gain, *refs):
    pieces, (out, grads) = refs[:-2], refs[-2:]
    height, width, channels = lat.shape
    mean, inv = stats[0:1, :], stats[1:2, :]
    per_group = channels // G
    count = height * width * lax.axis_size("row") * lax.axis_size("col") * per_group
    end = pieces[0].shape[1] - 32
    sums = jnp.zeros((8, pieces[0].shape[2]), F32)
    for ref in pieces:
        for z in range(ref.shape[0]):
            some = ref[z, end : end + 8, :] + ref[z, end + 8 : end + 16, :]
            sums = sums + some * jnp.exp2(-ref[z, end + 16 : end + 24, :])
    first = jnp.concatenate([sums[0:1, :], sums[1:2, :]], 1)
    second = jnp.concatenate([sums[2:3, :], sums[3:4, :]], 1)
    grads[0:1, :] = first
    grads[1:2, :] = second
    same = lax.broadcasted_iota(jnp.int32, (channels, channels), 0) // per_group
    same = same == lax.broadcasted_iota(jnp.int32, (channels, channels), 1) // per_group
    mix = jnp.where(same, 1.0, 0.0).astype(F32)
    both = jnp.concatenate([first * gain[...], second * gain[...]] + [first] * 6, 0)
    means = dot(both, mix, precision=HIGH) * (1.0 / count)

    lat, back_act, plane = use(lat, back_act, plane)

    def one(r, _):
        normed = (lat[r].astype(F32) - mean) * inv
        d = back_act[r] * gain[...]
        at = pl.multiple_of((r + 1) * (width + 2 * SIDE) + 2 * SIDE, 8)
        enc_back = plane[pl.ds(at, width), :]
        out[r] = (inv * (d - means[0:1] - normed * means[1:2]) + enc_back).astype(BF16)
        return 0

    lax.fori_loop(0, height, one, 0)


def owner_kernel(tags, wide, out):
    shard, channels = out.shape
    total = jnp.zeros((shard, 2 * channels), F32)
    rows = wide.shape[0]
    chunk = 1024
    code = lax.broadcasted_iota(jnp.int32, (shard, tags.shape[1]), 0) + 1
    lines = chunk // tags.shape[1]
    for k in range(rows // chunk):
        hit = jnp.concatenate(
            [
                (code == tags[k * lines + u : k * lines + u + 1, :]).astype(F32).astype(BF16)
                for u in range(lines)
            ],
            1,
        )
        total = total + dot(hit, wide[k * chunk : (k + 1) * chunk, :])
    out[...] = total[:, :channels] + total[:, channels:]


def exponent(biggest):
    return 14.0 - jnp.ceil(jnp.log2(jnp.maximum(biggest, 1e-30)))


def exchange(x):
    return lax.all_to_all(x, AXES, split_axis=0, concat_axis=0, tiled=True)


def pair_swap(x):
    size = lax.axis_size("row")
    return lax.ppermute(x, "row", [(i, i ^ 1) for i in range(size)])


def shifts(n, stride=1):
    size = n * stride
    return [[((i + s * stride) % size, i) for i in range(size)] for s in range(1, n)]


def columns_kernel(cols, *refs):
    ins, outs = refs[:-cols], refs[-cols:]
    col = lax.axis_index("col")
    extra = ins[0].shape[0] % 256
    taps = ins[0].shape[0] - extra
    lines = taps // cols
    for s, out in enumerate(outs):
        at = pl.ds(pl.multiple_of((col + cols - s) % cols * lines, 8), lines)
        out[:lines, :] = ins[0][at, :] + ins[1][at, :]
        if extra:
            out[lines:, :] = ins[0][taps:, :] + ins[1][taps:, :]


def rows_kernel(cols, *refs):
    parts, outs = (refs[:cols], refs[cols : 2 * cols]), refs[2 * cols :]
    row, _, rows, _ = place_of()
    depth = rows // 2
    lines = outs[0].shape[0] // 2 - 4

    def added(some, first, count):
        value = some[0][first : first + count, :]
        for ref in some[1:]:
            value = value + ref[first : first + count, :]
        return value

    tail = added(parts[0], depth * lines, 8)
    for z in range(depth):
        values = [added(some, z * lines, lines) for some in parts]
        for s, out in enumerate(outs):

            @pl.when((row // 2 + depth - s) % depth == z)
            def _():
                for i in range(2):
                    out[i * lines : (i + 1) * lines, :] = values[i]

    for out in outs:
        out[2 * lines :, :] = tail


def chunk_kernel(depth, *refs):
    parts, (tail, tail_b, out, powers) = refs[:depth], refs[depth:]
    half = out.shape[1]
    lines = parts[0].shape[0] // 2 - 4
    value = parts[0][...]
    for ref in parts[1:]:
        value = value + ref[...]
    powers[...] = value[2 * lines :]
    values = [value[:lines], value[lines : 2 * lines], tail[...] + tail_b[...]]
    ends = (2 * lines, 2 * lines + 8, 2 * lines + 32)
    for i, (some, at) in enumerate(zip(values, ends)):
        top = jnp.max(jnp.max(jnp.abs(some), 0, keepdims=True), 1, keepdims=True)
        power = exponent(top)
        some = some * jnp.exp2(power)
        if i < 2:
            out[i * lines : (i + 1) * lines, :] = some
        else:
            high = some.astype(BF16).astype(F32)
            out[at - 16 : at - 8, :] = high
            out[at - 8 : at, :] = some - high
        out[at : at + 8, :] = jnp.broadcast_to(power, (8, half))
    out[2 * lines + 40 :, :] = jnp.zeros((8, half), F32)


def column_parts(arrays):
    cols = lax.axis_size("col")
    taps, half = arrays[0].shape
    extra = taps % 256
    parts = call(
        lambda *refs: columns_kernel(cols, *refs),
        arrays,
        [shaped(((taps - extra) // cols + extra, half))] * cols,
        moved=4 * 10**6,
    )
    return list(parts)


def column_send(parts):
    cols = lax.axis_size("col")
    return [parts[0]] + [lax.ppermute(x, "col", p) for x, p in zip(parts[1:], shifts(cols))]


def row_sums(enc, dec, tail):
    cols, depth = len(enc), lax.axis_size("row") // 2
    taps, half = dec[0].shape
    lines = taps // depth
    parts = call(
        lambda *refs: rows_kernel(cols, *refs),
        enc + dec,
        [shaped((2 * lines + 8, half))] * depth,
        moved=4 * 10**6,
    )
    parts = [parts[0]] + [lax.ppermute(x, "row", p) for x, p in zip(parts[1:], shifts(depth, 2))]
    return call(
        lambda *refs: chunk_kernel(depth, *refs),
        parts + [tail, pair_swap(tail)],
        (shaped((2 * lines + 48, half)), shaped((8, half))),
        moved=10**6,
    )


def gather_rows(chunk):
    own = chunk.astype(F16)
    steps = shifts(lax.axis_size("row") // 2, 2)
    return jnp.stack([own] + [lax.ppermute(own, "row", p) for p in steps])


def gather_columns(own):
    return [own] + [lax.ppermute(own, "col", p) for p in shifts(lax.axis_size("col"))]


def gather_cores(own, other):
    rows, cols = lax.axis_size("row"), lax.axis_size("col")
    lines, half = own[0].shape[1] // 2 - 24, own[0].shape[2]
    chunks = cols * rows // 2
    return call(
        lambda *refs: assemble_kernel(lines, *refs),
        own + other,
        (shaped((chunks, lines, 2 * half)), shaped((chunks, lines, 2 * half))),
        moved=10**7,
    )


def assemble_kernel(lines, *refs):
    pieces, outs = refs[:-2], refs[-2:]
    row, col, rows, cols = place_of()
    depth = rows // 2
    half = outs[0].shape[2] // 2
    for k, ref in enumerate(pieces):
        core = (row + k // cols) % 2
        c = (col + k % cols) % cols
        lanes = pl.ds(pl.multiple_of(core * half, half), half)
        for s in range(depth):
            z = (row // 2 + s) % depth
            for i, out in enumerate(outs):
                at = 2 * lines + 8 * i
                scale = jnp.exp2(-ref[s, at : at + 1, :])
                value = ref[s, i * lines : (i + 1) * lines, :] * scale
                out[c * depth + z, :, lanes] = value


def halo(fields):
    rows, cols = lax.axis_size("row"), lax.axis_size("col")
    forth = lambda n: [(i, i + 1) for i in range(n - 1)]
    back = lambda n: [(i + 1, i) for i in range(n - 1)]
    left_edge = jnp.stack([x[:, :HALO] for x in fields])
    right_edge = jnp.stack([x[:, -HALO:] for x in fields])
    left = lax.ppermute(right_edge, "col", forth(cols))
    right = lax.ppermute(left_edge, "col", back(cols))

    def lines(at):
        return jnp.concatenate([left[:, at], jnp.stack([x[at] for x in fields]), right[:, at]], 2)

    up = lax.ppermute(lines(slice(-HALO, None)), "row", forth(rows))
    down = lax.ppermute(lines(slice(0, HALO)), "row", back(rows))
    return left, right, up, down


def body(
    latents,
    code_ids,
    norm_gain,
    norm_bias,
    encoder_weight,
    codebook,
    decoder_weight,
    decoded_cotangent,
):
    height, width, channels = latents.shape
    devices = lax.axis_size("row") * lax.axis_size("col")
    codes_total = codebook.shape[0]
    shard = codes_total // devices
    count = height * width
    cap = 2 * count // devices
    pitch = width + 2 * SIDE
    conv_flops = 2 * count * 9 * channels * channels
    taps = 9 * channels
    half = channels // 2
    plane = (height + 2) * pitch
    plane_rows = plane + 2 * SIDE
    big = (height + 4) * pitch
    after = lambda *x: lax.optimization_barrier(x)
    halos = lambda field, start: [(start + i, field) for i in range(4)]

    payload, slots = call(
        lambda *refs: front_kernel(devices, shard, cap, *refs),
        (latents, code_ids),
        (shaped((devices, 8, width)), shaped((height, width), jnp.int32)),
        flops=10**9,
        moved=10**6,
        late=[(0, None)],
    )
    payload, code_ids, latents, decoded_cotangent = after(
        payload, code_ids, latents, decoded_cotangent
    )
    gathered = exchange(payload)
    quantized = codebook[code_ids]
    left, right, up, down = halo((latents, decoded_cotangent, quantized))
    gain = norm_gain.reshape(1, channels)
    bias = norm_bias.reshape(1, channels)

    dec_grad = call(
        decoder_grad_kernel,
        (decoded_cotangent, quantized, left, right, up, down),
        (shaped((taps, half)), shaped((taps, half))),
        [
            pltpu.VMEM((plane_rows, channels), F32),
            pltpu.VMEM((plane, 3 * channels), BF16),
            pltpu.VMEM((channels, height * pitch), BF16),
        ],
        flops=conv_flops,
        moved=5 * 10**6,
        late=[(0, None), *halos(1, 2), (1, None)],
    )
    dec_keep, dec_give = dec_grad
    gathered, dec_keep, dec_give = after(gathered, dec_keep, dec_give)
    dec_given = pair_swap(dec_give)
    enc_fwd = encoder_weight.reshape(3, 3 * channels, channels)
    dec_fwd = decoder_weight.reshape(3, 3 * channels, channels)
    code_scale = codes_total / (count * devices)
    z, pull, turned, stats, power = call(
        lambda *refs: encoder_kernel(code_scale, *refs),
        (latents, left, right, up, down, quantized, gathered, gain, bias, enc_fwd),
        (
            shaped((plane_rows, channels)),
            shaped((count, channels)),
            shaped((channels, height * pitch), BF16),
            shaped((8, channels)),
            shaped((8, channels)),
        ),
        [
            pltpu.VMEM((big + 2 * SIDE, channels), F32),
            pltpu.VMEM((big, 3 * channels), BF16),
        ],
        flops=conv_flops,
        moved=10 * 10**6,
        room=20,
        late=[(0, None), *halos(0, 1), (9, None), (5, None)],
    )
    dec_parts = column_parts((dec_keep, dec_given))
    pull, *dec_parts = after(pull, *dec_parts)
    dec_parts = column_send(dec_parts)
    packed = call(
        pack_kernel,
        (slots.reshape(-1), pull, power),
        shaped((devices * cap, channels)),
        specs=[SMEM, VMEM, VMEM],
        flops=5 * 10**9,
        moved=6 * 10**6,
    )
    send = packed.astype(F16).reshape(devices, cap, channels)
    send, z, *dec_parts = after(send, z, *dec_parts)
    received = exchange(send)

    back_plane, keep_grad, give_grad = call(
        rotate_kernel,
        (
            decoded_cotangent, left, right, up, down, quantized, left, right, up, down, z, turned,
            decoder_weight, power,
        ),
        (
            shaped((plane_rows, channels)),
            shaped((taps + 8, half)),
            shaped((taps + 8, half)),
        ),
        [
            pltpu.VMEM((big + 2 * SIDE, channels), F32),
            pltpu.VMEM((plane_rows, channels), F32),
            pltpu.VMEM((big, 3 * channels), BF16),
            pltpu.VMEM((plane, 3 * channels), BF16),
            pltpu.VMEM((3, channels, 3 * channels), BF16),
        ],
        flops=2 * conv_flops,
        moved=15 * 10**6,
        room=32,
        late=[
            (0, None), *halos(1, 1), (5, None), *halos(2, 6), (12, None), (10, None), (11, None)
        ],
    )
    enc_parts = column_send(column_parts((keep_grad, pair_swap(give_grad))))
    back_act, tail = call(
        back_kernel,
        (latents, back_plane, stats, gain, bias, encoder_weight),
        (shaped((height, width, channels)), shaped((8, half))),
        [
            pltpu.VMEM((plane, 3 * channels), BF16),
            pltpu.VMEM((3, channels, 3 * channels), BF16),
        ],
        flops=conv_flops,
        moved=8 * 10**6,
        late=[(1, None), (5, None), (0, None)],
    )
    decoded = call(
        decoder_kernel,
        (quantized, left, right, up, down, dec_fwd),
        shaped((height, width, channels), BF16),
        [
            pltpu.VMEM((plane_rows, channels), F32),
            pltpu.VMEM((plane, 3 * channels), BF16),
        ],
        flops=conv_flops,
        moved=4 * 10**6,
        late=[(0, None), *halos(2, 1), (5, None)],
    )
    decoded, *enc_parts = after(decoded, *enc_parts)
    chunk, powers = row_sums(enc_parts, dec_parts, tail)
    own = gather_rows(chunk)
    pieces = gather_columns(own)

    rows_f = received.astype(F32) * jnp.exp2(-jnp.round(powers[0, :devices]))[:, None, None]
    rows_f = rows_f.reshape(devices * cap, channels)
    high = lax.reduce_precision(rows_f, 8, 7)
    low = rows_f - high
    wide = jnp.concatenate([high.astype(BF16), low.astype(BF16)], 1)
    tags = gathered[:, 4, :cap].astype(jnp.int32).reshape(-1, 128)
    codebook_grad = call(
        owner_kernel,
        (tags, wide),
        shaped((shard, channels)),
        flops=2 * 10**9,
        moved=6 * 10**6,
    )
    codebook_grad, *pieces = after(codebook_grad, *pieces)
    other = [pair_swap(x) for x in pieces]
    own = [x.astype(F32) for x in pieces]
    latents_grad, norm_grads = call(
        last_kernel,
        (latents, back_act, back_plane, stats, gain, *own),
        (shaped((height, width, channels), BF16), shaped((2, channels))),
        flops=10**8,
        moved=6 * 10**6,
    )
    other = [x.astype(F32) for x in other]
    encoder_weight_grad, decoder_weight_grad = [
        x.reshape(3, 3, channels, channels) for x in gather_cores(own, other)
    ]
    return (
        decoded,
        latents_grad,
        norm_grads[1],
        norm_grads[0],
        encoder_weight_grad,
        decoder_weight_grad,
        codebook_grad,
    )


def solution(mesh):
    return jax.shard_map(
        body,
        mesh=mesh,
        in_specs=(
            P("row", "col", None),
            P("row", "col"),
            P(),
            P(),
            P(),
            P(),
            P(),
            P("row", "col", None),
        ),
        out_specs=(
            P("row", "col", None),
            P("row", "col", None),
            P(),
            P(),
            P(),
            P(),
            P(("row", "col"), None),
        ),
        check_vma=False,
    )
```

```python
import jax
import jax.numpy as jnp
from jax import lax
from jax.experimental import pallas as pl
from jax.experimental.pallas import tpu as pltpu
from jax.sharding import PartitionSpec as P

G = 32
epsilon = 1e-06
commit_beta = 0.25
F32 = jnp.float32
BF16 = jnp.bfloat16
F16 = jnp.float16
AXES = ("row", "col")
SIDE = 8
HALO = 2
VMEM = pl.BlockSpec(memory_space=pltpu.VMEM)
SMEM = pl.BlockSpec(memory_space=pltpu.SMEM)
ANY = pl.BlockSpec(memory_space=pltpu.HBM)
NT = (((1,), (1,)), ((), ()))
NN = (((1,), (0,)), ((), ()))
HIGH = lax.Precision.HIGHEST


class Late:
    def __init__(self, ref, copy):
        self.ref, self.copy = ref, copy
        copy.start()

    def get(self):
        if self.copy is not None:
            self.copy.wait()
            self.copy = None
        return self.ref


def call(kernel, ins, outs, scratch=(), specs=None, flops=0, moved=0, room=16, late=(), far=()):
    room = 56 if late else room
    specs = list(specs or [VMEM] * len(ins))
    first = len(ins) + len(jax.tree.leaves(outs)) + len(scratch)
    scratch = list(scratch)
    for i, field in late:
        specs[i] = ANY
        shape = ins[i].shape if field is None else ins[i].shape[1:]
        scratch.append(pltpu.VMEM(shape, ins[i].dtype))
    if late:
        scratch.append(pltpu.SemaphoreType.DMA((len(late),)))

    def wrapped(*refs):
        given = list(refs[:first])
        loads = []
        for j, (i, field) in enumerate(late):
            source = refs[i] if field is None else refs[i].at[field]
            copy = pltpu.make_async_copy(source, refs[first + j], refs[-1].at[j])
            given[i] = Late(refs[first + j], copy)
            loads.append(given[i])
        kernel(*given)
        for load in loads:
            load.get()

    return pl.pallas_call(
        wrapped,
        in_specs=specs,
        out_specs=jax.tree.unflatten(
            jax.tree.structure(outs),
            [ANY if i in far else VMEM for i in range(len(jax.tree.leaves(outs)))],
        ),
        out_shape=outs,
        scratch_shapes=scratch,
        compiler_params=pltpu.CompilerParams(vmem_limit_bytes=room * 2**20),
        cost_estimate=pl.CostEstimate(flops=flops, bytes_accessed=moved, transcendentals=0),
    )(*ins)


def use(*refs):
    return [ref.get() if isinstance(ref, Late) else ref for ref in refs]


def shaped(shape, dtype=F32):
    return jax.ShapeDtypeStruct(shape, dtype)


def dot(a, b, dims=NN, precision=None):
    return lax.dot_general(a, b, dims, precision=precision, preferred_element_type=F32)


def front_kernel(devices, shard, cap, lat, ids, payload, slots):
    height, width = ids.shape
    count = height * width

    owner = lax.broadcasted_iota(jnp.int32, (devices, width), 0)
    upper = (
        lax.broadcasted_iota(jnp.int32, (width, width), 0)
        < lax.broadcasted_iota(jnp.int32, (width, width), 1)
    ).astype(BF16)
    slot_row = lax.broadcasted_iota(jnp.int32, (width, width), 0)
    members, codes, dests = [], [], []
    for r in range(height):
        code = ids[r : r + 1, :]
        dest = code // shard
        codes.append(code - dest * shard)
        dests.append(dest)
        members.append((owner == dest).astype(F32))
    stacked = jnp.concatenate([x.astype(BF16) for x in members], 0)
    before = dot(stacked, upper)
    base = jnp.zeros((devices, 1), F32)
    hits, parts = [], []
    for r in range(height):
        member = members[r]
        count_before = before[r * devices : (r + 1) * devices] + base
        rank = jnp.sum(member * count_before, 0, keepdims=True).astype(jnp.int32)
        slots[r : r + 1, :] = dests[r] * cap + rank
        hits.append((slot_row == rank).astype(BF16))
        tagged = codes[r] + 1
        high = tagged // 32
        low = tagged - high * 32
        both = [member * high.astype(F32), member * low.astype(F32)]
        parts.append(jnp.concatenate(both, 0).astype(BF16))
        base = base + jnp.sum(member, 1, keepdims=True)
    placed = dot(jnp.concatenate(parts, 1), jnp.concatenate(hits, 1), NT)
    placed = 32.0 * placed[:devices] + placed[devices:]
    (lat,) = use(lat)
    channels = lat.shape[2]

    def add_row(r, total):
        return total + jnp.sum(lat[r].astype(F32), 0, keepdims=True)

    mean = lax.fori_loop(0, height, add_row, jnp.zeros((1, channels), F32)) * (1.0 / count)

    def add_square(r, total):
        gap = lat[r].astype(F32) - mean
        return total + jnp.sum(gap * gap, 0, keepdims=True)

    square = lax.fori_loop(0, height, add_square, jnp.zeros((1, channels), F32))
    half = width
    rows = [mean[:, :half], mean[:, half:], square[:, :half], square[:, half:]]
    for i, part in enumerate(rows):
        payload[:, i, :] = jnp.broadcast_to(part, (devices, half))
    payload[:, 4, :] = placed
    payload[:, 5:, :] = jnp.zeros((devices, 3, half), F32)


def place_of():
    return (
        lax.axis_index("row"),
        lax.axis_index("col"),
        lax.axis_size("row"),
        lax.axis_size("col"),
    )


def place_of():
    return (
        lax.axis_index("row"),
        lax.axis_index("col"),
        lax.axis_size("row"),
        lax.axis_size("col"),
    )


def fill_tile(scr, own, left, right, up, down, ring):
    height, width, channels = own.shape
    pitch = width + 2 * SIDE
    for r in range(height):
        base = SIDE + (ring + r) * pitch
        scr[base + SIDE - HALO : base + SIDE] = left[r].astype(F32)
        scr[base + SIDE : base + SIDE + width] = own[r].astype(F32)
        scr[base + SIDE + width : base + SIDE + width + HALO] = right[r].astype(F32)
    span = up.shape[1]
    for i in range(ring):
        top = SIDE + i * pitch + SIDE - HALO
        scr[top : top + span] = up[HALO - ring + i].astype(F32)
        low = SIDE + (ring + height + i) * pitch + SIDE - HALO
        scr[low : low + span] = down[i].astype(F32)
    blank = jnp.zeros((SIDE - HALO, channels), F32)
    for r in range(height + 2 * ring):
        base = SIDE + r * pitch
        scr[base : base + SIDE - HALO] = blank
        scr[base + pitch - SIDE + HALO : base + pitch] = blank
    ends(scr, channels)


def ends(scr, channels):
    blank = jnp.zeros((SIDE, channels), F32)
    scr[0:SIDE] = blank
    scr[scr.shape[0] - SIDE :] = blank


def spread(scr, wide, count, pitch, channels):
    def one(r, _):
        value = scr[pl.ds(pl.multiple_of(r * pitch, 8), pitch + 2 * SIDE), :]
        at = pl.ds(pl.multiple_of(r * pitch, 16), pitch)
        for j in range(3):
            start = SIDE + j - 1
            wide[at, j * channels : (j + 1) * channels] = value[start : start + pitch].astype(BF16)
        return 0

    lax.fori_loop(0, count, one, 0)


def rows_at(r, pitch, count):
    if isinstance(r, int):
        return slice(r * pitch, (r + count) * pitch)
    return pl.ds(pl.multiple_of(r * pitch, 16), count * pitch)


def forward_rows(wide, weight, r, step, pitch):
    total = dot(wide[rows_at(r, pitch, step), :], weight[0])
    for dy in (1, 2):
        total = total + dot(wide[rows_at(r + dy, pitch, step), :], weight[dy])
    return total


def backward_rows(wide, weight, r, step, pitch):
    total = dot(wide[rows_at(r + 2, pitch, step), :], weight[0], NT)
    for dy in (1, 2):
        total = total + dot(wide[rows_at(r + 2 - dy, pitch, step), :], weight[dy], NT)
    return total


def kernel_grad(turned, wide, keep, give, pitch, height, first_row):
    channels = turned.shape[0]
    half = channels // 2
    count = height * pitch
    core = lax.axis_index("row") % 2
    for dy in range(3):
        start = (first_row + 1 - dy) * pitch
        product = dot(turned[...], wide[start : start + count, :])
        for j in range(3):
            at = (dy * 3 + 2 - j) * channels
            low = product[:, j * channels : j * channels + half]
            high = product[:, j * channels + half : (j + 1) * channels]

            keep[at : at + channels, :] = jnp.where(core == 0, low, high)
            give[at : at + channels, :] = jnp.where(core == 0, high, low)


def turn_own(own, turned):
    height, width, channels = own.shape
    pitch = width + 2 * SIDE
    blank = jnp.zeros((SIDE, channels), F32)
    for r in range(0, height, 8):
        parts = []
        for k in range(8):
            parts += [blank, own[r + k].astype(F32), blank]
        block = jnp.concatenate(parts, 0)
        turned[:, r * pitch : (r + 8) * pitch] = block.T.astype(BF16)


def decoder_grad_kernel(
    cot, codes, left, right, up, down, keep, give, scr, wide, turned
):
    cot, left, right, up, down = use(cot, left, right, up, down)
    height, width, channels = cot.shape
    pitch = width + 2 * SIDE
    fill_tile(scr, cot, left, right, up, down, 1)
    spread(scr, wide, height + 2, pitch, channels)
    turn_own(*use(codes), turned)
    kernel_grad(turned, wide, keep, give, pitch, height, 1)


def decoder_kernel(codes, left, right, up, down, weight, out, scr, wide):
    codes, left, right, up, down = use(codes, left, right, up, down)
    height, width, channels = codes.shape
    pitch = width + 2 * SIDE
    fill_tile(scr, codes, left, right, up, down, 1)
    spread(scr, wide, height + 2, pitch, channels)
    step = 4
    (weight,) = use(weight)

    def part(k, _):
        value = forward_rows(wide, weight, k * step, step, pitch)
        for u in range(step):
            at = u * pitch + SIDE
            out[k * step + u] = value[at : at + width].astype(BF16)
        return 0

    lax.fori_loop(0, height // step, part, 0)


def group_stats(gathered, height, width):
    devices = gathered.shape[0]
    rows, cols = lax.axis_size("row"), lax.axis_size("col")
    local = jnp.concatenate([gathered[:, 0, :], gathered[:, 1, :]], 1)
    square = jnp.concatenate([gathered[:, 2, :], gathered[:, 3, :]], 1)
    channels = local.shape[1]
    per_group = channels // G
    same = lax.broadcasted_iota(jnp.int32, (channels, channels), 0) // per_group
    same = same == lax.broadcasted_iota(jnp.int32, (channels, channels), 1) // per_group
    mix = jnp.where(same, 1.0 / per_group, 0.0).astype(F32)
    centre = jnp.broadcast_to(jnp.sum(local, 0, keepdims=True) * (1.0 / devices), (8, channels))
    mean = dot(centre, mix, precision=HIGH)[0:1]
    gap = local - mean
    spread_sum = square + (height * width) * (gap * gap)
    total = jnp.sum(spread_sum, 0, keepdims=True) * (1.0 / (devices * height * width))
    var = dot(jnp.broadcast_to(total, (8, channels)), mix, precision=HIGH)[0:1]
    return mean, lax.rsqrt(var + epsilon)


def inside_tile(row, col, rows, cols, height, width):
    pitch = width + 2 * SIDE
    place = lax.broadcasted_iota(jnp.int32, (pitch + 2 * SIDE, 1), 0) - 2 * SIDE + col * width
    inside_col = (place >= 0) & (place < cols * width)

    def keep(line):
        high = row * height + line
        return inside_col & (high >= 0) & (high < rows * height)

    return keep


def encoder_kernel(
    code_scale,
    lat, left, right, up, down, codes, gathered, gain, bias, weight,
    z_far, pull, turned_far, stats, power,
    tmp_s, wide, z_out, turned, own_s, sems,
):
    height, width, channels = codes.ref.shape
    pitch = width + 2 * SIDE
    keep = inside_tile(*place_of(), height, width)
    mean, inv = group_stats(gathered, height, width)
    stats[0:1, :] = mean
    stats[1:2, :] = inv
    fill_tile(tmp_s, *use(lat, left, right, up, down), 2)
    scale = inv * gain[...]
    offset = bias[...]

    blank = jnp.zeros((SIDE, channels), F32)

    def smooth_row(r):
        act = (tmp_s[r * pitch : (r + 1) * pitch + 2 * SIDE, :] - mean) * scale + offset
        value = jnp.where(keep(r - 2), act * jax.nn.sigmoid(act), 0.0)
        at = slice(r * pitch, (r + 1) * pitch)
        for j in range(3):
            start = SIDE + j - 1
            wide[at, j * channels : (j + 1) * channels] = value[start : start + pitch].astype(BF16)
        if 2 <= r < height + 2:
            base = (r - 2) * pitch
            own_s[base : base + SIDE, :] = blank
            own_s[base + SIDE : base + SIDE + width, :] = value[2 * SIDE : 2 * SIDE + width]
            own_s[base + SIDE + width : base + pitch, :] = blank

    step = 3
    steps = (height + 2) // step
    ends(z_out, channels)
    weight, codes = use(weight, codes)

    def z_copy(k):
        at = slice(SIDE + k * step * pitch, SIDE + (k + 1) * step * pitch)
        return pltpu.make_async_copy(z_out.at[at, :], z_far.at[at, :], sems.at[k])

    def part(k):
        first = SIDE + k * step * pitch
        count = step * pitch
        z = tmp_s[first + pitch : first + pitch + count, :]
        z = z + forward_rows(wide, weight, k * step, step, pitch)
        z_out[first : first + count, :] = z
        z_copy(k).start()
        tops = []
        for u in range(step):
            line = k * step + u - 1
            if 0 <= line < height:
                at = u * pitch + SIDE
                some = (codes[line].astype(F32) - z[at : at + width]) * code_scale
                pull[line * width : (line + 1) * width, :] = some
                tops.append(jnp.max(jnp.abs(some), 0, keepdims=True))
        return tops

    for r in range(step + 2):
        smooth_row(r)
    tops = []
    for k in range(steps):
        for r in range((k + 1) * step + 2, min((k + 2) * step + 2, height + 4)):
            smooth_row(r)
        tops += part(k)
    for r in range(0, height, 8):
        at = slice(r * pitch, (r + 8) * pitch)
        turned[:, at] = own_s[at, :].T.astype(BF16)
    turned_copy = pltpu.make_async_copy(turned, turned_far, sems.at[steps])
    turned_copy.start()
    top = jnp.max(jnp.concatenate(tops, 0), 0, keepdims=True)
    top = jnp.max(top, 1, keepdims=True)
    power[...] = jnp.broadcast_to(exponent(top), power.shape)
    for k in range(steps):
        z_copy(k).wait()
    turned_copy.wait()


def pack_kernel(slots, pull, power, packed):
    packed[...] = jnp.zeros(packed.shape, F32)
    scale = jnp.exp2(power[0:1, :])

    def some(i, _):
        value = pull[pl.ds(pl.multiple_of(i * 16, 8), 16), :] * scale
        for u in range(16):
            packed[pl.ds(slots[i * 16 + u], 1), :] = value[u : u + 1, :]
        return 0

    lax.fori_loop(0, pull.shape[0] // 16, some, 0)


def flip_weight(weight, flipped):
    channels = weight.shape[2]
    for dy in range(3):
        for j in range(3):
            flipped[dy, :, j * channels : (j + 1) * channels] = weight[dy, 2 - j]


def rotate_kernel(
    cot, left, right, up, down, codes, code_l, code_r, code_u, code_d, z_in, turned, dec_w, power,
    plane_far, keep_grad, give_grad,
    tmp_s, code_s, wide, back_wide, flipped, plane, sem,
):
    height, width, channels = cot.ref.shape
    pitch = width + 2 * SIDE
    fill_tile(tmp_s, *use(cot, left, right, up, down), 2)
    spread(tmp_s, wide, height + 4, pitch, channels)
    fill_tile(code_s, *use(codes, code_l, code_r, code_u, code_d), 1)
    flip_weight(*use(dec_w), flipped)
    ends(plane, channels)
    step = 3
    chunks = (height + 2) // step

    def part(k):
        at = slice(SIDE + k * step * pitch, SIDE + (k + 1) * step * pitch)
        plane[at, :] = backward_rows(wide, flipped, k * step, step, pitch)

    block = 24
    z_in, turned = use(z_in, turned)
    place = lax.broadcasted_iota(jnp.int32, (block, 1), 0)
    row, col, rows, cols = place_of()

    def total(x):
        return jnp.sum(x, 1, keepdims=True)

    def turn(line):
        spots = [
            slice(SIDE + line * pitch + b, SIDE + line * pitch + b + block)
            for b in range(0, pitch, block)
        ]
        sums = []
        for at in spots:
            z, e = z_in[at, :], code_s[at, :]
            sums.append((total(z * z) + epsilon, total(e * e) + epsilon))
        scales = []
        for at, (zz, ee) in zip(spots, sums):
            z, e, back = z_in[at, :], code_s[at, :], plane[at, :]
            z_inv, e_inv = lax.rsqrt(zz), lax.rsqrt(ee)
            e_unit = e * e_inv
            mirror = z * z_inv + e_unit
            scales.append(
                (z_inv, e_inv, ee, total(mirror * mirror) + epsilon, total(mirror * back),
                 total(e_unit * back))
            )
        high = row * height + line - 1
        keep = (high >= 0) & (high < rows * height)
        for b, (at, (z_inv, e_inv, ee, mm, along, code)) in enumerate(zip(spots, scales)):
            z, e, back = z_in[at, :], code_s[at, :], plane[at, :]
            stretch = ee * e_inv * z_inv
            along = 2.0 * along / mm
            z_part = stretch * z_inv * (2.0 * code - along) + commit_beta
            e_part = stretch * e_inv * along + commit_beta
            across = place + b * block - SIDE + col * width
            inside = keep & (across >= 0) & (across < cols * width)
            plane[at, :] = jnp.where(inside, stretch * back + z_part * z - e_part * e, 0.0)

    part(0)
    for k in range(chunks):
        if k + 1 < chunks:
            part(k + 1)
        for u in range(step):
            turn(k * step + u)
    plane_copy = pltpu.make_async_copy(plane, plane_far, sem)
    plane_copy.start()
    spread(plane, back_wide, height + 2, pitch, channels)
    kernel_grad(turned, back_wide, keep_grad, give_grad, pitch, height, 1)
    taps, half = keep_grad.shape[0] - 8, keep_grad.shape[1]
    lane = lax.broadcasted_iota(jnp.int32, (8, half), 1)
    mine = jnp.where(lane == row * cols + col, power[:, :half], 0.0)
    keep_grad[taps:, :] = mine
    give_grad[taps:, :] = mine
    plane_copy.wait()


def back_kernel(lat, plane, stats, gain, bias, enc_w, back_act, tail, back_wide, flipped):
    (plane,) = use(plane)
    height, width, channels = lat.ref.shape
    pitch = width + 2 * SIDE
    spread(plane, back_wide, height + 2, pitch, channels)
    flip_weight(*use(enc_w), flipped)
    (lat,) = use(lat)
    mean, inv = stats[0:1, :], stats[1:2, :]
    step = 4

    def last(k, totals):
        value = backward_rows(back_wide, flipped, k * step, step, pitch)
        first, second = totals
        for u in range(step):
            at = u * pitch + SIDE
            normed = (lat[k * step + u].astype(F32) - mean) * inv
            act = normed * gain[...] + bias[...]
            s = jax.nn.sigmoid(act)
            some = value[at : at + width] * s * (1.0 + act * (1.0 - s))
            back_act[k * step + u] = some
            first = first + jnp.sum(some, 0, keepdims=True)
            second = second + jnp.sum(some * normed, 0, keepdims=True)
        return first, second

    zero = jnp.zeros((1, channels), F32)
    first, second = lax.fori_loop(0, height // step, last, (zero, zero))
    half = channels // 2
    lines = [first[:, :half], first[:, half:], second[:, :half], second[:, half:]]
    tail[...] = jnp.concatenate(lines + [jnp.zeros((4, half), F32)], 0)


def last_kernel(lat, back_act, plane, stats, gain, *refs):
    pieces, (out, grads) = refs[:-2], refs[-2:]
    height, width, channels = lat.shape
    mean, inv = stats[0:1, :], stats[1:2, :]
    per_group = channels // G
    count = height * width * lax.axis_size("row") * lax.axis_size("col") * per_group
    end = pieces[0].shape[1] - 24
    sums = jnp.zeros((8, pieces[0].shape[2]), F32)
    for ref in pieces:
        for z in range(ref.shape[0]):
            some = ref[z, end : end + 8, :] + ref[z, end + 8 : end + 16, :]
            sums = sums + some * jnp.exp2(-ref[z, end + 18 : end + 19, :])
    first = jnp.concatenate([sums[0:1, :], sums[1:2, :]], 1)
    second = jnp.concatenate([sums[2:3, :], sums[3:4, :]], 1)
    grads[0:1, :] = first
    grads[1:2, :] = second
    same = lax.broadcasted_iota(jnp.int32, (channels, channels), 0) // per_group
    same = same == lax.broadcasted_iota(jnp.int32, (channels, channels), 1) // per_group
    mix = jnp.where(same, 1.0, 0.0).astype(F32)
    both = jnp.concatenate([first * gain[...], second * gain[...]] + [first] * 6, 0)
    means = dot(both, mix, precision=HIGH) * (1.0 / count)

    lat, back_act, plane = use(lat, back_act, plane)

    def one(r, _):
        normed = (lat[r].astype(F32) - mean) * inv
        d = back_act[r] * gain[...]
        at = pl.multiple_of((r + 1) * (width + 2 * SIDE) + 2 * SIDE, 8)
        enc_back = plane[pl.ds(at, width), :]
        out[r] = (inv * (d - means[0:1] - normed * means[1:2]) + enc_back).astype(BF16)
        return 0

    lax.fori_loop(0, height, one, 0)


def owner_kernel(tags, wide, out):
    shard, channels = out.shape
    total = jnp.zeros((shard, 2 * channels), F32)
    rows = wide.shape[0]
    chunk = 1024
    code = lax.broadcasted_iota(jnp.int32, (shard, tags.shape[1]), 0) + 1
    lines = chunk // tags.shape[1]
    for k in range(rows // chunk):
        hit = jnp.concatenate(
            [
                (code == tags[k * lines + u : k * lines + u + 1, :]).astype(F32).astype(BF16)
                for u in range(lines)
            ],
            1,
        )
        total = total + dot(hit, wide[k * chunk : (k + 1) * chunk, :])
    out[...] = total[:, :channels] + total[:, channels:]


def exponent(biggest):
    return 14.0 - jnp.ceil(jnp.log2(jnp.maximum(biggest, 1e-30)))


def exchange(x):
    return lax.all_to_all(x, AXES, split_axis=0, concat_axis=0, tiled=True)


def pair_swap(x):
    size = lax.axis_size("row")
    return lax.ppermute(x, "row", [(i, i ^ 1) for i in range(size)])


def shifts(n, stride=1):
    size = n * stride
    return [[((i + s * stride) % size, i) for i in range(size)] for s in range(1, n)]


def columns_kernel(cols, *refs):
    ins, outs = refs[:-cols], refs[-cols:]
    col = lax.axis_index("col")
    extra = ins[0].shape[0] % 256
    taps = ins[0].shape[0] - extra
    lines = taps // cols
    for s, out in enumerate(outs):
        at = pl.ds(pl.multiple_of((col + cols - s) % cols * lines, 8), lines)
        out[:lines, :] = ins[0][at, :] + ins[1][at, :]
        if extra:
            out[lines:, :] = ins[0][taps:, :] + ins[1][taps:, :]


def rows_kernel(cols, *refs):
    parts, outs = (refs[:cols], refs[cols : 2 * cols]), refs[2 * cols :]
    row, _, rows, _ = place_of()
    depth = rows // 2
    lines = outs[0].shape[0] // 2 - 4

    def added(some, first, count):
        value = some[0][first : first + count, :]
        for ref in some[1:]:
            value = value + ref[first : first + count, :]
        return value

    tail = added(parts[0], depth * lines, 8)
    for z in range(depth):
        values = [added(some, z * lines, lines) for some in parts]
        for s, out in enumerate(outs):

            @pl.when((row // 2 + depth - s) % depth == z)
            def _():
                for i in range(2):
                    out[i * lines : (i + 1) * lines, :] = values[i]

    for out in outs:
        out[2 * lines :, :] = tail


def chunk_kernel(depth, *refs):
    parts, (tail, tail_b, out, powers) = refs[:depth], refs[depth:]
    half = out.shape[1]
    lines = parts[0].shape[0] // 2 - 4
    value = parts[0][...]
    for ref in parts[1:]:
        value = value + ref[...]
    powers[...] = value[2 * lines :]
    values = [value[:lines], value[lines : 2 * lines], tail[...] + tail_b[...]]
    end = 2 * lines + 16
    out[end:, :] = jnp.zeros((8, half), F32)
    for i, some in enumerate(values):
        top = jnp.max(jnp.max(jnp.abs(some), 0, keepdims=True), 1, keepdims=True)
        power = exponent(top)
        some = some * jnp.exp2(power)
        if i < 2:
            out[i * lines : (i + 1) * lines, :] = some
        else:
            high = some.astype(BF16).astype(F32)
            out[end - 16 : end - 8, :] = high
            out[end - 8 : end, :] = some - high
        out[end + i : end + i + 1, :] = jnp.broadcast_to(power, (1, half))


def column_parts(arrays):
    cols = lax.axis_size("col")
    taps, half = arrays[0].shape
    extra = taps % 256
    parts = call(
        lambda *refs: columns_kernel(cols, *refs),
        arrays,
        [shaped(((taps - extra) // cols + extra, half))] * cols,
        moved=4 * 10**6,
    )
    return list(parts)


def column_send(parts):
    cols = lax.axis_size("col")
    return [parts[0]] + [lax.ppermute(x, "col", p) for x, p in zip(parts[1:], shifts(cols))]


def row_sums(enc, dec, tail):
    cols, depth = len(enc), lax.axis_size("row") // 2
    taps, half = dec[0].shape
    lines = taps // depth
    parts = call(
        lambda *refs: rows_kernel(cols, *refs),
        enc + dec,
        [shaped((2 * lines + 8, half))] * depth,
        moved=4 * 10**6,
    )
    parts = [parts[0]] + [lax.ppermute(x, "row", p) for x, p in zip(parts[1:], shifts(depth, 2))]
    return call(
        lambda *refs: chunk_kernel(depth, *refs),
        parts + [tail, pair_swap(tail)],
        (shaped((2 * lines + 24, half)), shaped((8, half))),
        moved=10**6,
    )


def gather_rows(chunk):
    own = chunk.astype(F16)
    steps = shifts(lax.axis_size("row") // 2, 2)
    return jnp.stack([own] + [lax.ppermute(own, "row", p) for p in steps])


def gather_columns(own):
    return [own] + [lax.ppermute(own, "col", p) for p in shifts(lax.axis_size("col"))]


def gather_cores(own, other):
    rows, cols = lax.axis_size("row"), lax.axis_size("col")
    lines, half = own[0].shape[1] // 2 - 12, own[0].shape[2]
    chunks = cols * rows // 2
    return call(
        lambda *refs: assemble_kernel(lines, *refs),
        own + other,
        (shaped((chunks, lines, 2 * half)), shaped((chunks, lines, 2 * half))),
        moved=10**7,
    )


def assemble_kernel(lines, *refs):
    pieces, outs = refs[:-2], refs[-2:]
    row, col, rows, cols = place_of()
    depth = rows // 2
    half = outs[0].shape[2] // 2
    for k, ref in enumerate(pieces):
        core = (row + k // cols) % 2
        c = (col + k % cols) % cols
        lanes = pl.ds(pl.multiple_of(core * half, half), half)
        for s in range(depth):
            z = (row // 2 + s) % depth
            for i, out in enumerate(outs):
                at = 2 * lines + 16 + i
                scale = jnp.exp2(-ref[s, at : at + 1, :])
                value = ref[s, i * lines : (i + 1) * lines, :] * scale
                out[c * depth + z, :, lanes] = value


def halo(fields):
    rows, cols = lax.axis_size("row"), lax.axis_size("col")
    forth = lambda n: [(i, i + 1) for i in range(n - 1)]
    back = lambda n: [(i + 1, i) for i in range(n - 1)]
    left_edge = jnp.stack([x[:, :HALO] for x in fields])
    right_edge = jnp.stack([x[:, -HALO:] for x in fields])
    left = lax.ppermute(right_edge, "col", forth(cols))
    right = lax.ppermute(left_edge, "col", back(cols))

    def lines(at):
        return jnp.concatenate([left[:, at], jnp.stack([x[at] for x in fields]), right[:, at]], 2)

    up = lax.ppermute(lines(slice(-HALO, None)), "row", forth(rows))
    down = lax.ppermute(lines(slice(0, HALO)), "row", back(rows))
    return left, right, up, down


def body(
    latents,
    code_ids,
    norm_gain,
    norm_bias,
    encoder_weight,
    codebook,
    decoder_weight,
    decoded_cotangent,
):
    height, width, channels = latents.shape
    devices = lax.axis_size("row") * lax.axis_size("col")
    codes_total = codebook.shape[0]
    shard = codes_total // devices
    count = height * width
    cap = 2 * count // devices
    pitch = width + 2 * SIDE
    conv_flops = 2 * count * 9 * channels * channels
    taps = 9 * channels
    half = channels // 2
    plane = (height + 2) * pitch
    plane_rows = plane + 2 * SIDE
    big = (height + 4) * pitch
    after = lambda *x: lax.optimization_barrier(x)
    halos = lambda field, start: [(start + i, field) for i in range(4)]

    payload, slots = call(
        lambda *refs: front_kernel(devices, shard, cap, *refs),
        (latents, code_ids),
        (shaped((devices, 8, width)), shaped((height, width), jnp.int32)),
        flops=10**9,
        moved=10**6,
        late=[(0, None)],
    )
    payload, code_ids, latents, decoded_cotangent = after(
        payload, code_ids, latents, decoded_cotangent
    )
    gathered = exchange(payload)
    quantized = codebook[code_ids]
    left, right, up, down = halo((latents, decoded_cotangent, quantized))
    gain = norm_gain.reshape(1, channels)
    bias = norm_bias.reshape(1, channels)

    dec_grad = call(
        decoder_grad_kernel,
        (decoded_cotangent, quantized, left, right, up, down),
        (shaped((taps, half)), shaped((taps, half))),
        [
            pltpu.VMEM((plane_rows, channels), F32),
            pltpu.VMEM((plane, 3 * channels), BF16),
            pltpu.VMEM((channels, height * pitch), BF16),
        ],
        flops=conv_flops,
        moved=5 * 10**6,
        late=[(0, None), *halos(1, 2), (1, None)],
    )
    dec_keep, dec_give = dec_grad
    gathered, dec_keep, dec_give = after(gathered, dec_keep, dec_give)
    dec_parts = column_parts((dec_keep, pair_swap(dec_give)))
    gathered, *dec_parts = after(gathered, *dec_parts)
    dec_parts = column_send(dec_parts)
    enc_fwd = encoder_weight.reshape(3, 3 * channels, channels)
    dec_fwd = decoder_weight.reshape(3, 3 * channels, channels)
    code_scale = codes_total / (count * devices)
    z, pull, turned, stats, power = call(
        lambda *refs: encoder_kernel(code_scale, *refs),
        (latents, left, right, up, down, quantized, gathered, gain, bias, enc_fwd),
        (
            shaped((plane_rows, channels)),
            shaped((count, channels)),
            shaped((channels, height * pitch), BF16),
            shaped((8, channels)),
            shaped((8, channels)),
        ),
        [
            pltpu.VMEM((big + 2 * SIDE, channels), F32),
            pltpu.VMEM((big, 3 * channels), BF16),
            pltpu.VMEM((plane_rows, channels), F32),
            pltpu.VMEM((channels, height * pitch), BF16),
            pltpu.VMEM((height * pitch, channels), F32),
            pltpu.SemaphoreType.DMA(((height + 2) // 3 + 1,)),
        ],
        far=(0, 2),
        flops=conv_flops,
        moved=10 * 10**6,
        room=20,
        late=[(0, None), *halos(0, 1), (9, None), (5, None)],
    )
    packed = call(
        pack_kernel,
        (slots.reshape(-1), pull, power),
        shaped((devices * cap, channels)),
        specs=[SMEM, VMEM, VMEM],
        flops=5 * 10**9,
        moved=6 * 10**6,
    )
    send = packed.astype(F16).reshape(devices, cap, channels)
    send, z, *dec_parts = after(send, z, *dec_parts)
    received = exchange(send)

    back_plane, keep_grad, give_grad = call(
        rotate_kernel,
        (
            decoded_cotangent, left, right, up, down, quantized, left, right, up, down, z, turned,
            decoder_weight, power,
        ),
        (
            shaped((plane_rows, channels)),
            shaped((taps + 8, half)),
            shaped((taps + 8, half)),
        ),
        [
            pltpu.VMEM((big + 2 * SIDE, channels), F32),
            pltpu.VMEM((plane_rows, channels), F32),
            pltpu.VMEM((big, 3 * channels), BF16),
            pltpu.VMEM((plane, 3 * channels), BF16),
            pltpu.VMEM((3, channels, 3 * channels), BF16),
            pltpu.VMEM((plane_rows, channels), F32),
            pltpu.SemaphoreType.DMA,
        ],
        far=(0,),
        flops=2 * conv_flops,
        moved=15 * 10**6,
        room=32,
        late=[
            (0, None), *halos(1, 1), (5, None), *halos(2, 6), (12, None), (10, None), (11, None)
        ],
    )
    enc_parts = column_send(column_parts((keep_grad, pair_swap(give_grad))))
    back_act, tail = call(
        back_kernel,
        (latents, back_plane, stats, gain, bias, encoder_weight),
        (shaped((height, width, channels)), shaped((8, half))),
        [
            pltpu.VMEM((plane, 3 * channels), BF16),
            pltpu.VMEM((3, channels, 3 * channels), BF16),
        ],
        flops=conv_flops,
        moved=8 * 10**6,
        late=[(1, None), (5, None), (0, None)],
    )
    decoded = call(
        decoder_kernel,
        (quantized, left, right, up, down, dec_fwd),
        shaped((height, width, channels), BF16),
        [
            pltpu.VMEM((plane_rows, channels), F32),
            pltpu.VMEM((plane, 3 * channels), BF16),
        ],
        flops=conv_flops,
        moved=4 * 10**6,
        late=[(0, None), *halos(2, 1), (5, None)],
    )
    decoded, *enc_parts = after(decoded, *enc_parts)
    chunk, powers = row_sums(enc_parts, dec_parts, tail)
    own = gather_rows(chunk)
    pieces = gather_columns(own)

    rows_f = received.astype(F32) * jnp.exp2(-jnp.round(powers[0, :devices]))[:, None, None]
    rows_f = rows_f.reshape(devices * cap, channels)
    high = lax.reduce_precision(rows_f, 8, 7)
    low = rows_f - high
    wide = jnp.concatenate([high.astype(BF16), low.astype(BF16)], 1)
    tags = gathered[:, 4, :cap].astype(jnp.int32).reshape(-1, 128)
    codebook_grad = call(
        owner_kernel,
        (tags, wide),
        shaped((shard, channels)),
        flops=2 * 10**9,
        moved=6 * 10**6,
    )
    codebook_grad, *pieces = after(codebook_grad, *pieces)
    other = [pair_swap(x) for x in pieces]
    own = [x.astype(F32) for x in pieces]
    latents_grad, norm_grads = call(
        last_kernel,
        (latents, back_act, back_plane, stats, gain, *own),
        (shaped((height, width, channels), BF16), shaped((2, channels))),
        flops=10**8,
        moved=6 * 10**6,
    )
    other = [x.astype(F32) for x in other]
    encoder_weight_grad, decoder_weight_grad = [
        x.reshape(3, 3, channels, channels) for x in gather_cores(own, other)
    ]
    return (
        decoded,
        latents_grad,
        norm_grads[1],
        norm_grads[0],
        encoder_weight_grad,
        decoder_weight_grad,
        codebook_grad,
    )


def solution(mesh):
    return jax.shard_map(
        body,
        mesh=mesh,
        in_specs=(
            P("row", "col", None),
            P("row", "col"),
            P(),
            P(),
            P(),
            P(),
            P(),
            P("row", "col", None),
        ),
        out_specs=(
            P("row", "col", None),
            P("row", "col", None),
            P(),
            P(),
            P(),
            P(),
            P(("row", "col"), None),
        ),
        check_vma=False,
    )
```

```python
import jax
import jax.numpy as jnp
from jax import lax
from jax.experimental import pallas as pl
from jax.experimental.pallas import tpu as pltpu
from jax.sharding import PartitionSpec as P

G = 32
epsilon = 1e-06
commit_beta = 0.25
F32 = jnp.float32
BF16 = jnp.bfloat16
F16 = jnp.float16
AXES = ("row", "col")
SIDE = 8
HALO = 2
VMEM = pl.BlockSpec(memory_space=pltpu.VMEM)
SMEM = pl.BlockSpec(memory_space=pltpu.SMEM)
ANY = pl.BlockSpec(memory_space=pltpu.HBM)
NT = (((1,), (1,)), ((), ()))
NN = (((1,), (0,)), ((), ()))
HIGH = lax.Precision.HIGHEST


class Late:
    def __init__(self, ref, copy):
        self.ref, self.copy = ref, copy
        copy.start()

    def get(self):
        if self.copy is not None:
            self.copy.wait()
            self.copy = None
        return self.ref


def call(kernel, ins, outs, scratch=(), specs=None, flops=0, moved=0, room=16, late=(), far=()):
    room = 56 if late else room
    specs = list(specs or [VMEM] * len(ins))
    first = len(ins) + len(jax.tree.leaves(outs)) + len(scratch)
    scratch = list(scratch)
    for i, field in late:
        specs[i] = ANY
        shape = ins[i].shape if field is None else ins[i].shape[1:]
        scratch.append(pltpu.VMEM(shape, ins[i].dtype))
    if late:
        scratch.append(pltpu.SemaphoreType.DMA((len(late),)))

    def wrapped(*refs):
        given = list(refs[:first])
        loads = []
        for j, (i, field) in enumerate(late):
            source = refs[i] if field is None else refs[i].at[field]
            copy = pltpu.make_async_copy(source, refs[first + j], refs[-1].at[j])
            given[i] = Late(refs[first + j], copy)
            loads.append(given[i])
        kernel(*given)
        for load in loads:
            load.get()

    return pl.pallas_call(
        wrapped,
        in_specs=specs,
        out_specs=jax.tree.unflatten(
            jax.tree.structure(outs),
            [ANY if i in far else VMEM for i in range(len(jax.tree.leaves(outs)))],
        ),
        out_shape=outs,
        scratch_shapes=scratch,
        compiler_params=pltpu.CompilerParams(vmem_limit_bytes=room * 2**20),
        cost_estimate=pl.CostEstimate(flops=flops, bytes_accessed=moved, transcendentals=0),
    )(*ins)


def use(*refs):
    return [ref.get() if isinstance(ref, Late) else ref for ref in refs]


def shaped(shape, dtype=F32):
    return jax.ShapeDtypeStruct(shape, dtype)


def dot(a, b, dims=NN, precision=None):
    return lax.dot_general(a, b, dims, precision=precision, preferred_element_type=F32)


def front_kernel(devices, shard, cap, lat, ids, payload, slots):
    height, width = ids.shape
    count = height * width

    owner = lax.broadcasted_iota(jnp.int32, (devices, width), 0)
    upper = (
        lax.broadcasted_iota(jnp.int32, (width, width), 0)
        < lax.broadcasted_iota(jnp.int32, (width, width), 1)
    ).astype(BF16)
    slot_row = lax.broadcasted_iota(jnp.int32, (width, width), 0)
    members, codes, dests = [], [], []
    for r in range(height):
        code = ids[r : r + 1, :]
        dest = code // shard
        codes.append(code - dest * shard)
        dests.append(dest)
        members.append((owner == dest).astype(F32))
    stacked = jnp.concatenate([x.astype(BF16) for x in members], 0)
    before = dot(stacked, upper)
    base = jnp.zeros((devices, 1), F32)
    hits, parts = [], []
    for r in range(height):
        member = members[r]
        count_before = before[r * devices : (r + 1) * devices] + base
        rank = jnp.sum(member * count_before, 0, keepdims=True).astype(jnp.int32)
        slots[r : r + 1, :] = dests[r] * cap + rank
        hits.append((slot_row == rank).astype(BF16))
        tagged = codes[r] + 1
        high = tagged // 32
        low = tagged - high * 32
        both = [member * high.astype(F32), member * low.astype(F32)]
        parts.append(jnp.concatenate(both, 0).astype(BF16))
        base = base + jnp.sum(member, 1, keepdims=True)
    placed = dot(jnp.concatenate(parts, 1), jnp.concatenate(hits, 1), NT)
    placed = 32.0 * placed[:devices] + placed[devices:]
    (lat,) = use(lat)
    channels = lat.shape[2]

    def add_row(r, total):
        return total + jnp.sum(lat[r].astype(F32), 0, keepdims=True)

    mean = lax.fori_loop(0, height, add_row, jnp.zeros((1, channels), F32)) * (1.0 / count)

    def add_square(r, total):
        gap = lat[r].astype(F32) - mean
        return total + jnp.sum(gap * gap, 0, keepdims=True)

    square = lax.fori_loop(0, height, add_square, jnp.zeros((1, channels), F32))
    half = width
    rows = [mean[:, :half], mean[:, half:], square[:, :half], square[:, half:]]
    for i, part in enumerate(rows):
        payload[:, i, :] = jnp.broadcast_to(part, (devices, half))
    payload[:, 4, :] = placed
    payload[:, 5:, :] = jnp.zeros((devices, 3, half), F32)


def place_of():
    return (
        lax.axis_index("row"),
        lax.axis_index("col"),
        lax.axis_size("row"),
        lax.axis_size("col"),
    )


def place_of():
    return (
        lax.axis_index("row"),
        lax.axis_index("col"),
        lax.axis_size("row"),
        lax.axis_size("col"),
    )


def fill_tile(scr, own, left, right, up, down, ring):
    height, width, channels = own.shape
    pitch = width + 2 * SIDE
    for r in range(height):
        base = SIDE + (ring + r) * pitch
        scr[base + SIDE - HALO : base + SIDE] = left[r].astype(F32)
        scr[base + SIDE : base + SIDE + width] = own[r].astype(F32)
        scr[base + SIDE + width : base + SIDE + width + HALO] = right[r].astype(F32)
    span = up.shape[1]
    for i in range(ring):
        top = SIDE + i * pitch + SIDE - HALO
        scr[top : top + span] = up[HALO - ring + i].astype(F32)
        low = SIDE + (ring + height + i) * pitch + SIDE - HALO
        scr[low : low + span] = down[i].astype(F32)
    blank = jnp.zeros((SIDE - HALO, channels), F32)
    for r in range(height + 2 * ring):
        base = SIDE + r * pitch
        scr[base : base + SIDE - HALO] = blank
        scr[base + pitch - SIDE + HALO : base + pitch] = blank
    ends(scr, channels)


def ends(scr, channels):
    blank = jnp.zeros((SIDE, channels), F32)
    scr[0:SIDE] = blank
    scr[scr.shape[0] - SIDE :] = blank


def spread(scr, wide, count, pitch, channels):
    def one(r, _):
        value = scr[pl.ds(pl.multiple_of(r * pitch, 8), pitch + 2 * SIDE), :]
        at = pl.ds(pl.multiple_of(r * pitch, 16), pitch)
        for j in range(3):
            start = SIDE + j - 1
            wide[at, j * channels : (j + 1) * channels] = value[start : start + pitch].astype(BF16)
        return 0

    lax.fori_loop(0, count, one, 0)


def rows_at(r, pitch, count):
    if isinstance(r, int):
        return slice(r * pitch, (r + count) * pitch)
    return pl.ds(pl.multiple_of(r * pitch, 16), count * pitch)


def forward_rows(wide, weight, r, step, pitch):
    total = dot(wide[rows_at(r, pitch, step), :], weight[0])
    for dy in (1, 2):
        total = total + dot(wide[rows_at(r + dy, pitch, step), :], weight[dy])
    return total


def backward_rows(wide, weight, r, step, pitch):
    total = dot(wide[rows_at(r + 2, pitch, step), :], weight[0], NT)
    for dy in (1, 2):
        total = total + dot(wide[rows_at(r + 2 - dy, pitch, step), :], weight[dy], NT)
    return total


def kernel_grad(turned, wide, keep, give, pitch, height, first_row):
    channels = turned.shape[0]
    half = channels // 2
    count = height * pitch
    core = lax.axis_index("row") % 2
    for dy in range(3):
        start = (first_row + 1 - dy) * pitch
        product = dot(turned[...], wide[start : start + count, :])
        for j in range(3):
            at = (dy * 3 + 2 - j) * channels
            low = product[:, j * channels : j * channels + half]
            high = product[:, j * channels + half : (j + 1) * channels]

            keep[at : at + channels, :] = jnp.where(core == 0, low, high)
            give[at : at + channels, :] = jnp.where(core == 0, high, low)


def turn_own(own, turned):
    height, width, channels = own.shape
    pitch = width + 2 * SIDE
    blank = jnp.zeros((SIDE, channels), F32)
    for r in range(0, height, 8):
        parts = []
        for k in range(8):
            parts += [blank, own[r + k].astype(F32), blank]
        block = jnp.concatenate(parts, 0)
        turned[:, r * pitch : (r + 8) * pitch] = block.T.astype(BF16)


def decoder_grad_kernel(
    cot, codes, left, right, up, down, keep, give, scr, wide, turned
):
    cot, left, right, up, down = use(cot, left, right, up, down)
    height, width, channels = cot.shape
    pitch = width + 2 * SIDE
    fill_tile(scr, cot, left, right, up, down, 1)
    spread(scr, wide, height + 2, pitch, channels)
    turn_own(*use(codes), turned)
    kernel_grad(turned, wide, keep, give, pitch, height, 1)


def decoder_kernel(codes, left, right, up, down, weight, out, scr, wide):
    codes, left, right, up, down = use(codes, left, right, up, down)
    height, width, channels = codes.shape
    pitch = width + 2 * SIDE
    fill_tile(scr, codes, left, right, up, down, 1)
    spread(scr, wide, height + 2, pitch, channels)
    step = 4
    (weight,) = use(weight)

    def part(k, _):
        value = forward_rows(wide, weight, k * step, step, pitch)
        for u in range(step):
            at = u * pitch + SIDE
            out[k * step + u] = value[at : at + width].astype(BF16)
        return 0

    lax.fori_loop(0, height // step, part, 0)


def group_stats(gathered, height, width):
    devices = gathered.shape[0]
    rows, cols = lax.axis_size("row"), lax.axis_size("col")
    local = jnp.concatenate([gathered[:, 0, :], gathered[:, 1, :]], 1)
    square = jnp.concatenate([gathered[:, 2, :], gathered[:, 3, :]], 1)
    channels = local.shape[1]
    per_group = channels // G
    same = lax.broadcasted_iota(jnp.int32, (channels, channels), 0) // per_group
    same = same == lax.broadcasted_iota(jnp.int32, (channels, channels), 1) // per_group
    mix = jnp.where(same, 1.0 / per_group, 0.0).astype(F32)
    centre = jnp.broadcast_to(jnp.sum(local, 0, keepdims=True) * (1.0 / devices), (8, channels))
    mean = dot(centre, mix, precision=HIGH)[0:1]
    gap = local - mean
    spread_sum = square + (height * width) * (gap * gap)
    total = jnp.sum(spread_sum, 0, keepdims=True) * (1.0 / (devices * height * width))
    var = dot(jnp.broadcast_to(total, (8, channels)), mix, precision=HIGH)[0:1]
    return mean, lax.rsqrt(var + epsilon)


def inside_tile(row, col, rows, cols, height, width):
    pitch = width + 2 * SIDE
    place = lax.broadcasted_iota(jnp.int32, (pitch + 2 * SIDE, 1), 0) - 2 * SIDE + col * width
    inside_col = (place >= 0) & (place < cols * width)

    def keep(line):
        high = row * height + line
        return inside_col & (high >= 0) & (high < rows * height)

    return keep


def encoder_kernel(
    code_scale,
    lat, left, right, up, down, codes, gathered, gain, bias, weight,
    z_far, pull, turned_far, stats, power,
    tmp_s, wide, z_out, turned, own_s, sems,
):
    height, width, channels = codes.ref.shape
    pitch = width + 2 * SIDE
    keep = inside_tile(*place_of(), height, width)
    mean, inv = group_stats(gathered, height, width)
    stats[0:1, :] = mean
    stats[1:2, :] = inv
    fill_tile(tmp_s, *use(lat, left, right, up, down), 2)
    scale = inv * gain[...]
    offset = bias[...]

    blank = jnp.zeros((SIDE, channels), F32)

    def smooth_row(r):
        act = (tmp_s[r * pitch : (r + 1) * pitch + 2 * SIDE, :] - mean) * scale + offset
        value = jnp.where(keep(r - 2), act * jax.nn.sigmoid(act), 0.0)
        at = slice(r * pitch, (r + 1) * pitch)
        for j in range(3):
            start = SIDE + j - 1
            wide[at, j * channels : (j + 1) * channels] = value[start : start + pitch].astype(BF16)
        if 2 <= r < height + 2:
            base = (r - 2) * pitch
            own_s[base : base + SIDE, :] = blank
            own_s[base + SIDE : base + SIDE + width, :] = value[2 * SIDE : 2 * SIDE + width]
            own_s[base + SIDE + width : base + pitch, :] = blank

    step = 3
    steps = (height + 2) // step
    ends(z_out, channels)
    weight, codes = use(weight, codes)

    def z_copy(k):
        at = slice(SIDE + k * step * pitch, SIDE + (k + 1) * step * pitch)
        return pltpu.make_async_copy(z_out.at[at, :], z_far.at[at, :], sems.at[k])

    def part(k):
        first = SIDE + k * step * pitch
        count = step * pitch
        z = tmp_s[first + pitch : first + pitch + count, :]
        z = z + forward_rows(wide, weight, k * step, step, pitch)
        z_out[first : first + count, :] = z
        z_copy(k).start()
        tops = []
        for u in range(step):
            line = k * step + u - 1
            if 0 <= line < height:
                at = u * pitch + SIDE
                some = (codes[line].astype(F32) - z[at : at + width]) * code_scale
                pull[line * width : (line + 1) * width, :] = some
                tops.append(jnp.max(jnp.abs(some), 0, keepdims=True))
        return tops

    for r in range(step + 2):
        smooth_row(r)
    tops = []
    for k in range(steps):
        for r in range((k + 1) * step + 2, min((k + 2) * step + 2, height + 4)):
            smooth_row(r)
        tops += part(k)
    for r in range(0, height, 8):
        at = slice(r * pitch, (r + 8) * pitch)
        turned[:, at] = own_s[at, :].T.astype(BF16)
    turned_copy = pltpu.make_async_copy(turned, turned_far, sems.at[steps])
    turned_copy.start()
    top = jnp.max(jnp.concatenate(tops, 0), 0, keepdims=True)
    top = jnp.max(top, 1, keepdims=True)
    power[...] = jnp.broadcast_to(exponent(top), power.shape)
    for k in range(steps):
        z_copy(k).wait()
    turned_copy.wait()


def pack_kernel(slots, pull, power, packed):
    packed[...] = jnp.zeros(packed.shape, F32)
    scale = jnp.exp2(power[0:1, :])

    def some(i, _):
        value = pull[pl.ds(pl.multiple_of(i * 16, 8), 16), :] * scale
        for u in range(16):
            packed[pl.ds(slots[i * 16 + u], 1), :] = value[u : u + 1, :]
        return 0

    lax.fori_loop(0, pull.shape[0] // 16, some, 0)


def flip_weight(weight, flipped):
    channels = weight.shape[2]
    for dy in range(3):
        for j in range(3):
            flipped[dy, :, j * channels : (j + 1) * channels] = weight[dy, 2 - j]


def rotate_kernel(
    cot, left, right, up, down, codes, code_l, code_r, code_u, code_d, z_in, turned, dec_w, power,
    plane_far, keep_grad, give_grad,
    tmp_s, code_s, wide, back_wide, flipped, plane, sem,
):
    height, width, channels = cot.ref.shape
    pitch = width + 2 * SIDE
    fill_tile(tmp_s, *use(cot, left, right, up, down), 2)
    spread(tmp_s, wide, height + 4, pitch, channels)
    fill_tile(code_s, *use(codes, code_l, code_r, code_u, code_d), 1)
    flip_weight(*use(dec_w), flipped)
    ends(plane, channels)
    step = 3
    chunks = (height + 2) // step

    def part(k):
        at = slice(SIDE + k * step * pitch, SIDE + (k + 1) * step * pitch)
        plane[at, :] = backward_rows(wide, flipped, k * step, step, pitch)

    block = 24
    z_in, turned = use(z_in, turned)
    place = lax.broadcasted_iota(jnp.int32, (block, 1), 0)
    row, col, rows, cols = place_of()

    def total(x):
        return jnp.sum(x, 1, keepdims=True)

    def turn(line):
        spots = [
            slice(SIDE + line * pitch + b, SIDE + line * pitch + b + block)
            for b in range(0, pitch, block)
        ]
        sums = []
        for at in spots:
            z, e = z_in[at, :], code_s[at, :]
            sums.append((total(z * z) + epsilon, total(e * e) + epsilon))
        scales = []
        for at, (zz, ee) in zip(spots, sums):
            z, e, back = z_in[at, :], code_s[at, :], plane[at, :]
            z_inv, e_inv = lax.rsqrt(zz), lax.rsqrt(ee)
            e_unit = e * e_inv
            mirror = z * z_inv + e_unit
            scales.append(
                (z_inv, e_inv, ee, total(mirror * mirror) + epsilon, total(mirror * back),
                 total(e_unit * back))
            )
        high = row * height + line - 1
        keep = (high >= 0) & (high < rows * height)
        for b, (at, (z_inv, e_inv, ee, mm, along, code)) in enumerate(zip(spots, scales)):
            z, e, back = z_in[at, :], code_s[at, :], plane[at, :]
            stretch = ee * e_inv * z_inv
            along = 2.0 * along / mm
            z_part = stretch * z_inv * (2.0 * code - along) + commit_beta
            e_part = stretch * e_inv * along + commit_beta
            across = place + b * block - SIDE + col * width
            inside = keep & (across >= 0) & (across < cols * width)
            plane[at, :] = jnp.where(inside, stretch * back + z_part * z - e_part * e, 0.0)

    part(0)
    for k in range(chunks):
        if k + 1 < chunks:
            part(k + 1)
        for u in range(step):
            turn(k * step + u)
    plane_copy = pltpu.make_async_copy(plane, plane_far, sem)
    plane_copy.start()
    spread(plane, back_wide, height + 2, pitch, channels)
    kernel_grad(turned, back_wide, keep_grad, give_grad, pitch, height, 1)
    taps, half = keep_grad.shape[0] - 8, keep_grad.shape[1]
    lane = lax.broadcasted_iota(jnp.int32, (8, half), 1)
    mine = jnp.where(lane == row * cols + col, power[:, :half], 0.0)
    keep_grad[taps:, :] = mine
    give_grad[taps:, :] = mine
    plane_copy.wait()


def back_kernel(lat, plane, stats, gain, bias, enc_w, back_act, tail, back_wide, flipped):
    (plane,) = use(plane)
    height, width, channels = lat.ref.shape
    pitch = width + 2 * SIDE
    spread(plane, back_wide, height + 2, pitch, channels)
    flip_weight(*use(enc_w), flipped)
    (lat,) = use(lat)
    mean, inv = stats[0:1, :], stats[1:2, :]
    step = 4

    def last(k, totals):
        value = backward_rows(back_wide, flipped, k * step, step, pitch)
        first, second = totals
        for u in range(step):
            at = u * pitch + SIDE
            normed = (lat[k * step + u].astype(F32) - mean) * inv
            act = normed * gain[...] + bias[...]
            s = jax.nn.sigmoid(act)
            some = value[at : at + width] * s * (1.0 + act * (1.0 - s))
            back_act[k * step + u] = some
            first = first + jnp.sum(some, 0, keepdims=True)
            second = second + jnp.sum(some * normed, 0, keepdims=True)
        return first, second

    zero = jnp.zeros((1, channels), F32)
    first, second = lax.fori_loop(0, height // step, last, (zero, zero))
    half = channels // 2
    lines = [first[:, :half], first[:, half:], second[:, :half], second[:, half:]]
    tail[...] = jnp.concatenate(lines + [jnp.zeros((4, half), F32)], 0)


def last_kernel(lat, back_act, plane, stats, gain, *refs):
    pieces, (out, grads) = refs[:-2], refs[-2:]
    height, width, channels = lat.shape
    mean, inv = stats[0:1, :], stats[1:2, :]
    per_group = channels // G
    count = height * width * lax.axis_size("row") * lax.axis_size("col") * per_group
    end = pieces[0].shape[1] - 24
    sums = jnp.zeros((8, pieces[0].shape[2]), F32)
    for ref in pieces:
        for z in range(ref.shape[0]):
            some = ref[z, end : end + 8, :] + ref[z, end + 8 : end + 16, :]
            sums = sums + some * jnp.exp2(-ref[z, end + 18 : end + 19, :])
    first = jnp.concatenate([sums[0:1, :], sums[1:2, :]], 1)
    second = jnp.concatenate([sums[2:3, :], sums[3:4, :]], 1)
    grads[0:1, :] = first
    grads[1:2, :] = second
    same = lax.broadcasted_iota(jnp.int32, (channels, channels), 0) // per_group
    same = same == lax.broadcasted_iota(jnp.int32, (channels, channels), 1) // per_group
    mix = jnp.where(same, 1.0, 0.0).astype(F32)
    both = jnp.concatenate([first * gain[...], second * gain[...]] + [first] * 6, 0)
    means = dot(both, mix, precision=HIGH) * (1.0 / count)

    lat, back_act, plane = use(lat, back_act, plane)

    def one(r, _):
        normed = (lat[r].astype(F32) - mean) * inv
        d = back_act[r] * gain[...]
        at = pl.multiple_of((r + 1) * (width + 2 * SIDE) + 2 * SIDE, 8)
        enc_back = plane[pl.ds(at, width), :]
        out[r] = (inv * (d - means[0:1] - normed * means[1:2]) + enc_back).astype(BF16)
        return 0

    lax.fori_loop(0, height, one, 0)


def owner_kernel(tags, wide, out):
    shard, channels = out.shape
    total = jnp.zeros((shard, 2 * channels), F32)
    rows = wide.shape[0]
    chunk = 1024
    code = lax.broadcasted_iota(jnp.int32, (shard, tags.shape[1]), 0) + 1
    lines = chunk // tags.shape[1]
    for k in range(rows // chunk):
        hit = jnp.concatenate(
            [
                (code == tags[k * lines + u : k * lines + u + 1, :]).astype(F32).astype(BF16)
                for u in range(lines)
            ],
            1,
        )
        total = total + dot(hit, wide[k * chunk : (k + 1) * chunk, :])
    out[...] = total[:, :channels] + total[:, channels:]


def exponent(biggest):
    return 14.0 - jnp.ceil(jnp.log2(jnp.maximum(biggest, 1e-30)))


def exchange(x):
    return lax.all_to_all(x, AXES, split_axis=0, concat_axis=0, tiled=True)


def pair_swap(x):
    size = lax.axis_size("row")
    return lax.ppermute(x, "row", [(i, i ^ 1) for i in range(size)])


def shifts(n, stride=1):
    size = n * stride
    return [[((i + s * stride) % size, i) for i in range(size)] for s in range(1, n)]


def columns_kernel(cols, *refs):
    ins, outs = refs[:-cols], refs[-cols:]
    col = lax.axis_index("col")
    extra = ins[0].shape[0] % 256
    taps = ins[0].shape[0] - extra
    lines = taps // cols
    for s, out in enumerate(outs):
        at = pl.ds(pl.multiple_of((col + cols - s) % cols * lines, 8), lines)
        out[:lines, :] = ins[0][at, :] + ins[1][at, :]
        if extra:
            out[lines:, :] = ins[0][taps:, :] + ins[1][taps:, :]


def rows_kernel(cols, *refs):
    parts, outs = (refs[:cols], refs[cols : 2 * cols]), refs[2 * cols :]
    row, _, rows, _ = place_of()
    depth = rows // 2
    lines = outs[0].shape[0] // 2 - 4

    def added(some, first, count):
        value = some[0][first : first + count, :]
        for ref in some[1:]:
            value = value + ref[first : first + count, :]
        return value

    tail = added(parts[0], depth * lines, 8)
    tops = [jnp.zeros((1, tail.shape[1]), F32)] * 2
    for z in range(depth):
        values = [added(some, z * lines, lines) for some in parts]
        tops = [
            jnp.maximum(top, jnp.max(jnp.abs(some), 0, keepdims=True))
            for top, some in zip(tops, values)
        ]
        for s, out in enumerate(outs):

            @pl.when((row // 2 + depth - s) % depth == z)
            def _():
                for i in range(2):
                    out[i * lines : (i + 1) * lines, :] = values[i]

    end = 2 * lines
    powers = [exponent(jnp.max(top, 1, keepdims=True)) for top in tops]
    outs[0][end:, :] = tail
    for out in outs[1:]:
        out[end : end + 8, :] = tail
        out[end + 8 :, :] = jnp.zeros((8, tail.shape[1]), F32)
        for i, power in enumerate(powers):
            at = slice(i * lines, (i + 1) * lines)
            out[at, :] = out[at, :] * jnp.exp2(power)
            out[end + 8 + i : end + 9 + i, :] = jnp.broadcast_to(power, (1, tail.shape[1]))


def chunk_kernel(depth, *refs):
    parts, (tail, tail_b, out, powers) = refs[:depth], refs[depth:]
    half = out.shape[1]
    lines = parts[0].shape[0] // 2 - 4
    end = 2 * lines
    total = parts[0][end:, :]
    values = [parts[0][i * lines : (i + 1) * lines, :] for i in range(2)]
    for ref in parts[1:]:
        total = total + ref[end : end + 8, :]
        for i in range(2):
            scale = jnp.exp2(-ref[end + 8 + i : end + 9 + i, :])
            values[i] = values[i] + ref[i * lines : (i + 1) * lines, :] * scale
    powers[...] = total
    values.append(tail[...] + tail_b[...])
    end = 2 * lines + 16
    out[end:, :] = jnp.zeros((8, half), F32)
    for i, some in enumerate(values):
        top = jnp.max(jnp.max(jnp.abs(some), 0, keepdims=True), 1, keepdims=True)
        power = exponent(top)
        some = some * jnp.exp2(power)
        if i < 2:
            out[i * lines : (i + 1) * lines, :] = some
        else:
            high = some.astype(BF16).astype(F32)
            out[end - 16 : end - 8, :] = high
            out[end - 8 : end, :] = some - high
        out[end + i : end + i + 1, :] = jnp.broadcast_to(power, (1, half))


def column_parts(arrays):
    cols = lax.axis_size("col")
    taps, half = arrays[0].shape
    extra = taps % 256
    parts = call(
        lambda *refs: columns_kernel(cols, *refs),
        arrays,
        [shaped(((taps - extra) // cols + extra, half))] * cols,
        moved=4 * 10**6,
    )
    return list(parts)


def column_send(parts):
    cols = lax.axis_size("col")
    return [parts[0]] + [lax.ppermute(x, "col", p) for x, p in zip(parts[1:], shifts(cols))]


def row_sums(enc, dec, tail):
    cols, depth = len(enc), lax.axis_size("row") // 2
    taps, half = dec[0].shape
    lines = taps // depth
    parts = call(
        lambda *refs: rows_kernel(cols, *refs),
        enc + dec,
        [shaped((2 * lines + 8, half))] + [shaped((2 * lines + 16, half))] * (depth - 1),
        moved=4 * 10**6,
    )
    sent = [x.astype(F16) for x in parts[1:]]
    sent = [lax.ppermute(x, "row", p) for x, p in zip(sent, shifts(depth, 2))]
    parts = [parts[0]] + [x.astype(F32) for x in sent]
    return call(
        lambda *refs: chunk_kernel(depth, *refs),
        parts + [tail, pair_swap(tail)],
        (shaped((2 * lines + 24, half)), shaped((8, half))),
        moved=10**6,
    )


def gather_rows(chunk):
    own = chunk.astype(F16)
    steps = shifts(lax.axis_size("row") // 2, 2)
    return jnp.stack([own] + [lax.ppermute(own, "row", p) for p in steps])


def gather_columns(own):
    return [own] + [lax.ppermute(own, "col", p) for p in shifts(lax.axis_size("col"))]


def gather_cores(own, other):
    rows, cols = lax.axis_size("row"), lax.axis_size("col")
    lines, half = own[0].shape[1] // 2 - 12, own[0].shape[2]
    chunks = cols * rows // 2
    return call(
        lambda *refs: assemble_kernel(lines, *refs),
        own + other,
        (shaped((chunks, lines, 2 * half)), shaped((chunks, lines, 2 * half))),
        moved=10**7,
    )


def assemble_kernel(lines, *refs):
    pieces, outs = refs[:-2], refs[-2:]
    row, col, rows, cols = place_of()
    depth = rows // 2
    half = outs[0].shape[2] // 2
    for k, ref in enumerate(pieces):
        core = (row + k // cols) % 2
        c = (col + k % cols) % cols
        lanes = pl.ds(pl.multiple_of(core * half, half), half)
        for s in range(depth):
            z = (row // 2 + s) % depth
            for i, out in enumerate(outs):
                at = 2 * lines + 16 + i
                scale = jnp.exp2(-ref[s, at : at + 1, :])
                value = ref[s, i * lines : (i + 1) * lines, :] * scale
                out[c * depth + z, :, lanes] = value


def halo(fields):
    rows, cols = lax.axis_size("row"), lax.axis_size("col")
    forth = lambda n: [(i, i + 1) for i in range(n - 1)]
    back = lambda n: [(i + 1, i) for i in range(n - 1)]
    left_edge = jnp.stack([x[:, :HALO] for x in fields])
    right_edge = jnp.stack([x[:, -HALO:] for x in fields])
    left = lax.ppermute(right_edge, "col", forth(cols))
    right = lax.ppermute(left_edge, "col", back(cols))

    def lines(at):
        return jnp.concatenate([left[:, at], jnp.stack([x[at] for x in fields]), right[:, at]], 2)

    up = lax.ppermute(lines(slice(-HALO, None)), "row", forth(rows))
    down = lax.ppermute(lines(slice(0, HALO)), "row", back(rows))
    return left, right, up, down


def body(
    latents,
    code_ids,
    norm_gain,
    norm_bias,
    encoder_weight,
    codebook,
    decoder_weight,
    decoded_cotangent,
):
    height, width, channels = latents.shape
    devices = lax.axis_size("row") * lax.axis_size("col")
    codes_total = codebook.shape[0]
    shard = codes_total // devices
    count = height * width
    cap = 2 * count // devices
    pitch = width + 2 * SIDE
    conv_flops = 2 * count * 9 * channels * channels
    taps = 9 * channels
    half = channels // 2
    plane = (height + 2) * pitch
    plane_rows = plane + 2 * SIDE
    big = (height + 4) * pitch
    after = lambda *x: lax.optimization_barrier(x)
    halos = lambda field, start: [(start + i, field) for i in range(4)]

    payload, slots = call(
        lambda *refs: front_kernel(devices, shard, cap, *refs),
        (latents, code_ids),
        (shaped((devices, 8, width)), shaped((height, width), jnp.int32)),
        flops=10**9,
        moved=10**6,
        late=[(0, None)],
    )
    payload, code_ids, latents, decoded_cotangent = after(
        payload, code_ids, latents, decoded_cotangent
    )
    gathered = exchange(payload)
    quantized = codebook[code_ids]
    left, right, up, down = halo((latents, decoded_cotangent, quantized))
    gain = norm_gain.reshape(1, channels)
    bias = norm_bias.reshape(1, channels)

    dec_grad = call(
        decoder_grad_kernel,
        (decoded_cotangent, quantized, left, right, up, down),
        (shaped((taps, half)), shaped((taps, half))),
        [
            pltpu.VMEM((plane_rows, channels), F32),
            pltpu.VMEM((plane, 3 * channels), BF16),
            pltpu.VMEM((channels, height * pitch), BF16),
        ],
        flops=conv_flops,
        moved=5 * 10**6,
        late=[(0, None), *halos(1, 2), (1, None)],
    )
    dec_keep, dec_give = dec_grad
    gathered, dec_keep, dec_give = after(gathered, dec_keep, dec_give)
    dec_parts = column_parts((dec_keep, pair_swap(dec_give)))
    gathered, *dec_parts = after(gathered, *dec_parts)
    dec_parts = column_send(dec_parts)
    enc_fwd = encoder_weight.reshape(3, 3 * channels, channels)
    dec_fwd = decoder_weight.reshape(3, 3 * channels, channels)
    code_scale = codes_total / (count * devices)
    z, pull, turned, stats, power = call(
        lambda *refs: encoder_kernel(code_scale, *refs),
        (latents, left, right, up, down, quantized, gathered, gain, bias, enc_fwd),
        (
            shaped((plane_rows, channels)),
            shaped((count, channels)),
            shaped((channels, height * pitch), BF16),
            shaped((8, channels)),
            shaped((8, channels)),
        ),
        [
            pltpu.VMEM((big + 2 * SIDE, channels), F32),
            pltpu.VMEM((big, 3 * channels), BF16),
            pltpu.VMEM((plane_rows, channels), F32),
            pltpu.VMEM((channels, height * pitch), BF16),
            pltpu.VMEM((height * pitch, channels), F32),
            pltpu.SemaphoreType.DMA(((height + 2) // 3 + 1,)),
        ],
        far=(0, 2),
        flops=conv_flops,
        moved=10 * 10**6,
        room=20,
        late=[(0, None), *halos(0, 1), (9, None), (5, None)],
    )
    packed = call(
        pack_kernel,
        (slots.reshape(-1), pull, power),
        shaped((devices * cap, channels)),
        specs=[SMEM, VMEM, VMEM],
        flops=5 * 10**9,
        moved=6 * 10**6,
    )
    send = packed.astype(F16).reshape(devices, cap, channels)
    send, z, *dec_parts = after(send, z, *dec_parts)
    received = exchange(send)

    back_plane, keep_grad, give_grad = call(
        rotate_kernel,
        (
            decoded_cotangent, left, right, up, down, quantized, left, right, up, down, z, turned,
            decoder_weight, power,
        ),
        (
            shaped((plane_rows, channels)),
            shaped((taps + 8, half)),
            shaped((taps + 8, half)),
        ),
        [
            pltpu.VMEM((big + 2 * SIDE, channels), F32),
            pltpu.VMEM((plane_rows, channels), F32),
            pltpu.VMEM((big, 3 * channels), BF16),
            pltpu.VMEM((plane, 3 * channels), BF16),
            pltpu.VMEM((3, channels, 3 * channels), BF16),
            pltpu.VMEM((plane_rows, channels), F32),
            pltpu.SemaphoreType.DMA,
        ],
        far=(0,),
        flops=2 * conv_flops,
        moved=15 * 10**6,
        room=32,
        late=[
            (0, None), *halos(1, 1), (5, None), *halos(2, 6), (12, None), (10, None), (11, None)
        ],
    )
    enc_parts = column_send(column_parts((keep_grad, pair_swap(give_grad))))
    back_act, tail = call(
        back_kernel,
        (latents, back_plane, stats, gain, bias, encoder_weight),
        (shaped((height, width, channels)), shaped((8, half))),
        [
            pltpu.VMEM((plane, 3 * channels), BF16),
            pltpu.VMEM((3, channels, 3 * channels), BF16),
        ],
        flops=conv_flops,
        moved=8 * 10**6,
        late=[(1, None), (5, None), (0, None)],
    )
    decoded = call(
        decoder_kernel,
        (quantized, left, right, up, down, dec_fwd),
        shaped((height, width, channels), BF16),
        [
            pltpu.VMEM((plane_rows, channels), F32),
            pltpu.VMEM((plane, 3 * channels), BF16),
        ],
        flops=conv_flops,
        moved=4 * 10**6,
        late=[(0, None), *halos(2, 1), (5, None)],
    )
    decoded, *enc_parts = after(decoded, *enc_parts)
    chunk, powers = row_sums(enc_parts, dec_parts, tail)
    own = gather_rows(chunk)
    pieces = gather_columns(own)

    rows_f = received.astype(F32) * jnp.exp2(-jnp.round(powers[0, :devices]))[:, None, None]
    rows_f = rows_f.reshape(devices * cap, channels)
    high = lax.reduce_precision(rows_f, 8, 7)
    low = rows_f - high
    wide = jnp.concatenate([high.astype(BF16), low.astype(BF16)], 1)
    tags = gathered[:, 4, :cap].astype(jnp.int32).reshape(-1, 128)
    codebook_grad = call(
        owner_kernel,
        (tags, wide),
        shaped((shard, channels)),
        flops=2 * 10**9,
        moved=6 * 10**6,
    )
    codebook_grad, *pieces = after(codebook_grad, *pieces)
    other = [pair_swap(x) for x in pieces]
    own = [x.astype(F32) for x in pieces]
    latents_grad, norm_grads = call(
        last_kernel,
        (latents, back_act, back_plane, stats, gain, *own),
        (shaped((height, width, channels), BF16), shaped((2, channels))),
        flops=10**8,
        moved=6 * 10**6,
    )
    other = [x.astype(F32) for x in other]
    encoder_weight_grad, decoder_weight_grad = [
        x.reshape(3, 3, channels, channels) for x in gather_cores(own, other)
    ]
    return (
        decoded,
        latents_grad,
        norm_grads[1],
        norm_grads[0],
        encoder_weight_grad,
        decoder_weight_grad,
        codebook_grad,
    )


def solution(mesh):
    return jax.shard_map(
        body,
        mesh=mesh,
        in_specs=(
            P("row", "col", None),
            P("row", "col"),
            P(),
            P(),
            P(),
            P(),
            P(),
            P("row", "col", None),
        ),
        out_specs=(
            P("row", "col", None),
            P("row", "col", None),
            P(),
            P(),
            P(),
            P(),
            P(("row", "col"), None),
        ),
        check_vma=False,
    )
```

```python
import jax
import jax.numpy as jnp
from jax import lax
from jax.experimental import pallas as pl
from jax.experimental.pallas import tpu as pltpu
from jax.sharding import PartitionSpec as P

G = 32
epsilon = 1e-06
commit_beta = 0.25
F32 = jnp.float32
BF16 = jnp.bfloat16
F16 = jnp.float16
AXES = ("row", "col")
SIDE = 8
HALO = 2
VMEM = pl.BlockSpec(memory_space=pltpu.VMEM)
SMEM = pl.BlockSpec(memory_space=pltpu.SMEM)
ANY = pl.BlockSpec(memory_space=pltpu.HBM)
NT = (((1,), (1,)), ((), ()))
NN = (((1,), (0,)), ((), ()))
HIGH = lax.Precision.HIGHEST


class Late:
    def __init__(self, ref, copy):
        self.ref, self.copy = ref, copy
        copy.start()

    def get(self):
        if self.copy is not None:
            self.copy.wait()
            self.copy = None
        return self.ref


def call(kernel, ins, outs, scratch=(), specs=None, flops=0, moved=0, room=16, late=(), far=()):
    room = 56 if late else room
    specs = list(specs or [VMEM] * len(ins))
    first = len(ins) + len(jax.tree.leaves(outs)) + len(scratch)
    scratch = list(scratch)
    for i, field in late:
        specs[i] = ANY
        shape = ins[i].shape if field is None else ins[i].shape[1:]
        scratch.append(pltpu.VMEM(shape, ins[i].dtype))
    if late:
        scratch.append(pltpu.SemaphoreType.DMA((len(late),)))

    def wrapped(*refs):
        given = list(refs[:first])
        loads = []
        for j, (i, field) in enumerate(late):
            source = refs[i] if field is None else refs[i].at[field]
            copy = pltpu.make_async_copy(source, refs[first + j], refs[-1].at[j])
            given[i] = Late(refs[first + j], copy)
            loads.append(given[i])
        kernel(*given)
        for load in loads:
            load.get()

    return pl.pallas_call(
        wrapped,
        in_specs=specs,
        out_specs=jax.tree.unflatten(
            jax.tree.structure(outs),
            [ANY if i in far else VMEM for i in range(len(jax.tree.leaves(outs)))],
        ),
        out_shape=outs,
        scratch_shapes=scratch,
        compiler_params=pltpu.CompilerParams(vmem_limit_bytes=room * 2**20),
        cost_estimate=pl.CostEstimate(flops=flops, bytes_accessed=moved, transcendentals=0),
    )(*ins)


def use(*refs):
    return [ref.get() if isinstance(ref, Late) else ref for ref in refs]


def shaped(shape, dtype=F32):
    return jax.ShapeDtypeStruct(shape, dtype)


def dot(a, b, dims=NN, precision=None):
    return lax.dot_general(a, b, dims, precision=precision, preferred_element_type=F32)


def front_kernel(devices, shard, cap, lat, ids, payload, slots):
    height, width = ids.shape
    count = height * width

    owner = lax.broadcasted_iota(jnp.int32, (devices, width), 0)
    upper = (
        lax.broadcasted_iota(jnp.int32, (width, width), 0)
        < lax.broadcasted_iota(jnp.int32, (width, width), 1)
    ).astype(BF16)
    slot_row = lax.broadcasted_iota(jnp.int32, (width, width), 0)
    members, codes, dests = [], [], []
    for r in range(height):
        code = ids[r : r + 1, :]
        dest = code // shard
        codes.append(code - dest * shard)
        dests.append(dest)
        members.append((owner == dest).astype(F32))
    stacked = jnp.concatenate([x.astype(BF16) for x in members], 0)
    before = dot(stacked, upper)
    base = jnp.zeros((devices, 1), F32)
    hits, parts = [], []
    for r in range(height):
        member = members[r]
        count_before = before[r * devices : (r + 1) * devices] + base
        rank = jnp.sum(member * count_before, 0, keepdims=True).astype(jnp.int32)
        slots[r : r + 1, :] = dests[r] * cap + rank
        hits.append((slot_row == rank).astype(BF16))
        tagged = codes[r] + 1
        high = tagged // 32
        low = tagged - high * 32
        both = [member * high.astype(F32), member * low.astype(F32)]
        parts.append(jnp.concatenate(both, 0).astype(BF16))
        base = base + jnp.sum(member, 1, keepdims=True)
    placed = dot(jnp.concatenate(parts, 1), jnp.concatenate(hits, 1), NT)
    placed = 32.0 * placed[:devices] + placed[devices:]
    (lat,) = use(lat)
    channels = lat.shape[2]

    def add_row(r, total):
        return total + jnp.sum(lat[r].astype(F32), 0, keepdims=True)

    mean = lax.fori_loop(0, height, add_row, jnp.zeros((1, channels), F32), unroll=4) * (1.0 / count)

    def add_square(r, total):
        gap = lat[r].astype(F32) - mean
        return total + jnp.sum(gap * gap, 0, keepdims=True)

    square = lax.fori_loop(0, height, add_square, jnp.zeros((1, channels), F32), unroll=4)
    half = width
    rows = [mean[:, :half], mean[:, half:], square[:, :half], square[:, half:]]
    for i, part in enumerate(rows):
        payload[:, i, :] = jnp.broadcast_to(part, (devices, half))
    payload[:, 4, :] = placed
    payload[:, 5:, :] = jnp.zeros((devices, 3, half), F32)


def place_of():
    return (
        lax.axis_index("row"),
        lax.axis_index("col"),
        lax.axis_size("row"),
        lax.axis_size("col"),
    )


def place_of():
    return (
        lax.axis_index("row"),
        lax.axis_index("col"),
        lax.axis_size("row"),
        lax.axis_size("col"),
    )


def fill_tile(scr, own, left, right, up, down, ring):
    height, width, channels = own.shape
    pitch = width + 2 * SIDE
    for r in range(height):
        base = SIDE + (ring + r) * pitch
        scr[base + SIDE - HALO : base + SIDE] = left[r].astype(F32)
        scr[base + SIDE : base + SIDE + width] = own[r].astype(F32)
        scr[base + SIDE + width : base + SIDE + width + HALO] = right[r].astype(F32)
    span = up.shape[1]
    for i in range(ring):
        top = SIDE + i * pitch + SIDE - HALO
        scr[top : top + span] = up[HALO - ring + i].astype(F32)
        low = SIDE + (ring + height + i) * pitch + SIDE - HALO
        scr[low : low + span] = down[i].astype(F32)
    blank = jnp.zeros((SIDE - HALO, channels), F32)
    for r in range(height + 2 * ring):
        base = SIDE + r * pitch
        scr[base : base + SIDE - HALO] = blank
        scr[base + pitch - SIDE + HALO : base + pitch] = blank
    ends(scr, channels)


def ends(scr, channels):
    blank = jnp.zeros((SIDE, channels), F32)
    scr[0:SIDE] = blank
    scr[scr.shape[0] - SIDE :] = blank


def spread(scr, wide, count, pitch, channels):
    for r in range(count):
        value = scr[r * pitch : (r + 1) * pitch + 2 * SIDE, :]
        at = slice(r * pitch, (r + 1) * pitch)
        for j in range(3):
            start = SIDE + j - 1
            wide[at, j * channels : (j + 1) * channels] = value[start : start + pitch].astype(BF16)


def rows_at(r, pitch, count):
    if isinstance(r, int):
        return slice(r * pitch, (r + count) * pitch)
    return pl.ds(pl.multiple_of(r * pitch, 16), count * pitch)


def forward_rows(wide, weight, r, step, pitch):
    total = dot(wide[rows_at(r, pitch, step), :], weight[0])
    for dy in (1, 2):
        total = total + dot(wide[rows_at(r + dy, pitch, step), :], weight[dy])
    return total


def backward_rows(wide, weight, r, step, pitch):
    total = dot(wide[rows_at(r + 2, pitch, step), :], weight[0], NT)
    for dy in (1, 2):
        total = total + dot(wide[rows_at(r + 2 - dy, pitch, step), :], weight[dy], NT)
    return total


def kernel_grad(turned, wide, keep, give, pitch, height, first_row):
    channels = turned.shape[0]
    half = channels // 2
    count = height * pitch
    core = lax.axis_index("row") % 2
    for dy in range(3):
        start = (first_row + 1 - dy) * pitch
        product = dot(turned[...], wide[start : start + count, :])
        for j in range(3):
            at = (dy * 3 + 2 - j) * channels
            low = product[:, j * channels : j * channels + half]
            high = product[:, j * channels + half : (j + 1) * channels]

            keep[at : at + channels, :] = jnp.where(core == 0, low, high)
            give[at : at + channels, :] = jnp.where(core == 0, high, low)


def turn_own(own, turned):
    height, width, channels = own.shape
    pitch = width + 2 * SIDE
    blank = jnp.zeros((SIDE, channels), F32)
    for r in range(0, height, 8):
        parts = []
        for k in range(8):
            parts += [blank, own[r + k].astype(F32), blank]
        block = jnp.concatenate(parts, 0)
        turned[:, r * pitch : (r + 8) * pitch] = block.T.astype(BF16)


def decoder_grad_kernel(
    cot, codes, left, right, up, down, keep, give, scr, wide, turned
):
    cot, left, right, up, down = use(cot, left, right, up, down)
    height, width, channels = cot.shape
    pitch = width + 2 * SIDE
    fill_tile(scr, cot, left, right, up, down, 1)
    spread(scr, wide, height + 2, pitch, channels)
    turn_own(*use(codes), turned)
    kernel_grad(turned, wide, keep, give, pitch, height, 1)


def decoder_kernel(codes, left, right, up, down, weight, out, scr, wide):
    codes, left, right, up, down = use(codes, left, right, up, down)
    height, width, channels = codes.shape
    pitch = width + 2 * SIDE
    fill_tile(scr, codes, left, right, up, down, 1)
    spread(scr, wide, height + 2, pitch, channels)
    step = 4
    (weight,) = use(weight)

    def part(k, _):
        value = forward_rows(wide, weight, k * step, step, pitch)
        for u in range(step):
            at = u * pitch + SIDE
            out[k * step + u] = value[at : at + width].astype(BF16)
        return 0

    lax.fori_loop(0, height // step, part, 0)


def group_stats(gathered, height, width):
    devices = gathered.shape[0]
    rows, cols = lax.axis_size("row"), lax.axis_size("col")
    local = jnp.concatenate([gathered[:, 0, :], gathered[:, 1, :]], 1)
    square = jnp.concatenate([gathered[:, 2, :], gathered[:, 3, :]], 1)
    channels = local.shape[1]
    per_group = channels // G
    same = lax.broadcasted_iota(jnp.int32, (channels, channels), 0) // per_group
    same = same == lax.broadcasted_iota(jnp.int32, (channels, channels), 1) // per_group
    mix = jnp.where(same, 1.0 / per_group, 0.0).astype(F32)
    centre = jnp.broadcast_to(jnp.sum(local, 0, keepdims=True) * (1.0 / devices), (8, channels))
    mean = dot(centre, mix, precision=HIGH)[0:1]
    gap = local - mean
    spread_sum = square + (height * width) * (gap * gap)
    total = jnp.sum(spread_sum, 0, keepdims=True) * (1.0 / (devices * height * width))
    var = dot(jnp.broadcast_to(total, (8, channels)), mix, precision=HIGH)[0:1]
    return mean, lax.rsqrt(var + epsilon)


def inside_tile(row, col, rows, cols, height, width):
    pitch = width + 2 * SIDE
    place = lax.broadcasted_iota(jnp.int32, (pitch + 2 * SIDE, 1), 0) - 2 * SIDE + col * width
    inside_col = (place >= 0) & (place < cols * width)

    def keep(line):
        high = row * height + line
        return inside_col & (high >= 0) & (high < rows * height)

    return keep


def encoder_kernel(
    code_scale,
    lat, left, right, up, down, codes, gathered, gain, bias, weight,
    z_far, pull, turned_far, stats, power,
    tmp_s, wide, z_out, turned, own_s, sems,
):
    height, width, channels = codes.ref.shape
    pitch = width + 2 * SIDE
    keep = inside_tile(*place_of(), height, width)
    mean, inv = group_stats(gathered, height, width)
    stats[0:1, :] = mean
    stats[1:2, :] = inv
    fill_tile(tmp_s, *use(lat, left, right, up, down), 2)
    scale = inv * gain[...]
    offset = bias[...]

    blank = jnp.zeros((SIDE, channels), F32)

    def smooth_row(r):
        act = (tmp_s[r * pitch : (r + 1) * pitch + 2 * SIDE, :] - mean) * scale + offset
        value = jnp.where(keep(r - 2), act * jax.nn.sigmoid(act), 0.0)
        at = slice(r * pitch, (r + 1) * pitch)
        for j in range(3):
            start = SIDE + j - 1
            wide[at, j * channels : (j + 1) * channels] = value[start : start + pitch].astype(BF16)
        if 2 <= r < height + 2:
            base = (r - 2) * pitch
            own_s[base : base + SIDE, :] = blank
            own_s[base + SIDE : base + SIDE + width, :] = value[2 * SIDE : 2 * SIDE + width]
            own_s[base + SIDE + width : base + pitch, :] = blank

    step = 3
    steps = (height + 2) // step
    ends(z_out, channels)
    weight, codes = use(weight, codes)

    def z_copy(k):
        at = slice(SIDE + k * step * pitch, SIDE + (k + 1) * step * pitch)
        return pltpu.make_async_copy(z_out.at[at, :], z_far.at[at, :], sems.at[k])

    def part(k):
        first = SIDE + k * step * pitch
        count = step * pitch
        z = tmp_s[first + pitch : first + pitch + count, :]
        z = z + forward_rows(wide, weight, k * step, step, pitch)
        z_out[first : first + count, :] = z
        z_copy(k).start()
        tops = []
        for u in range(step):
            line = k * step + u - 1
            if 0 <= line < height:
                at = u * pitch + SIDE
                some = (codes[line].astype(F32) - z[at : at + width]) * code_scale
                pull[line * width : (line + 1) * width, :] = some
                tops.append(jnp.max(jnp.abs(some), 0, keepdims=True))
        return tops

    for r in range(step + 2):
        smooth_row(r)
    tops = []
    for k in range(steps):
        for r in range((k + 1) * step + 2, min((k + 2) * step + 2, height + 4)):
            smooth_row(r)
        tops += part(k)
    for r in range(0, height, 8):
        at = slice(r * pitch, (r + 8) * pitch)
        turned[:, at] = own_s[at, :].T.astype(BF16)
    turned_copy = pltpu.make_async_copy(turned, turned_far, sems.at[steps])
    turned_copy.start()
    top = jnp.max(jnp.concatenate(tops, 0), 0, keepdims=True)
    top = jnp.max(top, 1, keepdims=True)
    power[...] = jnp.broadcast_to(exponent(top), power.shape)
    for k in range(steps):
        z_copy(k).wait()
    turned_copy.wait()


def pack_kernel(slots, pull, power, packed):
    packed[...] = jnp.zeros(packed.shape, F32)
    scale = jnp.exp2(power[0:1, :])

    def some(i, _):
        value = pull[pl.ds(pl.multiple_of(i * 16, 8), 16), :] * scale
        for u in range(16):
            packed[pl.ds(slots[i * 16 + u], 1), :] = value[u : u + 1, :]
        return 0

    lax.fori_loop(0, pull.shape[0] // 16, some, 0, unroll=2)


def flip_weight(weight, flipped):
    channels = weight.shape[2]
    for dy in range(3):
        for j in range(3):
            flipped[dy, :, j * channels : (j + 1) * channels] = weight[dy, 2 - j]


def rotate_kernel(
    cot, left, right, up, down, codes, code_l, code_r, code_u, code_d, z_in, turned, dec_w, power,
    plane_far, keep_grad, give_grad,
    tmp_s, code_s, wide, back_wide, flipped, plane, sem,
):
    height, width, channels = cot.ref.shape
    pitch = width + 2 * SIDE
    fill_tile(tmp_s, *use(cot, left, right, up, down), 2)
    spread(tmp_s, wide, height + 4, pitch, channels)
    fill_tile(code_s, *use(codes, code_l, code_r, code_u, code_d), 1)
    flip_weight(*use(dec_w), flipped)
    ends(plane, channels)
    step = 3
    chunks = (height + 2) // step

    def part(k):
        at = slice(SIDE + k * step * pitch, SIDE + (k + 1) * step * pitch)
        plane[at, :] = backward_rows(wide, flipped, k * step, step, pitch)

    block = 24
    z_in, turned = use(z_in, turned)
    place = lax.broadcasted_iota(jnp.int32, (block, 1), 0)
    row, col, rows, cols = place_of()

    def total(x):
        return jnp.sum(x, 1, keepdims=True)

    def turn(line):
        spots = [
            slice(SIDE + line * pitch + b, SIDE + line * pitch + b + block)
            for b in range(0, pitch, block)
        ]
        sums = []
        for at in spots:
            z, e = z_in[at, :], code_s[at, :]
            sums.append((total(z * z) + epsilon, total(e * e) + epsilon))
        scales = []
        for at, (zz, ee) in zip(spots, sums):
            z, e, back = z_in[at, :], code_s[at, :], plane[at, :]
            z_inv, e_inv = lax.rsqrt(zz), lax.rsqrt(ee)
            e_unit = e * e_inv
            mirror = z * z_inv + e_unit
            scales.append(
                (z_inv, e_inv, ee, total(mirror * mirror) + epsilon, total(mirror * back),
                 total(e_unit * back))
            )
        high = row * height + line - 1
        keep = (high >= 0) & (high < rows * height)
        for b, (at, (z_inv, e_inv, ee, mm, along, code)) in enumerate(zip(spots, scales)):
            z, e, back = z_in[at, :], code_s[at, :], plane[at, :]
            stretch = ee * e_inv * z_inv
            along = 2.0 * along / mm
            z_part = stretch * z_inv * (2.0 * code - along) + commit_beta
            e_part = stretch * e_inv * along + commit_beta
            across = place + b * block - SIDE + col * width
            inside = keep & (across >= 0) & (across < cols * width)
            plane[at, :] = jnp.where(inside, stretch * back + z_part * z - e_part * e, 0.0)

    part(0)
    for k in range(chunks):
        if k + 1 < chunks:
            part(k + 1)
        for u in range(step):
            turn(k * step + u)
    plane_copy = pltpu.make_async_copy(plane, plane_far, sem)
    plane_copy.start()
    spread(plane, back_wide, height + 2, pitch, channels)
    kernel_grad(turned, back_wide, keep_grad, give_grad, pitch, height, 1)
    taps, half = keep_grad.shape[0] - 8, keep_grad.shape[1]
    lane = lax.broadcasted_iota(jnp.int32, (8, half), 1)
    mine = jnp.where(lane == row * cols + col, power[:, :half], 0.0)
    keep_grad[taps:, :] = mine
    give_grad[taps:, :] = mine
    plane_copy.wait()


def back_kernel(lat, plane, stats, gain, bias, enc_w, back_act, tail, back_wide, flipped):
    (plane,) = use(plane)
    height, width, channels = lat.ref.shape
    pitch = width + 2 * SIDE
    spread(plane, back_wide, height + 2, pitch, channels)
    flip_weight(*use(enc_w), flipped)
    (lat,) = use(lat)
    mean, inv = stats[0:1, :], stats[1:2, :]
    step = 4

    def last(k, totals):
        value = backward_rows(back_wide, flipped, k * step, step, pitch)
        first, second = totals
        for u in range(step):
            at = u * pitch + SIDE
            normed = (lat[k * step + u].astype(F32) - mean) * inv
            act = normed * gain[...] + bias[...]
            s = jax.nn.sigmoid(act)
            some = value[at : at + width] * s * (1.0 + act * (1.0 - s))
            back_act[k * step + u] = some
            first = first + jnp.sum(some, 0, keepdims=True)
            second = second + jnp.sum(some * normed, 0, keepdims=True)
        return first, second

    zero = jnp.zeros((1, channels), F32)
    first, second = lax.fori_loop(0, height // step, last, (zero, zero))
    half = channels // 2
    lines = [first[:, :half], first[:, half:], second[:, :half], second[:, half:]]
    tail[...] = jnp.concatenate(lines + [jnp.zeros((4, half), F32)], 0)


def last_kernel(lat, back_act, plane, stats, gain, *refs):
    pieces, (out, grads) = refs[:-2], refs[-2:]
    height, width, channels = lat.shape
    mean, inv = stats[0:1, :], stats[1:2, :]
    per_group = channels // G
    count = height * width * lax.axis_size("row") * lax.axis_size("col") * per_group
    end = pieces[0].shape[1] - 24
    sums = jnp.zeros((8, pieces[0].shape[2]), F32)
    for ref in pieces:
        for z in range(ref.shape[0]):
            some = ref[z, end : end + 8, :] + ref[z, end + 8 : end + 16, :]
            sums = sums + some * jnp.exp2(-ref[z, end + 18 : end + 19, :])
    first = jnp.concatenate([sums[0:1, :], sums[1:2, :]], 1)
    second = jnp.concatenate([sums[2:3, :], sums[3:4, :]], 1)
    grads[0:1, :] = first
    grads[1:2, :] = second
    same = lax.broadcasted_iota(jnp.int32, (channels, channels), 0) // per_group
    same = same == lax.broadcasted_iota(jnp.int32, (channels, channels), 1) // per_group
    mix = jnp.where(same, 1.0, 0.0).astype(F32)
    both = jnp.concatenate([first * gain[...], second * gain[...]] + [first] * 6, 0)
    means = dot(both, mix, precision=HIGH) * (1.0 / count)

    lat, back_act, plane = use(lat, back_act, plane)

    def one(r, _):
        normed = (lat[r].astype(F32) - mean) * inv
        d = back_act[r] * gain[...]
        at = pl.multiple_of((r + 1) * (width + 2 * SIDE) + 2 * SIDE, 8)
        enc_back = plane[pl.ds(at, width), :]
        out[r] = (inv * (d - means[0:1] - normed * means[1:2]) + enc_back).astype(BF16)
        return 0

    lax.fori_loop(0, height, one, 0)


def owner_kernel(tags, wide, out):
    shard, channels = out.shape
    total = jnp.zeros((shard, 2 * channels), F32)
    rows = wide.shape[0]
    chunk = 1024
    code = lax.broadcasted_iota(jnp.int32, (shard, tags.shape[1]), 0) + 1
    lines = chunk // tags.shape[1]
    for k in range(rows // chunk):
        hit = jnp.concatenate(
            [
                (code == tags[k * lines + u : k * lines + u + 1, :]).astype(F32).astype(BF16)
                for u in range(lines)
            ],
            1,
        )
        total = total + dot(hit, wide[k * chunk : (k + 1) * chunk, :])
    out[...] = total[:, :channels] + total[:, channels:]


def exponent(biggest):
    return 14.0 - jnp.ceil(jnp.log2(jnp.maximum(biggest, 1e-30)))


def exchange(x):
    return lax.all_to_all(x, AXES, split_axis=0, concat_axis=0, tiled=True)


def pair_swap(x):
    size = lax.axis_size("row")
    return lax.ppermute(x, "row", [(i, i ^ 1) for i in range(size)])


def shifts(n, stride=1):
    size = n * stride
    return [[((i + s * stride) % size, i) for i in range(size)] for s in range(1, n)]


def finish(outs, lines, tail, tops):
    end = 2 * lines
    powers = [exponent(jnp.max(top, 1, keepdims=True)) for top in tops]
    outs[0][end:, :] = tail
    for out in outs[1:]:
        out[end : end + 8, :] = tail
        out[end + 8 :, :] = jnp.zeros((8, tail.shape[1]), F32)
        for i, power in enumerate(powers):
            at = slice(i * lines, (i + 1) * lines)
            out[at, :] = out[at, :] * jnp.exp2(power)
            out[end + 8 + i : end + 9 + i, :] = jnp.broadcast_to(power, (1, tail.shape[1]))


def columns_kernel(cols, enc, enc_b, dec, dec_b, *outs):
    col = lax.axis_index("col")
    taps = dec.shape[0]
    lines = taps // cols
    tops = [jnp.zeros((1, dec.shape[1]), F32)] * 2
    for s, out in enumerate(outs):
        at = pl.ds(pl.multiple_of((col + cols - s) % cols * lines, 8), lines)
        for i, (one, two) in enumerate(((enc, enc_b), (dec, dec_b))):
            some = one[at, :] + two[at, :]
            out[i * lines : (i + 1) * lines, :] = some
            tops[i] = jnp.maximum(tops[i], jnp.max(jnp.abs(some), 0, keepdims=True))
    finish(outs, lines, enc[taps:, :] + enc_b[taps:, :], tops)


def rows_kernel(cols, *refs):
    parts, outs = refs[:cols], refs[cols:]
    row, _, rows, _ = place_of()
    depth = rows // 2
    lines = outs[0].shape[0] // 2 - 4
    wide = depth * lines
    end = 2 * wide
    scales = [
        [jnp.exp2(-ref[end + 8 + i : end + 9 + i, :]) for ref in parts[1:]] for i in range(2)
    ]

    def added(i, first, count):
        at = slice(i * wide + first, i * wide + first + count)
        value = parts[0][at, :]
        for ref, scale in zip(parts[1:], scales[i]):
            value = value + ref[at, :] * scale
        return value

    tail = parts[0][end:, :]
    for ref in parts[1:]:
        tail = tail + ref[end : end + 8, :]
    tops = [jnp.zeros((1, tail.shape[1]), F32)] * 2
    for z in range(depth):
        values = [added(i, z * lines, lines) for i in range(2)]
        tops = [
            jnp.maximum(top, jnp.max(jnp.abs(some), 0, keepdims=True))
            for top, some in zip(tops, values)
        ]
        for s, out in enumerate(outs):

            @pl.when((row // 2 + depth - s) % depth == z)
            def _():
                for i in range(2):
                    out[i * lines : (i + 1) * lines, :] = values[i]

    finish(outs, lines, tail, tops)


def chunk_kernel(depth, *refs):
    parts, (tail, tail_b, out, powers) = refs[:depth], refs[depth:]
    half = out.shape[1]
    lines = parts[0].shape[0] // 2 - 4
    end = 2 * lines
    total = parts[0][end:, :]
    values = [parts[0][i * lines : (i + 1) * lines, :] for i in range(2)]
    for ref in parts[1:]:
        total = total + ref[end : end + 8, :]
        for i in range(2):
            scale = jnp.exp2(-ref[end + 8 + i : end + 9 + i, :])
            values[i] = values[i] + ref[i * lines : (i + 1) * lines, :] * scale
    powers[...] = total
    values.append(tail[...] + tail_b[...])
    end = 2 * lines + 16
    out[end:, :] = jnp.zeros((8, half), F32)
    for i, some in enumerate(values):
        top = jnp.max(jnp.max(jnp.abs(some), 0, keepdims=True), 1, keepdims=True)
        power = exponent(top)
        some = some * jnp.exp2(power)
        if i < 2:
            out[i * lines : (i + 1) * lines, :] = some
        else:
            high = some.astype(BF16).astype(F32)
            out[end - 16 : end - 8, :] = high
            out[end - 8 : end, :] = some - high
        out[end + i : end + i + 1, :] = jnp.broadcast_to(power, (1, half))


def message_shapes(lines, half, count):
    return [shaped((2 * lines + 8, half))] + [shaped((2 * lines + 16, half))] * (count - 1)


def pass_on(parts, axis, perms):
    sent = [lax.ppermute(x.astype(F16), axis, p) for x, p in zip(parts[1:], perms)]
    return [parts[0]] + [x.astype(F32) for x in sent]


def column_sums(arrays):
    cols = lax.axis_size("col")
    taps, half = arrays[2].shape
    parts = call(
        lambda *refs: columns_kernel(cols, *refs),
        arrays,
        message_shapes(taps // cols, half, cols),
        moved=8 * 10**6,
    )
    return pass_on(parts, "col", shifts(cols))


def row_sums(parts, tail):
    cols, depth = len(parts), lax.axis_size("row") // 2
    half = parts[0].shape[1]
    lines = (parts[0].shape[0] // 2 - 4) // depth
    parts = call(
        lambda *refs: rows_kernel(cols, *refs),
        parts,
        message_shapes(lines, half, depth),
        moved=4 * 10**6,
    )
    parts = pass_on(parts, "row", shifts(depth, 2))
    return call(
        lambda *refs: chunk_kernel(depth, *refs),
        parts + [tail, pair_swap(tail)],
        (shaped((2 * lines + 24, half)), shaped((8, half))),
        moved=10**6,
    )


def gather_rows(chunk):
    own = chunk.astype(F16)
    steps = shifts(lax.axis_size("row") // 2, 2)
    return jnp.stack([own] + [lax.ppermute(own, "row", p) for p in steps])


def gather_columns(own):
    return [own] + [lax.ppermute(own, "col", p) for p in shifts(lax.axis_size("col"))]


def gather_cores(own, other):
    rows, cols = lax.axis_size("row"), lax.axis_size("col")
    lines, half = own[0].shape[1] // 2 - 12, own[0].shape[2]
    chunks = cols * rows // 2
    return call(
        lambda *refs: assemble_kernel(lines, *refs),
        own + other,
        (shaped((chunks, lines, 2 * half)), shaped((chunks, lines, 2 * half))),
        moved=10**7,
    )


def assemble_kernel(lines, *refs):
    pieces, outs = refs[:-2], refs[-2:]
    row, col, rows, cols = place_of()
    depth = rows // 2
    half = outs[0].shape[2] // 2
    for k, ref in enumerate(pieces):
        core = (row + k // cols) % 2
        c = (col + k % cols) % cols
        lanes = pl.ds(pl.multiple_of(core * half, half), half)
        for s in range(depth):
            z = (row // 2 + s) % depth
            for i, out in enumerate(outs):
                at = 2 * lines + 16 + i
                scale = jnp.exp2(-ref[s, at : at + 1, :])
                value = ref[s, i * lines : (i + 1) * lines, :] * scale
                out[c * depth + z, :, lanes] = value


def halo(fields):
    rows, cols = lax.axis_size("row"), lax.axis_size("col")
    forth = lambda n: [(i, i + 1) for i in range(n - 1)]
    back = lambda n: [(i + 1, i) for i in range(n - 1)]
    left_edge = jnp.stack([x[:, :HALO] for x in fields])
    right_edge = jnp.stack([x[:, -HALO:] for x in fields])
    left = lax.ppermute(right_edge, "col", forth(cols))
    right = lax.ppermute(left_edge, "col", back(cols))

    def lines(at):
        return jnp.concatenate([left[:, at], jnp.stack([x[at] for x in fields]), right[:, at]], 2)

    up = lax.ppermute(lines(slice(-HALO, None)), "row", forth(rows))
    down = lax.ppermute(lines(slice(0, HALO)), "row", back(rows))
    return left, right, up, down


def body(
    latents,
    code_ids,
    norm_gain,
    norm_bias,
    encoder_weight,
    codebook,
    decoder_weight,
    decoded_cotangent,
):
    height, width, channels = latents.shape
    devices = lax.axis_size("row") * lax.axis_size("col")
    codes_total = codebook.shape[0]
    shard = codes_total // devices
    count = height * width
    cap = 2 * count // devices
    pitch = width + 2 * SIDE
    conv_flops = 2 * count * 9 * channels * channels
    taps = 9 * channels
    half = channels // 2
    plane = (height + 2) * pitch
    plane_rows = plane + 2 * SIDE
    big = (height + 4) * pitch
    after = lambda *x: lax.optimization_barrier(x)
    halos = lambda field, start: [(start + i, field) for i in range(4)]

    payload, slots = call(
        lambda *refs: front_kernel(devices, shard, cap, *refs),
        (latents, code_ids),
        (shaped((devices, 8, width)), shaped((height, width), jnp.int32)),
        flops=10**9,
        moved=10**6,
        late=[(0, None)],
    )
    payload, code_ids, latents, decoded_cotangent = after(
        payload, code_ids, latents, decoded_cotangent
    )
    gathered = exchange(payload)
    quantized = codebook[code_ids]
    left, right, up, down = halo((latents, decoded_cotangent, quantized))
    gain = norm_gain.reshape(1, channels)
    bias = norm_bias.reshape(1, channels)

    dec_grad = call(
        decoder_grad_kernel,
        (decoded_cotangent, quantized, left, right, up, down),
        (shaped((taps, half)), shaped((taps, half))),
        [
            pltpu.VMEM((plane_rows, channels), F32),
            pltpu.VMEM((plane, 3 * channels), BF16),
            pltpu.VMEM((channels, height * pitch), BF16),
        ],
        flops=conv_flops,
        moved=5 * 10**6,
        late=[(0, None), *halos(1, 2), (1, None)],
    )
    dec_keep, dec_give = dec_grad
    gathered, dec_keep, dec_give = after(gathered, dec_keep, dec_give)
    dec_given = pair_swap(dec_give)
    enc_fwd = encoder_weight.reshape(3, 3 * channels, channels)
    dec_fwd = decoder_weight.reshape(3, 3 * channels, channels)
    code_scale = codes_total / (count * devices)
    z, pull, turned, stats, power = call(
        lambda *refs: encoder_kernel(code_scale, *refs),
        (latents, left, right, up, down, quantized, gathered, gain, bias, enc_fwd),
        (
            shaped((plane_rows, channels)),
            shaped((count, channels)),
            shaped((channels, height * pitch), BF16),
            shaped((8, channels)),
            shaped((8, channels)),
        ),
        [
            pltpu.VMEM((big + 2 * SIDE, channels), F32),
            pltpu.VMEM((big, 3 * channels), BF16),
            pltpu.VMEM((plane_rows, channels), F32),
            pltpu.VMEM((channels, height * pitch), BF16),
            pltpu.VMEM((height * pitch, channels), F32),
            pltpu.SemaphoreType.DMA(((height + 2) // 3 + 1,)),
        ],
        far=(0, 2),
        flops=conv_flops,
        moved=10 * 10**6,
        room=20,
        late=[(0, None), *halos(0, 1), (9, None), (5, None)],
    )
    packed = call(
        pack_kernel,
        (slots.reshape(-1), pull, power),
        shaped((devices * cap, channels)),
        specs=[SMEM, VMEM, VMEM],
        flops=5 * 10**9,
        moved=6 * 10**6,
    )
    send = packed.astype(F16).reshape(devices, cap, channels)
    send, z, dec_given = after(send, z, dec_given)
    received = exchange(send)

    back_plane, keep_grad, give_grad = call(
        rotate_kernel,
        (
            decoded_cotangent, left, right, up, down, quantized, left, right, up, down, z, turned,
            decoder_weight, power,
        ),
        (
            shaped((plane_rows, channels)),
            shaped((taps + 8, half)),
            shaped((taps + 8, half)),
        ),
        [
            pltpu.VMEM((big + 2 * SIDE, channels), F32),
            pltpu.VMEM((plane_rows, channels), F32),
            pltpu.VMEM((big, 3 * channels), BF16),
            pltpu.VMEM((plane, 3 * channels), BF16),
            pltpu.VMEM((3, channels, 3 * channels), BF16),
            pltpu.VMEM((plane_rows, channels), F32),
            pltpu.SemaphoreType.DMA,
        ],
        far=(0,),
        flops=2 * conv_flops,
        moved=15 * 10**6,
        room=32,
        late=[
            (0, None), *halos(1, 1), (5, None), *halos(2, 6), (12, None), (10, None), (11, None)
        ],
    )
    parts = column_sums((keep_grad, pair_swap(give_grad), dec_keep, dec_given))
    back_act, tail = call(
        back_kernel,
        (latents, back_plane, stats, gain, bias, encoder_weight),
        (shaped((height, width, channels)), shaped((8, half))),
        [
            pltpu.VMEM((plane, 3 * channels), BF16),
            pltpu.VMEM((3, channels, 3 * channels), BF16),
        ],
        flops=conv_flops,
        moved=8 * 10**6,
        late=[(1, None), (5, None), (0, None)],
    )
    decoded = call(
        decoder_kernel,
        (quantized, left, right, up, down, dec_fwd),
        shaped((height, width, channels), BF16),
        [
            pltpu.VMEM((plane_rows, channels), F32),
            pltpu.VMEM((plane, 3 * channels), BF16),
        ],
        flops=conv_flops,
        moved=4 * 10**6,
        late=[(0, None), *halos(2, 1), (5, None)],
    )
    decoded, *parts = after(decoded, *parts)
    chunk, powers = row_sums(parts, tail)
    own = gather_rows(chunk)
    pieces = gather_columns(own)

    rows_f = received.astype(F32) * jnp.exp2(-jnp.round(powers[0, :devices]))[:, None, None]
    rows_f = rows_f.reshape(devices * cap, channels)
    high = lax.reduce_precision(rows_f, 8, 7)
    low = rows_f - high
    wide = jnp.concatenate([high.astype(BF16), low.astype(BF16)], 1)
    tags = gathered[:, 4, :cap].astype(jnp.int32).reshape(-1, 128)
    codebook_grad = call(
        owner_kernel,
        (tags, wide),
        shaped((shard, channels)),
        flops=2 * 10**9,
        moved=6 * 10**6,
    )
    codebook_grad, *pieces = after(codebook_grad, *pieces)
    other = [pair_swap(x) for x in pieces]
    own = [x.astype(F32) for x in pieces]
    latents_grad, norm_grads = call(
        last_kernel,
        (latents, back_act, back_plane, stats, gain, *own),
        (shaped((height, width, channels), BF16), shaped((2, channels))),
        flops=10**8,
        moved=6 * 10**6,
    )
    other = [x.astype(F32) for x in other]
    encoder_weight_grad, decoder_weight_grad = [
        x.reshape(3, 3, channels, channels) for x in gather_cores(own, other)
    ]
    return (
        decoded,
        latents_grad,
        norm_grads[1],
        norm_grads[0],
        encoder_weight_grad,
        decoder_weight_grad,
        codebook_grad,
    )


def solution(mesh):
    return jax.shard_map(
        body,
        mesh=mesh,
        in_specs=(
            P("row", "col", None),
            P("row", "col"),
            P(),
            P(),
            P(),
            P(),
            P(),
            P("row", "col", None),
        ),
        out_specs=(
            P("row", "col", None),
            P("row", "col", None),
            P(),
            P(),
            P(),
            P(),
            P(("row", "col"), None),
        ),
        check_vma=False,
    )
```

```python
import jax
import jax.numpy as jnp
from jax import lax
from jax.experimental import pallas as pl
from jax.experimental.pallas import tpu as pltpu
from jax.sharding import PartitionSpec as P

G = 32
epsilon = 1e-06
commit_beta = 0.25
F32 = jnp.float32
BF16 = jnp.bfloat16
F16 = jnp.float16
AXES = ("row", "col")
SIDE = 8
HALO = 2
VMEM = pl.BlockSpec(memory_space=pltpu.VMEM)
SMEM = pl.BlockSpec(memory_space=pltpu.SMEM)
ANY = pl.BlockSpec(memory_space=pltpu.HBM)
NT = (((1,), (1,)), ((), ()))
NN = (((1,), (0,)), ((), ()))
HIGH = lax.Precision.HIGHEST


class Late:
    def __init__(self, ref, copy):
        self.ref, self.copy = ref, copy
        copy.start()

    def get(self):
        if self.copy is not None:
            self.copy.wait()
            self.copy = None
        return self.ref


def call(kernel, ins, outs, scratch=(), specs=None, flops=0, moved=0, room=16, late=(), far=()):
    room = 56 if late else room
    specs = list(specs or [VMEM] * len(ins))
    first = len(ins) + len(jax.tree.leaves(outs)) + len(scratch)
    scratch = list(scratch)
    for i, field in late:
        specs[i] = ANY
        shape = ins[i].shape if field is None else ins[i].shape[1:]
        scratch.append(pltpu.VMEM(shape, ins[i].dtype))
    if late:
        scratch.append(pltpu.SemaphoreType.DMA((len(late),)))

    def wrapped(*refs):
        given = list(refs[:first])
        loads = []
        for j, (i, field) in enumerate(late):
            source = refs[i] if field is None else refs[i].at[field]
            copy = pltpu.make_async_copy(source, refs[first + j], refs[-1].at[j])
            given[i] = Late(refs[first + j], copy)
            loads.append(given[i])
        kernel(*given)
        for load in loads:
            load.get()

    return pl.pallas_call(
        wrapped,
        in_specs=specs,
        out_specs=jax.tree.unflatten(
            jax.tree.structure(outs),
            [ANY if i in far else VMEM for i in range(len(jax.tree.leaves(outs)))],
        ),
        out_shape=outs,
        scratch_shapes=scratch,
        compiler_params=pltpu.CompilerParams(vmem_limit_bytes=room * 2**20),
        cost_estimate=pl.CostEstimate(flops=flops, bytes_accessed=moved, transcendentals=0),
    )(*ins)


def use(*refs):
    return [ref.get() if isinstance(ref, Late) else ref for ref in refs]


def shaped(shape, dtype=F32):
    return jax.ShapeDtypeStruct(shape, dtype)


def dot(a, b, dims=NN, precision=None):
    return lax.dot_general(a, b, dims, precision=precision, preferred_element_type=F32)


def front_kernel(devices, shard, cap, lat, ids, payload, slots):
    height, width = ids.shape
    count = height * width

    owner = lax.broadcasted_iota(jnp.int32, (devices, width), 0)
    upper = (
        lax.broadcasted_iota(jnp.int32, (width, width), 0)
        < lax.broadcasted_iota(jnp.int32, (width, width), 1)
    ).astype(BF16)
    slot_row = lax.broadcasted_iota(jnp.int32, (width, width), 0)
    members, codes, dests = [], [], []
    for r in range(height):
        code = ids[r : r + 1, :]
        dest = code // shard
        codes.append(code - dest * shard)
        dests.append(dest)
        members.append((owner == dest).astype(F32))
    stacked = jnp.concatenate([x.astype(BF16) for x in members], 0)
    before = dot(stacked, upper)
    base = jnp.zeros((devices, 1), F32)
    hits, parts = [], []
    for r in range(height):
        member = members[r]
        count_before = before[r * devices : (r + 1) * devices] + base
        rank = jnp.sum(member * count_before, 0, keepdims=True).astype(jnp.int32)
        slots[r : r + 1, :] = dests[r] * cap + rank
        hits.append((slot_row == rank).astype(BF16))
        tagged = codes[r] + 1
        high = tagged // 32
        low = tagged - high * 32
        both = [member * high.astype(F32), member * low.astype(F32)]
        parts.append(jnp.concatenate(both, 0).astype(BF16))
        base = base + jnp.sum(member, 1, keepdims=True)
    placed = dot(jnp.concatenate(parts, 1), jnp.concatenate(hits, 1), NT)
    placed = 32.0 * placed[:devices] + placed[devices:]
    (lat,) = use(lat)
    channels = lat.shape[2]

    def add_row(r, total):
        return total + jnp.sum(lat[r].astype(F32), 0, keepdims=True)

    mean = lax.fori_loop(0, height, add_row, jnp.zeros((1, channels), F32), unroll=4) * (1.0 / count)

    def add_square(r, total):
        gap = lat[r].astype(F32) - mean
        return total + jnp.sum(gap * gap, 0, keepdims=True)

    square = lax.fori_loop(0, height, add_square, jnp.zeros((1, channels), F32), unroll=4)
    half = width
    rows = [mean[:, :half], mean[:, half:], square[:, :half], square[:, half:]]
    for i, part in enumerate(rows):
        payload[:, i, :] = jnp.broadcast_to(part, (devices, half))
    payload[:, 4, :] = placed
    payload[:, 5:, :] = jnp.zeros((devices, 3, half), F32)


def place_of():
    return (
        lax.axis_index("row"),
        lax.axis_index("col"),
        lax.axis_size("row"),
        lax.axis_size("col"),
    )


def place_of():
    return (
        lax.axis_index("row"),
        lax.axis_index("col"),
        lax.axis_size("row"),
        lax.axis_size("col"),
    )


def fill_tile(scr, own, left, right, up, down, ring):
    height, width, channels = own.shape
    pitch = width + 2 * SIDE
    for r in range(height):
        base = SIDE + (ring + r) * pitch
        scr[base + SIDE - HALO : base + SIDE] = left[r].astype(F32)
        scr[base + SIDE : base + SIDE + width] = own[r].astype(F32)
        scr[base + SIDE + width : base + SIDE + width + HALO] = right[r].astype(F32)
    span = up.shape[1]
    for i in range(ring):
        top = SIDE + i * pitch + SIDE - HALO
        scr[top : top + span] = up[HALO - ring + i].astype(F32)
        low = SIDE + (ring + height + i) * pitch + SIDE - HALO
        scr[low : low + span] = down[i].astype(F32)
    blank = jnp.zeros((SIDE - HALO, channels), F32)
    for r in range(height + 2 * ring):
        base = SIDE + r * pitch
        scr[base : base + SIDE - HALO] = blank
        scr[base + pitch - SIDE + HALO : base + pitch] = blank
    ends(scr, channels)


def ends(scr, channels):
    blank = jnp.zeros((SIDE, channels), F32)
    scr[0:SIDE] = blank
    scr[scr.shape[0] - SIDE :] = blank


def spread(scr, wide, count, pitch, channels):
    for r in range(count):
        value = scr[r * pitch : (r + 1) * pitch + 2 * SIDE, :]
        at = slice(r * pitch, (r + 1) * pitch)
        for j in range(3):
            start = SIDE + j - 1
            wide[at, j * channels : (j + 1) * channels] = value[start : start + pitch].astype(BF16)


def rows_at(r, pitch, count):
    if isinstance(r, int):
        return slice(r * pitch, (r + count) * pitch)
    return pl.ds(pl.multiple_of(r * pitch, 16), count * pitch)


def forward_rows(wide, weight, r, step, pitch):
    total = dot(wide[rows_at(r, pitch, step), :], weight[0])
    for dy in (1, 2):
        total = total + dot(wide[rows_at(r + dy, pitch, step), :], weight[dy])
    return total


def backward_rows(wide, weight, r, step, pitch):
    total = dot(wide[rows_at(r + 2, pitch, step), :], weight[0], NT)
    for dy in (1, 2):
        total = total + dot(wide[rows_at(r + 2 - dy, pitch, step), :], weight[dy], NT)
    return total


def kernel_grad(turned, wide, keep, give, pitch, height, first_row):
    channels = turned.shape[0]
    half = channels // 2
    count = height * pitch
    core = lax.axis_index("row") % 2
    for dy in range(3):
        start = (first_row + 1 - dy) * pitch
        product = dot(turned[...], wide[start : start + count, :])
        for j in range(3):
            at = (dy * 3 + 2 - j) * channels
            low = product[:, j * channels : j * channels + half]
            high = product[:, j * channels + half : (j + 1) * channels]

            keep[at : at + channels, :] = jnp.where(core == 0, low, high)
            give[at : at + channels, :] = jnp.where(core == 0, high, low)


def turn_own(own, turned):
    height, width, channels = own.shape
    pitch = width + 2 * SIDE
    blank = jnp.zeros((SIDE, channels), F32)
    for r in range(0, height, 8):
        parts = []
        for k in range(8):
            parts += [blank, own[r + k].astype(F32), blank]
        block = jnp.concatenate(parts, 0)
        turned[:, r * pitch : (r + 8) * pitch] = block.T.astype(BF16)


def decoder_grad_kernel(
    cot, codes, left, right, up, down, keep, give, scr, wide, turned
):
    cot, left, right, up, down = use(cot, left, right, up, down)
    height, width, channels = cot.shape
    pitch = width + 2 * SIDE
    fill_tile(scr, cot, left, right, up, down, 1)
    spread(scr, wide, height + 2, pitch, channels)
    turn_own(*use(codes), turned)
    kernel_grad(turned, wide, keep, give, pitch, height, 1)


def decoder_kernel(codes, left, right, up, down, weight, out, scr, wide):
    codes, left, right, up, down = use(codes, left, right, up, down)
    height, width, channels = codes.shape
    pitch = width + 2 * SIDE
    fill_tile(scr, codes, left, right, up, down, 1)
    spread(scr, wide, height + 2, pitch, channels)
    step = 4
    (weight,) = use(weight)

    def part(k, _):
        value = forward_rows(wide, weight, k * step, step, pitch)
        for u in range(step):
            at = u * pitch + SIDE
            out[k * step + u] = value[at : at + width].astype(BF16)
        return 0

    lax.fori_loop(0, height // step, part, 0)


def group_stats(gathered, height, width):
    devices = gathered.shape[0]
    rows, cols = lax.axis_size("row"), lax.axis_size("col")
    local = jnp.concatenate([gathered[:, 0, :], gathered[:, 1, :]], 1)
    square = jnp.concatenate([gathered[:, 2, :], gathered[:, 3, :]], 1)
    channels = local.shape[1]
    per_group = channels // G
    same = lax.broadcasted_iota(jnp.int32, (channels, channels), 0) // per_group
    same = same == lax.broadcasted_iota(jnp.int32, (channels, channels), 1) // per_group
    mix = jnp.where(same, 1.0 / per_group, 0.0).astype(F32)
    centre = jnp.broadcast_to(jnp.sum(local, 0, keepdims=True) * (1.0 / devices), (8, channels))
    mean = dot(centre, mix, precision=HIGH)[0:1]
    gap = local - mean
    spread_sum = square + (height * width) * (gap * gap)
    total = jnp.sum(spread_sum, 0, keepdims=True) * (1.0 / (devices * height * width))
    var = dot(jnp.broadcast_to(total, (8, channels)), mix, precision=HIGH)[0:1]
    return mean, lax.rsqrt(var + epsilon)


def inside_tile(row, col, rows, cols, height, width):
    pitch = width + 2 * SIDE
    place = lax.broadcasted_iota(jnp.int32, (pitch + 2 * SIDE, 1), 0) - 2 * SIDE + col * width
    inside_col = (place >= 0) & (place < cols * width)

    def keep(line):
        high = row * height + line
        return inside_col & (high >= 0) & (high < rows * height)

    return keep


def encoder_kernel(
    code_scale,
    lat, left, right, up, down, codes, gathered, gain, bias, weight,
    z_far, pull, turned_far, stats, power,
    tmp_s, wide, z_out, turned, own_s, sems,
):
    height, width, channels = codes.ref.shape
    pitch = width + 2 * SIDE
    keep = inside_tile(*place_of(), height, width)
    mean, inv = group_stats(gathered, height, width)
    stats[0:1, :] = mean
    stats[1:2, :] = inv
    fill_tile(tmp_s, *use(lat, left, right, up, down), 2)
    scale = inv * gain[...]
    offset = bias[...]

    blank = jnp.zeros((SIDE, channels), F32)

    def smooth_row(r):
        act = (tmp_s[r * pitch : (r + 1) * pitch + 2 * SIDE, :] - mean) * scale + offset
        value = jnp.where(keep(r - 2), act * jax.nn.sigmoid(act), 0.0)
        at = slice(r * pitch, (r + 1) * pitch)
        for j in range(3):
            start = SIDE + j - 1
            wide[at, j * channels : (j + 1) * channels] = value[start : start + pitch].astype(BF16)
        if 2 <= r < height + 2:
            base = (r - 2) * pitch
            own_s[base : base + SIDE, :] = blank
            own_s[base + SIDE : base + SIDE + width, :] = value[2 * SIDE : 2 * SIDE + width]
            own_s[base + SIDE + width : base + pitch, :] = blank

    step = 3
    steps = (height + 2) // step
    ends(z_out, channels)
    weight, codes = use(weight, codes)

    def z_copy(k):
        at = slice(SIDE + k * step * pitch, SIDE + (k + 1) * step * pitch)
        return pltpu.make_async_copy(z_out.at[at, :], z_far.at[at, :], sems.at[k])

    def part(k):
        first = SIDE + k * step * pitch
        count = step * pitch
        z = tmp_s[first + pitch : first + pitch + count, :]
        z = z + forward_rows(wide, weight, k * step, step, pitch)
        z_out[first : first + count, :] = z
        z_copy(k).start()
        tops = []
        for u in range(step):
            line = k * step + u - 1
            if 0 <= line < height:
                at = u * pitch + SIDE
                some = (codes[line].astype(F32) - z[at : at + width]) * code_scale
                pull[line * width : (line + 1) * width, :] = some
                tops.append(jnp.max(jnp.abs(some), 0, keepdims=True))
        return tops

    for r in range(step + 2):
        smooth_row(r)
    tops = []
    for k in range(steps):
        for r in range((k + 1) * step + 2, min((k + 2) * step + 2, height + 4)):
            smooth_row(r)
        tops += part(k)
    for r in range(0, height, 8):
        at = slice(r * pitch, (r + 8) * pitch)
        turned[:, at] = own_s[at, :].T.astype(BF16)
    turned_copy = pltpu.make_async_copy(turned, turned_far, sems.at[steps])
    turned_copy.start()
    top = jnp.max(jnp.concatenate(tops, 0), 0, keepdims=True)
    top = jnp.max(top, 1, keepdims=True)
    power[...] = jnp.broadcast_to(exponent(top), power.shape)
    for k in range(steps):
        z_copy(k).wait()
    turned_copy.wait()


def pack_kernel(slots, pull, power, packed):
    packed[...] = jnp.zeros(packed.shape, F32)
    scale = jnp.exp2(power[0:1, :])

    def some(i, _):
        value = pull[pl.ds(pl.multiple_of(i * 16, 8), 16), :] * scale
        for u in range(16):
            packed[pl.ds(slots[i * 16 + u], 1), :] = value[u : u + 1, :]
        return 0

    lax.fori_loop(0, pull.shape[0] // 16, some, 0, unroll=4)


def flip_weight(weight, flipped):
    channels = weight.shape[2]
    for dy in range(3):
        for j in range(3):
            flipped[dy, :, j * channels : (j + 1) * channels] = weight[dy, 2 - j]


def rotate_kernel(
    cot, left, right, up, down, codes, code_l, code_r, code_u, code_d, z_in, turned, dec_w, power,
    plane_far, keep_grad, give_grad,
    tmp_s, code_s, wide, back_wide, flipped, plane, sem,
):
    height, width, channels = cot.ref.shape
    pitch = width + 2 * SIDE
    fill_tile(tmp_s, *use(cot, left, right, up, down), 2)
    spread(tmp_s, wide, height + 4, pitch, channels)
    fill_tile(code_s, *use(codes, code_l, code_r, code_u, code_d), 1)
    flip_weight(*use(dec_w), flipped)
    ends(plane, channels)
    step = 3
    chunks = (height + 2) // step

    def part(k):
        at = slice(SIDE + k * step * pitch, SIDE + (k + 1) * step * pitch)
        plane[at, :] = backward_rows(wide, flipped, k * step, step, pitch)

    block = 24
    z_in, turned = use(z_in, turned)
    place = lax.broadcasted_iota(jnp.int32, (block, 1), 0)
    row, col, rows, cols = place_of()

    def total(x):
        return jnp.sum(x, 1, keepdims=True)

    def turn(line):
        spots = [
            slice(SIDE + line * pitch + b, SIDE + line * pitch + b + block)
            for b in range(0, pitch, block)
        ]
        sums = []
        for at in spots:
            z, e = z_in[at, :], code_s[at, :]
            sums.append((total(z * z) + epsilon, total(e * e) + epsilon))
        scales = []
        for at, (zz, ee) in zip(spots, sums):
            z, e, back = z_in[at, :], code_s[at, :], plane[at, :]
            z_inv, e_inv = lax.rsqrt(zz), lax.rsqrt(ee)
            e_unit = e * e_inv
            mirror = z * z_inv + e_unit
            scales.append(
                (z_inv, e_inv, ee, total(mirror * mirror) + epsilon, total(mirror * back),
                 total(e_unit * back))
            )
        high = row * height + line - 1
        keep = (high >= 0) & (high < rows * height)
        for b, (at, (z_inv, e_inv, ee, mm, along, code)) in enumerate(zip(spots, scales)):
            z, e, back = z_in[at, :], code_s[at, :], plane[at, :]
            stretch = ee * e_inv * z_inv
            along = 2.0 * along / mm
            z_part = stretch * z_inv * (2.0 * code - along) + commit_beta
            e_part = stretch * e_inv * along + commit_beta
            across = place + b * block - SIDE + col * width
            inside = keep & (across >= 0) & (across < cols * width)
            plane[at, :] = jnp.where(inside, stretch * back + z_part * z - e_part * e, 0.0)

    part(0)
    for k in range(chunks):
        if k + 1 < chunks:
            part(k + 1)
        for u in range(step):
            turn(k * step + u)
    plane_copy = pltpu.make_async_copy(plane, plane_far, sem)
    plane_copy.start()
    spread(plane, back_wide, height + 2, pitch, channels)
    kernel_grad(turned, back_wide, keep_grad, give_grad, pitch, height, 1)
    taps, half = keep_grad.shape[0] - 8, keep_grad.shape[1]
    lane = lax.broadcasted_iota(jnp.int32, (8, half), 1)
    mine = jnp.where(lane == row * cols + col, power[:, :half], 0.0)
    keep_grad[taps:, :] = mine
    give_grad[taps:, :] = mine
    plane_copy.wait()


def back_kernel(lat, plane, stats, gain, bias, enc_w, back_act, tail, back_wide, flipped):
    (plane,) = use(plane)
    height, width, channels = lat.ref.shape
    pitch = width + 2 * SIDE
    spread(plane, back_wide, height + 2, pitch, channels)
    flip_weight(*use(enc_w), flipped)
    (lat,) = use(lat)
    mean, inv = stats[0:1, :], stats[1:2, :]
    step = 4

    def last(k, totals):
        value = backward_rows(back_wide, flipped, k * step, step, pitch)
        first, second = totals
        for u in range(step):
            at = u * pitch + SIDE
            normed = (lat[k * step + u].astype(F32) - mean) * inv
            act = normed * gain[...] + bias[...]
            s = jax.nn.sigmoid(act)
            some = value[at : at + width] * s * (1.0 + act * (1.0 - s))
            back_act[k * step + u] = some
            first = first + jnp.sum(some, 0, keepdims=True)
            second = second + jnp.sum(some * normed, 0, keepdims=True)
        return first, second

    zero = jnp.zeros((1, channels), F32)
    first, second = lax.fori_loop(0, height // step, last, (zero, zero))
    half = channels // 2
    lines = [first[:, :half], first[:, half:], second[:, :half], second[:, half:]]
    tail[...] = jnp.concatenate(lines + [jnp.zeros((4, half), F32)], 0)


def last_kernel(lat, back_act, plane, stats, gain, *refs):
    pieces, (out, grads) = refs[:-2], refs[-2:]
    height, width, channels = lat.shape
    mean, inv = stats[0:1, :], stats[1:2, :]
    per_group = channels // G
    count = height * width * lax.axis_size("row") * lax.axis_size("col") * per_group
    end = pieces[0].shape[1] - 24
    sums = jnp.zeros((8, pieces[0].shape[2]), F32)
    for ref in pieces:
        for z in range(ref.shape[0]):
            some = ref[z, end : end + 8, :] + ref[z, end + 8 : end + 16, :]
            sums = sums + some * jnp.exp2(-ref[z, end + 18 : end + 19, :])
    first = jnp.concatenate([sums[0:1, :], sums[1:2, :]], 1)
    second = jnp.concatenate([sums[2:3, :], sums[3:4, :]], 1)
    grads[0:1, :] = first
    grads[1:2, :] = second
    same = lax.broadcasted_iota(jnp.int32, (channels, channels), 0) // per_group
    same = same == lax.broadcasted_iota(jnp.int32, (channels, channels), 1) // per_group
    mix = jnp.where(same, 1.0, 0.0).astype(F32)
    both = jnp.concatenate([first * gain[...], second * gain[...]] + [first] * 6, 0)
    means = dot(both, mix, precision=HIGH) * (1.0 / count)

    lat, back_act, plane = use(lat, back_act, plane)

    def one(r, _):
        normed = (lat[r].astype(F32) - mean) * inv
        d = back_act[r] * gain[...]
        at = pl.multiple_of((r + 1) * (width + 2 * SIDE) + 2 * SIDE, 8)
        enc_back = plane[pl.ds(at, width), :]
        out[r] = (inv * (d - means[0:1] - normed * means[1:2]) + enc_back).astype(BF16)
        return 0

    lax.fori_loop(0, height, one, 0)


def owner_kernel(tags, wide, out):
    shard, channels = out.shape
    total = jnp.zeros((shard, 2 * channels), F32)
    rows = wide.shape[0]
    chunk = 1024
    code = lax.broadcasted_iota(jnp.int32, (shard, tags.shape[1]), 0) + 1
    lines = chunk // tags.shape[1]
    for k in range(rows // chunk):
        hit = jnp.concatenate(
            [
                (code == tags[k * lines + u : k * lines + u + 1, :]).astype(F32).astype(BF16)
                for u in range(lines)
            ],
            1,
        )
        total = total + dot(hit, wide[k * chunk : (k + 1) * chunk, :])
    out[...] = total[:, :channels] + total[:, channels:]


def exponent(biggest):
    return 14.0 - jnp.ceil(jnp.log2(jnp.maximum(biggest, 1e-30)))


def exchange(x):
    return lax.all_to_all(x, AXES, split_axis=0, concat_axis=0, tiled=True)


def pair_swap(x):
    size = lax.axis_size("row")
    return lax.ppermute(x, "row", [(i, i ^ 1) for i in range(size)])


def shifts(n, stride=1):
    size = n * stride
    return [[((i + s * stride) % size, i) for i in range(size)] for s in range(1, n)]


def finish(outs, lines, tail, tops):
    end = 2 * lines
    powers = [exponent(jnp.max(top, 1, keepdims=True)) for top in tops]
    outs[0][end:, :] = tail
    for out in outs[1:]:
        out[end : end + 8, :] = tail
        out[end + 8 :, :] = jnp.zeros((8, tail.shape[1]), F32)
        for i, power in enumerate(powers):
            at = slice(i * lines, (i + 1) * lines)
            out[at, :] = out[at, :] * jnp.exp2(power)
            out[end + 8 + i : end + 9 + i, :] = jnp.broadcast_to(power, (1, tail.shape[1]))


def columns_kernel(cols, enc, enc_b, dec, dec_b, *outs):
    col = lax.axis_index("col")
    taps = dec.shape[0]
    lines = taps // cols
    tops = [jnp.zeros((1, dec.shape[1]), F32)] * 2
    for s, out in enumerate(outs):
        at = pl.ds(pl.multiple_of((col + cols - s) % cols * lines, 8), lines)
        for i, (one, two) in enumerate(((enc, enc_b), (dec, dec_b))):
            some = one[at, :] + two[at, :]
            out[i * lines : (i + 1) * lines, :] = some
            tops[i] = jnp.maximum(tops[i], jnp.max(jnp.abs(some), 0, keepdims=True))
    finish(outs, lines, enc[taps:, :] + enc_b[taps:, :], tops)


def rows_kernel(cols, *refs):
    parts, outs = refs[:cols], refs[cols:]
    row, _, rows, _ = place_of()
    depth = rows // 2
    lines = outs[0].shape[0] // 2 - 4
    wide = depth * lines
    end = 2 * wide
    scales = [
        [jnp.exp2(-ref[end + 8 + i : end + 9 + i, :]) for ref in parts[1:]] for i in range(2)
    ]

    def added(i, first, count):
        at = slice(i * wide + first, i * wide + first + count)
        value = parts[0][at, :]
        for ref, scale in zip(parts[1:], scales[i]):
            value = value + ref[at, :] * scale
        return value

    tail = parts[0][end:, :]
    for ref in parts[1:]:
        tail = tail + ref[end : end + 8, :]
    tops = [jnp.zeros((1, tail.shape[1]), F32)] * 2
    for z in range(depth):
        values = [added(i, z * lines, lines) for i in range(2)]
        tops = [
            jnp.maximum(top, jnp.max(jnp.abs(some), 0, keepdims=True))
            for top, some in zip(tops, values)
        ]
        for s, out in enumerate(outs):

            @pl.when((row // 2 + depth - s) % depth == z)
            def _():
                for i in range(2):
                    out[i * lines : (i + 1) * lines, :] = values[i]

    finish(outs, lines, tail, tops)


def chunk_kernel(depth, *refs):
    parts, (tail, tail_b, out, powers) = refs[:depth], refs[depth:]
    half = out.shape[1]
    lines = parts[0].shape[0] // 2 - 4
    end = 2 * lines
    total = parts[0][end:, :]
    values = [parts[0][i * lines : (i + 1) * lines, :] for i in range(2)]
    for ref in parts[1:]:
        total = total + ref[end : end + 8, :]
        for i in range(2):
            scale = jnp.exp2(-ref[end + 8 + i : end + 9 + i, :])
            values[i] = values[i] + ref[i * lines : (i + 1) * lines, :] * scale
    powers[...] = total
    values.append(tail[...] + tail_b[...])
    end = 2 * lines + 16
    out[end:, :] = jnp.zeros((8, half), F32)
    for i, some in enumerate(values):
        top = jnp.max(jnp.max(jnp.abs(some), 0, keepdims=True), 1, keepdims=True)
        power = exponent(top)
        some = some * jnp.exp2(power)
        if i < 2:
            out[i * lines : (i + 1) * lines, :] = some
        else:
            high = some.astype(BF16).astype(F32)
            out[end - 16 : end - 8, :] = high
            out[end - 8 : end, :] = some - high
        out[end + i : end + i + 1, :] = jnp.broadcast_to(power, (1, half))


def message_shapes(lines, half, count):
    return [shaped((2 * lines + 8, half))] + [shaped((2 * lines + 16, half))] * (count - 1)


def pass_on(parts, axis, perms):
    sent = [lax.ppermute(x.astype(F16), axis, p) for x, p in zip(parts[1:], perms)]
    return [parts[0]] + [x.astype(F32) for x in sent]


def column_sums(arrays):
    cols = lax.axis_size("col")
    taps, half = arrays[2].shape
    parts = call(
        lambda *refs: columns_kernel(cols, *refs),
        arrays,
        message_shapes(taps // cols, half, cols),
        moved=8 * 10**6,
    )
    return pass_on(parts, "col", shifts(cols))


def row_sums(parts, tail):
    cols, depth = len(parts), lax.axis_size("row") // 2
    half = parts[0].shape[1]
    lines = (parts[0].shape[0] // 2 - 4) // depth
    parts = call(
        lambda *refs: rows_kernel(cols, *refs),
        parts,
        message_shapes(lines, half, depth),
        moved=4 * 10**6,
    )
    parts = pass_on(parts, "row", shifts(depth, 2))
    return call(
        lambda *refs: chunk_kernel(depth, *refs),
        parts + [tail, pair_swap(tail)],
        (shaped((2 * lines + 24, half)), shaped((8, half))),
        moved=10**6,
    )


def gather_rows(chunk):
    own = chunk.astype(F16)
    steps = shifts(lax.axis_size("row") // 2, 2)
    return jnp.stack([own] + [lax.ppermute(own, "row", p) for p in steps])


def gather_columns(own):
    return [own] + [lax.ppermute(own, "col", p) for p in shifts(lax.axis_size("col"))]


def gather_cores(own, other):
    rows, cols = lax.axis_size("row"), lax.axis_size("col")
    lines, half = own[0].shape[1] // 2 - 12, own[0].shape[2]
    chunks = cols * rows // 2
    return call(
        lambda *refs: assemble_kernel(lines, *refs),
        own + other,
        (shaped((chunks, lines, 2 * half)), shaped((chunks, lines, 2 * half))),
        moved=10**7,
    )


def assemble_kernel(lines, *refs):
    pieces, outs = refs[:-2], refs[-2:]
    row, col, rows, cols = place_of()
    depth = rows // 2
    half = outs[0].shape[2] // 2
    for k, ref in enumerate(pieces):
        core = (row + k // cols) % 2
        c = (col + k % cols) % cols
        lanes = pl.ds(pl.multiple_of(core * half, half), half)
        for s in range(depth):
            z = (row // 2 + s) % depth
            for i, out in enumerate(outs):
                at = 2 * lines + 16 + i
                scale = jnp.exp2(-ref[s, at : at + 1, :])
                value = ref[s, i * lines : (i + 1) * lines, :] * scale
                out[c * depth + z, :, lanes] = value


def halo(fields):
    rows, cols = lax.axis_size("row"), lax.axis_size("col")
    forth = lambda n: [(i, i + 1) for i in range(n - 1)]
    back = lambda n: [(i + 1, i) for i in range(n - 1)]
    left_edge = jnp.stack([x[:, :HALO] for x in fields])
    right_edge = jnp.stack([x[:, -HALO:] for x in fields])
    left = lax.ppermute(right_edge, "col", forth(cols))
    right = lax.ppermute(left_edge, "col", back(cols))

    def lines(at):
        return jnp.concatenate([left[:, at], jnp.stack([x[at] for x in fields]), right[:, at]], 2)

    up = lax.ppermute(lines(slice(-HALO, None)), "row", forth(rows))
    down = lax.ppermute(lines(slice(0, HALO)), "row", back(rows))
    return left, right, up, down


def body(
    latents,
    code_ids,
    norm_gain,
    norm_bias,
    encoder_weight,
    codebook,
    decoder_weight,
    decoded_cotangent,
):
    height, width, channels = latents.shape
    devices = lax.axis_size("row") * lax.axis_size("col")
    codes_total = codebook.shape[0]
    shard = codes_total // devices
    count = height * width
    cap = 2 * count // devices
    pitch = width + 2 * SIDE
    conv_flops = 2 * count * 9 * channels * channels
    taps = 9 * channels
    half = channels // 2
    plane = (height + 2) * pitch
    plane_rows = plane + 2 * SIDE
    big = (height + 4) * pitch
    after = lambda *x: lax.optimization_barrier(x)
    halos = lambda field, start: [(start + i, field) for i in range(4)]

    payload, slots = call(
        lambda *refs: front_kernel(devices, shard, cap, *refs),
        (latents, code_ids),
        (shaped((devices, 8, width)), shaped((height, width), jnp.int32)),
        flops=10**9,
        moved=10**6,
        late=[(0, None)],
    )
    payload, code_ids, latents, decoded_cotangent = after(
        payload, code_ids, latents, decoded_cotangent
    )
    gathered = exchange(payload)
    quantized = codebook[code_ids]
    left, right, up, down = halo((latents, decoded_cotangent, quantized))
    gain = norm_gain.reshape(1, channels)
    bias = norm_bias.reshape(1, channels)

    dec_grad = call(
        decoder_grad_kernel,
        (decoded_cotangent, quantized, left, right, up, down),
        (shaped((taps, half)), shaped((taps, half))),
        [
            pltpu.VMEM((plane_rows, channels), F32),
            pltpu.VMEM((plane, 3 * channels), BF16),
            pltpu.VMEM((channels, height * pitch), BF16),
        ],
        flops=conv_flops,
        moved=5 * 10**6,
        late=[(0, None), *halos(1, 2), (1, None)],
    )
    dec_keep, dec_give = dec_grad
    gathered, dec_keep, dec_give = after(gathered, dec_keep, dec_give)
    dec_given = pair_swap(dec_give)
    enc_fwd = encoder_weight.reshape(3, 3 * channels, channels)
    dec_fwd = decoder_weight.reshape(3, 3 * channels, channels)
    code_scale = codes_total / (count * devices)
    z, pull, turned, stats, power = call(
        lambda *refs: encoder_kernel(code_scale, *refs),
        (latents, left, right, up, down, quantized, gathered, gain, bias, enc_fwd),
        (
            shaped((plane_rows, channels)),
            shaped((count, channels)),
            shaped((channels, height * pitch), BF16),
            shaped((8, channels)),
            shaped((8, channels)),
        ),
        [
            pltpu.VMEM((big + 2 * SIDE, channels), F32),
            pltpu.VMEM((big, 3 * channels), BF16),
            pltpu.VMEM((plane_rows, channels), F32),
            pltpu.VMEM((channels, height * pitch), BF16),
            pltpu.VMEM((height * pitch, channels), F32),
            pltpu.SemaphoreType.DMA(((height + 2) // 3 + 1,)),
        ],
        far=(0, 2),
        flops=conv_flops,
        moved=10 * 10**6,
        room=20,
        late=[(0, None), *halos(0, 1), (9, None), (5, None)],
    )
    packed = call(
        pack_kernel,
        (slots.reshape(-1), pull, power),
        shaped((devices * cap, channels)),
        specs=[SMEM, VMEM, VMEM],
        flops=5 * 10**9,
        moved=6 * 10**6,
    )
    send = packed.astype(F16).reshape(devices, cap, channels)
    send, z, dec_given = after(send, z, dec_given)
    received = exchange(send)

    back_plane, keep_grad, give_grad = call(
        rotate_kernel,
        (
            decoded_cotangent, left, right, up, down, quantized, left, right, up, down, z, turned,
            decoder_weight, power,
        ),
        (
            shaped((plane_rows, channels)),
            shaped((taps + 8, half)),
            shaped((taps + 8, half)),
        ),
        [
            pltpu.VMEM((big + 2 * SIDE, channels), F32),
            pltpu.VMEM((plane_rows, channels), F32),
            pltpu.VMEM((big, 3 * channels), BF16),
            pltpu.VMEM((plane, 3 * channels), BF16),
            pltpu.VMEM((3, channels, 3 * channels), BF16),
            pltpu.VMEM((plane_rows, channels), F32),
            pltpu.SemaphoreType.DMA,
        ],
        far=(0,),
        flops=2 * conv_flops,
        moved=15 * 10**6,
        room=32,
        late=[
            (0, None), *halos(1, 1), (5, None), *halos(2, 6), (12, None), (10, None), (11, None)
        ],
    )
    parts = column_sums((keep_grad, pair_swap(give_grad), dec_keep, dec_given))
    back_act, tail = call(
        back_kernel,
        (latents, back_plane, stats, gain, bias, encoder_weight),
        (shaped((height, width, channels)), shaped((8, half))),
        [
            pltpu.VMEM((plane, 3 * channels), BF16),
            pltpu.VMEM((3, channels, 3 * channels), BF16),
        ],
        flops=conv_flops,
        moved=8 * 10**6,
        late=[(1, None), (5, None), (0, None)],
    )
    decoded = call(
        decoder_kernel,
        (quantized, left, right, up, down, dec_fwd),
        shaped((height, width, channels), BF16),
        [
            pltpu.VMEM((plane_rows, channels), F32),
            pltpu.VMEM((plane, 3 * channels), BF16),
        ],
        flops=conv_flops,
        moved=4 * 10**6,
        late=[(0, None), *halos(2, 1), (5, None)],
    )
    decoded, *parts = after(decoded, *parts)
    chunk, powers = row_sums(parts, tail)
    own = gather_rows(chunk)
    pieces = gather_columns(own)

    rows_f = received.astype(F32) * jnp.exp2(-jnp.round(powers[0, :devices]))[:, None, None]
    rows_f = rows_f.reshape(devices * cap, channels)
    high = lax.reduce_precision(rows_f, 8, 7)
    low = rows_f - high
    wide = jnp.concatenate([high.astype(BF16), low.astype(BF16)], 1)
    tags = gathered[:, 4, :cap].astype(jnp.int32).reshape(-1, 128)
    codebook_grad = call(
        owner_kernel,
        (tags, wide),
        shaped((shard, channels)),
        flops=2 * 10**9,
        moved=6 * 10**6,
    )
    codebook_grad, *pieces = after(codebook_grad, *pieces)
    other = [pair_swap(x) for x in pieces]
    own = [x.astype(F32) for x in pieces]
    latents_grad, norm_grads = call(
        last_kernel,
        (latents, back_act, back_plane, stats, gain, *own),
        (shaped((height, width, channels), BF16), shaped((2, channels))),
        flops=10**8,
        moved=6 * 10**6,
    )
    other = [x.astype(F32) for x in other]
    encoder_weight_grad, decoder_weight_grad = [
        x.reshape(3, 3, channels, channels) for x in gather_cores(own, other)
    ]
    return (
        decoded,
        latents_grad,
        norm_grads[1],
        norm_grads[0],
        encoder_weight_grad,
        decoder_weight_grad,
        codebook_grad,
    )


def solution(mesh):
    return jax.shard_map(
        body,
        mesh=mesh,
        in_specs=(
            P("row", "col", None),
            P("row", "col"),
            P(),
            P(),
            P(),
            P(),
            P(),
            P("row", "col", None),
        ),
        out_specs=(
            P("row", "col", None),
            P("row", "col", None),
            P(),
            P(),
            P(),
            P(),
            P(("row", "col"), None),
        ),
        check_vma=False,
    )
```
